128 devices in a mesh: dp: 4 (over x_lo, core), ctx: 32 (over z, x_hi, y).
Axes of the slice: x: 4 (x_hi: 2, x_lo: 2; x = x_hi * 2 + x_lo), y: 4, z: 4, core: 2. Of those that a mesh axis runs over, the one named last changes fastest.
Arguments:
- queries: bfloat16 [4, 6144, 2048], P('dp', 'ctx'), may hold values from -128 to 128
- keys: bfloat16 [4, 6144, 2048], P('dp', 'ctx'), may hold values from -4 to 4
- values: bfloat16 [4, 6144, 2048], P('dp', 'ctx'), may hold values from -6 to 6
- grad_out: bfloat16 [4, 6144, 2048], P('dp', 'ctx'), may hold values from -6 to 6
- lengths: int32 [4, 32], P('dp'), may hold values from 1 to 384, 6144 in all within a row
- image_flags: int32 [4, 32], P('dp'), may hold values 0 or 1
Outputs:
- grad_queries: bfloat16 [4, 6144, 2048], P('dp', 'ctx')
- grad_keys: bfloat16 [4, 6144, 2048], P('dp', 'ctx')
- grad_values: bfloat16 [4, 6144, 2048], P('dp', 'ctx')
The draws below stay inside these ranges and needn't reach their ends.
Inputs may be any that keep to these rules, and one draw needn't show every extreme that they name: Each sample's 32 lengths sum to 6144, and the largest is 384.
All inputs are finite; a program needn't handle non-finite values. No bound on the sum of `image_flags` on one device may be relied on, other than what follows from the above.
Results may differ from the reference program's by a relative error of at most 0.027.
Values may be sent and summed in bfloat16 or wider, within the bound.
No kernel may reach another device: no remote copies, remote signals or barrier semaphores. Data moves between devices by JAX's collectives and lax.ppermute only.
A program may use at most 128 MiB of HBM per device.

```python
import math
import jax
import jax.numpy as jnp
import numpy as np
from jax import lax

HEADS = 16
HEAD = 128
C = 96
STEPS = 4
SEGS = 32
SAMPLES = 4
LEN = 6144
HD = 2048
MOST = 384
N_CTX = 32


def shared_normal(key):
    return jnp.clip(jax.random.normal(key, (SAMPLES, LEN, HD), jnp.float32), -4.0, 4.0)


def draw_keys(key, part):
    common = shared_normal(key)
    return common.astype(jnp.bfloat16)


def draw_queries(key, part):
    key = jax.random.fold_in(key, 12)
    fresh_key = jax.random.fold_in(key, 0)
    fresh = jnp.clip(jax.random.normal(fresh_key, (SAMPLES, LEN, HD), jnp.float32), -4.0, 4.0)
    return fresh.astype(jnp.bfloat16)


def plant(values, stream_key, low, top_value):
    longest = values.shape.index(max(values.shape))
    spots = []
    for shift in (0, 1):
        where = [jax.random.randint(jax.random.fold_in(stream_key, axis), (), 0, length) for axis, length in enumerate(values.shape)]
        where[longest] = (where[longest] + shift) % values.shape[longest]
        spots.append(tuple(where))
    return values.at[spots[0]].set(low).at[spots[1]].set(top_value)


def block_scale(stream_key, shape, pieces, smallest, top_value):
    def one(dim, shards_of):
        draws = jax.random.uniform(jax.random.fold_in(jax.random.fold_in(stream_key, 6), dim), (shards_of,), jnp.float32, smallest / len(pieces), top_value / len(pieces))
        return jnp.repeat(jnp.exp(draws), shape[dim] // shards_of).reshape((-1,) + (1,) * (len(shape) - dim - 1))

    level = one(*pieces[0])
    for cut in pieces[1:]:
        level = level * one(*cut)
    return level


def split_up(number_of, total, limit, lean):
    portions = [(1 << 20) // math.isqrt(grade ** lean) + 1 for grade in range(2, number_of + 1)]
    spare, holding = total - limit - (number_of - 1), [1] * (number_of - 1)
    while spare > 0:
        free = [i for i in range(number_of - 1) if holding[i] < limit]
        whole, budget = sum([portions[i] for i in free]), spare
        for i in free:
            addition = min(limit - holding[i], max(1, budget * portions[i] // whole), spare)
            holding[i] = holding[i] + addition
            spare = spare - addition
    return np.array([limit] + holding)


def ragged(rng, amount, total, bound, slope):
    if amount == 2:
        one = jax.random.randint(rng, (), max(1, total - bound), min(bound, total - 1) + 1)
        return jnp.stack([one, total - one])
    tallies = jnp.asarray(split_up(amount, total, bound, slope), jnp.int32)
    couples = (amount - 1) // 2
    source_of, sink = tallies[1:1 + 2 * couples:2], tallies[2:2 + 2 * couples:2]
    slack = jnp.minimum(source_of - 1, bound - sink)
    passed = jax.random.randint(jax.random.fold_in(rng, 1), (couples,), 0, 1 << 20) % (slack + 1)
    tallies = tallies.at[1:1 + 2 * couples:2].set(source_of - passed).at[2:2 + 2 * couples:2].set(sink + passed)
    return tallies[jax.random.permutation(jax.random.fold_in(rng, 2), amount)]


def normal_values(rng, shape, scale, limit, cuts=(), kind=jnp.bfloat16):
    loudness = block_scale(rng, shape, cuts, -0.22, 0.18) if cuts else 1.0
    drawn = jax.random.normal(rng, shape, jnp.float32) * scale * loudness
    return jnp.minimum(jnp.maximum(drawn, -limit), limit).astype(kind)


def setup_inputs(seed: int = 0) -> dict:
    key_of = jax.random.split(jax.random.key(seed), 7)
    queries = draw_queries(jax.random.fold_in(key_of[6], 71), 0)
    keys = draw_keys(jax.random.fold_in(key_of[6], 71), 0)
    values = normal_values(key_of[2], (SAMPLES, LEN, HD), 1.0, 6.0, ((0, 4), (1, 32)))
    grad_out = normal_values(key_of[3], (SAMPLES, LEN, HD), 1.0, 6.0, ((0, 4), (1, 32)))
    lengths = jax.vmap(lambda own: ragged(own, SEGS, LEN, MOST, 2))(jax.random.split(key_of[4], SAMPLES)).reshape((SAMPLES, SEGS)).astype(jnp.int32)
    image_flags = plant((jax.random.randint(key_of[5], (SAMPLES, SEGS), 0, 2) < 1).astype(jnp.int32), jax.random.fold_in(key_of[5], 1), 0, 1)
    return dict(queries=queries, keys=keys, values=values, grad_out=grad_out, lengths=lengths, image_flags=image_flags)


def layout(device, stretch_rows, cycle_size, ending, flag_list):
    offsets = jnp.arange(stretch_rows, dtype=jnp.int32)
    first_pos = device * stretch_rows + offsets
    second_pos = (2 * cycle_size - 1 - device) * stretch_rows + offsets
    position = jnp.concatenate([first_pos, second_pos]).astype(jnp.int32)
    segment = jnp.sum((position[:, None] >= ending[None, :]).astype(jnp.int32), axis=1)
    labels = jnp.arange(ending.shape[0], dtype=jnp.int32)
    is_image = jnp.sum(jnp.where(segment[:, None] == labels[None, :], flag_list[None, :], 0), axis=1)
    return position, segment, is_image


def visible(query_side, key_side):
    causal = key_side[0][None, :] <= query_side[0][:, None]
    within = (key_side[1][None, :] == query_side[1][:, None]) & (query_side[2][:, None] == 1)
    return causal | within


def rounded(values_in):
    return lax.optimization_barrier(values_in.astype(jnp.bfloat16)).astype(values_in.dtype)


def reference(queries, keys, values, grad_out, lengths, image_flags):
    scale = HEAD ** -0.5
    block_rows = 2 * C
    devices = jnp.arange(N_CTX, dtype=jnp.int32)
    endings = jnp.cumsum(lengths, axis=1).astype(jnp.int32)

    def sample_layout(ending, flag_list):
        def per_device(device):
            return layout(device, C, N_CTX, ending, flag_list)
        return jax.vmap(per_device)(devices)

    positions, segments, images = jax.vmap(sample_layout)(endings, image_flags)
    text_rows = (1 - images).astype(jnp.float32)
    text_count = jnp.sum(text_rows)
    weight = text_rows * (float(SAMPLES * LEN) / text_count)
    weighted = (grad_out.astype(jnp.float32) * weight.reshape(SAMPLES, LEN)[:, :, None]).astype(jnp.bfloat16)

    def one_sample(packed):
        query_all, key_all, value_all, weighted_all, position, segment, is_image = packed
        query_blocks = query_all.reshape(N_CTX, block_rows, HD)
        key_blocks = key_all.reshape(N_CTX, block_rows, HD)
        value_blocks = value_all.reshape(N_CTX, block_rows, HD)
        weighted_blocks = weighted_all.reshape(N_CTX, block_rows, HD)

        def take(source, index):
            return lax.dynamic_index_in_dim(source, index, 0, keepdims=False)

        def one_block(device):
            query_blk = take(query_blocks, device).astype(jnp.float32).reshape(block_rows, HEADS, HEAD)
            weighted_blk = take(weighted_blocks, device).astype(jnp.float32).reshape(block_rows, HEADS, HEAD)
            query_side = (take(position, device), take(segment, device), take(is_image, device))
            key_list, value_list, kpos_list, kseg_list = [], [], [], []
            for step_index in range(STEPS):
                source = ((device - step_index) % N_CTX).astype(jnp.int32)
                key_list.append(take(key_blocks, source))
                value_list.append(take(value_blocks, source))
                kpos_list.append(take(position, source))
                kseg_list.append(take(segment, source))
            key_win = jnp.concatenate(key_list, axis=0).astype(jnp.float32).reshape(-1, HEADS, HEAD)
            value_win = jnp.concatenate(value_list, axis=0).astype(jnp.float32).reshape(-1, HEADS, HEAD)
            key_side = (jnp.concatenate(kpos_list), jnp.concatenate(kseg_list))
            allowed = visible(query_side, key_side)
            scores = jnp.einsum("qhd,khd->hqk", query_blk, key_win, precision=lax.Precision.HIGHEST) * scale
            masked = jnp.where(allowed[None], scores, -jnp.inf)
            largest = jnp.max(masked, axis=-1)
            lse = largest + jnp.log(jnp.sum(jnp.exp(masked - largest[:, :, None]), axis=-1))
            prob = jnp.exp(masked - lse[:, :, None])
            prob_half = rounded(prob)
            attended = rounded(jnp.einsum("hqk,khd->qhd", prob_half, value_win, precision=lax.Precision.HIGHEST))
            delta = jnp.einsum("qhd,qhd->hq", weighted_blk, attended, precision=lax.Precision.HIGHEST)
            dprob = jnp.einsum("qhd,khd->hqk", weighted_blk, value_win, precision=lax.Precision.HIGHEST)
            dscore = rounded(prob * (dprob - delta[:, :, None]))
            grad_query = (jnp.einsum("hqk,khd->qhd", dscore, key_win, precision=lax.Precision.HIGHEST) * scale)
            grad_key = jnp.einsum("hqk,qhd->khd", dscore, query_blk, precision=lax.Precision.HIGHEST) * scale
            grad_value = jnp.einsum("hqk,qhd->khd", prob_half, weighted_blk, precision=lax.Precision.HIGHEST)
            return (grad_query.astype(jnp.bfloat16).reshape(block_rows, HD),
                    grad_key.reshape(STEPS, block_rows, HD),
                    grad_value.reshape(STEPS, block_rows, HD))

        grad_query, key_parts, value_parts = lax.map(one_block, devices)
        grad_key = jnp.zeros((N_CTX, block_rows, HD), key_parts.dtype)
        grad_value = jnp.zeros((N_CTX, block_rows, HD), value_parts.dtype)
        for step_index in range(STEPS):
            grad_key = grad_key + jnp.roll(key_parts[:, step_index], -step_index, axis=0)
            grad_value = grad_value + jnp.roll(value_parts[:, step_index], -step_index, axis=0)
        return (grad_query.reshape(LEN, HD),
                grad_key.reshape(LEN, HD).astype(jnp.bfloat16),
                grad_value.reshape(LEN, HD).astype(jnp.bfloat16))

    grad_queries, grad_keys, grad_values = lax.map(
        one_sample, (queries, keys, values, weighted, positions, segments, images))
    return (grad_queries, grad_keys, grad_values)
```

```python
import functools

import jax
import jax.numpy as jnp
from jax import lax
from jax.experimental import pallas as pl
from jax.experimental.pallas import tpu as pltpu
from jax.sharding import PartitionSpec as P

HEAD = 128
STEPS = 4
GROUP = 4
CHUNKS = 2
LOG2E = 1.4426950408889634
MASKED = -1e30
VMEM = pl.BlockSpec(memory_space=pltpu.VMEM)
ANY = pl.BlockSpec(memory_space=pl.ANY)
LARGE = pltpu.CompilerParams(vmem_limit_bytes=60 * 1024 * 1024)
EDGE_COST = (0, 6000000000)
SETTLE_COST = 3000000000
SMALL = pltpu.CompilerParams(vmem_limit_bytes=10 * 1024 * 1024)


def columns(place, away, chunk, width):
    index = lax.rem(place + GROUP + away, GROUP)
    return pl.ds(pl.multiple_of((index * CHUNKS + chunk) * width, width), width)


def pack_kernel(chunk, first, second, after, one, two, three):
    width = one.shape[2]
    for away, message in ((1, one), (2, two), (3, three)):
        lanes = columns(lax.rem(lax.axis_index("ctx"), GROUP), away, chunk, width)
        message[0] = first[:, lanes]
        message[1] = second[:, lanes]


def first_pack_kernel(first, second, lengths, flags, one, two, three, text, sems):
    width = one.shape[2]
    place = lax.rem(lax.axis_index("ctx"), GROUP)
    copies = []
    for away, message in ((1, one), (2, two), (3, three)):
        lanes = columns(place, away, 0, width)
        for part, source in enumerate((first, second)):
            copies.append(
                pltpu.make_async_copy(source.at[:, lanes], message.at[part], sems.at[len(copies)])
            )
    for copy in copies:
        copy.start()
    text[...] = (lengths[...] * (1 - flags[...])).astype(jnp.float32)
    for copy in copies:
        copy.wait()


def pack(first, second, after, chunk):
    rows, total = first.shape
    width = total // (GROUP * CHUNKS)
    message = jax.ShapeDtypeStruct((2, rows, width), first.dtype)
    return pl.pallas_call(
        functools.partial(pack_kernel, chunk),
        out_shape=(message,) * (GROUP - 1),
        in_specs=[VMEM, VMEM, ANY],
        out_specs=(VMEM,) * (GROUP - 1),
        compiler_params=SMALL,
        cost_estimate=pl.CostEstimate(flops=0, bytes_accessed=12 * rows * width * 2, transcendentals=0),
        name="pack",
    )(first, second, after)


def first_pack(first, second, lengths, flags):
    rows, total = first.shape
    width = total // (GROUP * CHUNKS)
    message = jax.ShapeDtypeStruct((2, rows, width), first.dtype)
    *messages, text = pl.pallas_call(
        first_pack_kernel,
        out_shape=(message,) * (GROUP - 1) + (jax.ShapeDtypeStruct(lengths.shape, jnp.float32),),
        in_specs=[ANY, ANY, VMEM, VMEM],
        out_specs=(VMEM,) * GROUP,
        scratch_shapes=[pltpu.SemaphoreType.DMA((2 * (GROUP - 1),))],
        compiler_params=LARGE,
        cost_estimate=pl.CostEstimate(flops=0, bytes_accessed=12 * rows * width * 2, transcendentals=0),
        name="first_pack",
    )(first, second, lengths, flags)
    return messages, text


def edge_kernel(chunk, first, second, one, two, three, *refs):
    edge = refs[-1]
    rows = edge.shape[1] // (GROUP - 1)
    width = edge.shape[2]
    place = lax.rem(lax.axis_index("ctx"), GROUP)
    for away, message in enumerate((None, one, two, three)):
        index = lax.rem(place + GROUP - away, GROUP)

        @pl.when(index > 0)
        def put():
            at = pl.ds(pl.multiple_of((index - 1) * rows, rows), rows)
            if message is None:
                lanes = columns(place, 0, chunk, width)
                edge[0, at, :] = first[:, lanes]
                edge[1, at, :] = second[:, lanes]
            else:
                edge[:, at, :] = message[...]


def make_edge(first, second, blocks, afters, chunk, cost):
    _, rows, width = blocks[0].shape
    return pl.pallas_call(
        functools.partial(edge_kernel, chunk),
        out_shape=jax.ShapeDtypeStruct((2, (GROUP - 1) * rows, width), first.dtype),
        in_specs=[VMEM] * 5 + [ANY] * len(afters),
        out_specs=VMEM,
        compiler_params=SMALL,
        cost_estimate=pl.CostEstimate(flops=cost, bytes_accessed=0, transcendentals=0),
        name="edge",
    )(first, second, *blocks, *afters)


def sides_kernel(stretch_rows, cycle_size, bounds_ref, after, limit_ref, text_ref, key_ref):
    rows = 2 * stretch_rows
    device_here = lax.axis_index("ctx")
    start = device_here - lax.rem(device_here, GROUP)
    first = bounds_ref[0:1, :]
    ending = bounds_ref[1:2, :]
    flag = bounds_ref[2:3, :].astype(jnp.float32)
    last = ending.astype(jnp.float32)
    shape = (rows, HEAD)
    offset = lax.broadcasted_iota(jnp.int32, shape, 0)
    for block in range(GROUP):
        device = start + block
        position = jnp.where(
            offset < stretch_rows,
            device * stretch_rows + offset,
            (2 * cycle_size - 2 - device) * stretch_rows + offset,
        )
        inside = (position >= first) & (position < ending)
        image = jnp.sum(jnp.where(inside, flag, 0.0), axis=1, keepdims=True)
        final = jnp.sum(jnp.where(inside, last, 0.0), axis=1, keepdims=True).astype(jnp.int32) - 1
        limit_ref[block] = jnp.where(image > 0.5, final, position)
        text_ref[block] = jnp.broadcast_to(1.0 - image, shape)
        lane = lax.broadcasted_iota(jnp.int32, (8, STEPS * rows), 1)
        step = jnp.zeros_like(lane)
        for edge in range(1, STEPS):
            step = step + (lane >= edge * rows).astype(jnp.int32)
        owner = device - (STEPS - 1) + step
        owner = jnp.where(owner < 0, owner + cycle_size, owner)
        within = lane - step * rows
        key_ref[block] = jnp.where(
            within < stretch_rows,
            owner * stretch_rows + within,
            (2 * cycle_size - 2 - owner) * stretch_rows + within,
        )


def sides(bounds, after, stretch_rows, cycle_size):
    rows = 2 * stretch_rows
    return pl.pallas_call(
        functools.partial(sides_kernel, stretch_rows, cycle_size),
        out_shape=(
            jax.ShapeDtypeStruct((GROUP, rows, HEAD), jnp.int32),
            jax.ShapeDtypeStruct((GROUP, rows, HEAD), jnp.float32),
            jax.ShapeDtypeStruct((GROUP, 8, STEPS * rows), jnp.int32),
        ),
        in_specs=[VMEM, ANY],
        out_specs=(VMEM,) * 3,
        compiler_params=SMALL,
        cost_estimate=pl.CostEstimate(flops=GROUP * rows * HEAD * 8, bytes_accessed=GROUP * rows * HEAD * 8, transcendentals=0),
        name="sides",
    )(bounds, after)


def attend_kernel(
    chunk, total_rows, text_one, text_two, text_three, text_four, limit_ref, text_ref, keypos_ref,
    queries, keys, values, grads, key_one, key_two, key_three, query_one, query_two, query_three,
    edge_ref, query_own, query_to_one, query_to_two, query_to_three, main_ref, far_ref,
    key_all, value_all, query_all, grad_all, key_grad, value_grad, query_out,
):
    rows, width = queries.shape[0], edge_ref.shape[2]
    edge = (GROUP - 1) * rows
    span = STEPS * rows
    scale = HEAD ** (-0.5)
    place = lax.rem(lax.axis_index("ctx"), GROUP)
    counted = text_one[...] + text_two[...] + text_three[...] + text_four[...]
    factor = total_rows / jnp.sum(counted, axis=1, keepdims=True)
    lanes = columns(place, 0, chunk, width)
    key_all[:edge, :] = edge_ref[0]
    value_all[:edge, :] = edge_ref[1]
    sources = [(keys.at[:, lanes], values.at[:, lanes], queries.at[:, lanes], grads.at[:, lanes])]
    for pair, query_pair in ((key_one, query_one), (key_two, query_two), (key_three, query_three)):
        sources.append((pair.at[0], pair.at[1], query_pair.at[0], query_pair.at[1]))
    for away in range(GROUP):
        start = pl.multiple_of(lax.rem(place + GROUP - away, GROUP) * rows, rows)
        key, value, query, grad = sources[away]
        key_all[pl.ds(edge + start, rows), :] = key[...]
        value_all[pl.ds(edge + start, rows), :] = value[...]
        query_all[pl.ds(start, rows), :] = query[...]
        grad_all[pl.ds(start, rows), :] = grad[...]
    key_grad[...] = jnp.zeros_like(key_grad)
    value_grad[...] = jnp.zeros_like(value_grad)
    for block in range(GROUP):
        at = slice(block * rows, (block + 1) * rows)
        window = slice(block * rows, block * rows + span)
        limit = limit_ref[block]
        allowed = jnp.concatenate(
            [
                keypos_ref[block, 0:1, tile * HEAD : (tile + 1) * HEAD] <= limit
                for tile in range(span // HEAD)
            ],
            axis=1,
        )
        weight = text_ref[block] * factor
        for head in range(width // HEAD):
            lanes = slice(head * HEAD, (head + 1) * HEAD)
            query = query_all[at, lanes]
            grad = (grad_all[at, lanes].astype(jnp.float32) * weight).astype(jnp.bfloat16)
            key = key_all[window, lanes]
            value = value_all[window, lanes]
            scores = lax.dot_general(
                query, key, (((1,), (1,)), ((), ())), preferred_element_type=jnp.float32
            )
            scores = jnp.where(allowed, scores, MASKED)
            largest = jnp.max(scores, axis=1, keepdims=True)
            prob = jnp.exp2((scores - largest) * (scale * LOG2E))
            dprob = lax.dot_general(
                grad, value, (((1,), (1,)), ((), ())), preferred_element_type=jnp.float32
            )
            total = jnp.sum(prob, axis=1, keepdims=True)
            inverse = 1.0 / total
            delta = jnp.sum(prob * dprob, axis=1, keepdims=True) * inverse
            prob = prob * inverse
            dscore = (prob * (dprob - delta)).astype(jnp.bfloat16)
            prob_half = prob.astype(jnp.bfloat16)
            query_out[at, lanes] = (
                jnp.dot(dscore, key, preferred_element_type=jnp.float32) * scale
            ).astype(jnp.bfloat16)
            key_grad[window, lanes] += lax.dot_general(
                dscore, query, (((0,), (0,)), ((), ())), preferred_element_type=jnp.float32
            )
            value_grad[window, lanes] += lax.dot_general(
                prob_half, grad, (((0,), (0,)), ((), ())), preferred_element_type=jnp.float32
            )
    for away, block in enumerate((query_own, query_to_one, query_to_two, query_to_three)):
        index = lax.rem(place + away, GROUP)
        block[...] = query_out[pl.ds(pl.multiple_of(index * rows, rows), rows), :]
    far_ref[0] = (key_grad[:edge, :] * scale).astype(jnp.bfloat16)
    far_ref[1] = value_grad[:edge, :].astype(jnp.bfloat16)
    main_ref[0] = (key_grad[edge:, :] * scale).astype(jnp.bfloat16)
    main_ref[1] = value_grad[edge:, :].astype(jnp.bfloat16)


def attend(texts, marks, arrays, key_blocks, query_blocks, edge, chunk, total_rows):
    _, rows, width = key_blocks[0].shape
    heads = width // HEAD
    keys = (2 * GROUP - 1) * rows
    pairs = heads * GROUP * rows * STEPS * rows
    return pl.pallas_call(
        functools.partial(attend_kernel, chunk, total_rows),
        out_shape=(
            *[jax.ShapeDtypeStruct((rows, width), jnp.bfloat16)] * GROUP,
            jax.ShapeDtypeStruct((2, GROUP * rows, width), jnp.bfloat16),
            jax.ShapeDtypeStruct((2, (GROUP - 1) * rows, width), jnp.bfloat16),
        ),
        in_specs=[VMEM] * (len(texts) + 14),
        out_specs=(VMEM,) * (GROUP + 2),
        scratch_shapes=[
            pltpu.VMEM((keys, width), jnp.bfloat16),
            pltpu.VMEM((keys, width), jnp.bfloat16),
            pltpu.VMEM((GROUP * rows, width), jnp.bfloat16),
            pltpu.VMEM((GROUP * rows, width), jnp.bfloat16),
            pltpu.VMEM((keys, width), jnp.float32),
            pltpu.VMEM((keys, width), jnp.float32),
            pltpu.VMEM((GROUP * rows, width), jnp.bfloat16),
        ],
        compiler_params=pltpu.CompilerParams(vmem_limit_bytes=24 * 1024 * 1024),
        cost_estimate=pl.CostEstimate(
            flops=4500000000, bytes_accessed=0, transcendentals=0
        ),
        name="attend",
    )(*texts, *marks, *arrays, *key_blocks, *query_blocks, edge)


def settle_kernel(main_ref, far_ref, *refs):
    extra = refs[: len(refs) // GROUP * GROUP - GROUP]
    outs = refs[len(refs) - GROUP :]
    rows = outs[0].shape[1]
    first_kind = 1 if extra else 0
    place = lax.rem(lax.axis_index("ctx"), GROUP)
    for away, block in enumerate(outs):
        index = lax.rem(place + away, GROUP)
        start = pl.multiple_of(index * rows, rows)
        if extra:
            block[0] = extra[away][...]

        @pl.when(index == 0)
        def first():
            block[first_kind:] = main_ref[:, :rows, :]

        @pl.when(index > 0)
        def later():
            behind = pl.multiple_of(start - rows, rows)
            block[first_kind:] = (
                main_ref[:, pl.ds(start, rows), :].astype(jnp.float32)
                + far_ref[:, pl.ds(behind, rows), :].astype(jnp.float32)
            ).astype(jnp.bfloat16)


def settle(main, far, extra=(), after=()):
    _, total, width = main.shape
    rows = total // GROUP
    count = 2 + (1 if extra else 0)

    def kernel(main_ref, far_ref, *refs):
        refs = list(refs)
        settle_kernel(main_ref, far_ref, *refs[: len(extra)], *refs[-GROUP:])

    return pl.pallas_call(
        kernel,
        out_shape=(jax.ShapeDtypeStruct((count, rows, width), jnp.bfloat16),) * GROUP,
        in_specs=[VMEM, VMEM] + [VMEM] * len(extra) + [ANY] * len(after),
        out_specs=(VMEM,) * GROUP,
        compiler_params=SMALL,
        cost_estimate=pl.CostEstimate(
            flops=SETTLE_COST if extra else 0, bytes_accessed=main.size * 8, transcendentals=0
        ),
        name="settle",
    )(main, far, *extra, *after)


def place_copies(moves, sems):
    copies = []
    for source, target, chunk, away in moves:
        lanes = columns(lax.rem(lax.axis_index("ctx"), GROUP), -away, chunk, source.shape[1])
        copies.append(pltpu.make_async_copy(source, target.at[:, lanes], sems.at[len(copies)]))
    for copy in copies:
        copy.start()
    for copy in copies:
        copy.wait()


def early_kernel(*refs):
    queries, mixed = refs[:GROUP], refs[GROUP : 2 * GROUP]
    query_ref, key_ref, value_ref, sems = refs[2 * GROUP :]
    moves = []
    for away in range(GROUP):
        moves += [
            (queries[away], query_ref, 0, away),
            (mixed[away].at[0], query_ref, 1, away),
            (mixed[away].at[1], key_ref, 0, away),
            (mixed[away].at[2], value_ref, 0, away),
        ]
    place_copies(moves, sems)


def late_kernel(*refs):
    pairs = refs[:GROUP]
    key_ref, value_ref, sems = refs[GROUP + 2 :]
    moves = []
    for away in range(GROUP):
        moves += [
            (pairs[away].at[0], key_ref, 1, away),
            (pairs[away].at[1], value_ref, 1, away),
        ]
    place_copies(moves, sems)


def gathered(queries, mixed, pairs):
    rows, width = queries[0].shape
    out = jax.ShapeDtypeStruct((rows, width * CHUNKS * GROUP), jnp.bfloat16)
    grad_queries, grad_keys, grad_values = pl.pallas_call(
        early_kernel,
        out_shape=(out, out, out),
        in_specs=[VMEM] * (2 * GROUP),
        out_specs=(ANY,) * 3,
        scratch_shapes=[pltpu.SemaphoreType.DMA((4 * GROUP,))],
        compiler_params=SMALL,
        cost_estimate=pl.CostEstimate(flops=0, bytes_accessed=out.size * 6, transcendentals=0),
        name="early",
    )(*queries, *mixed)
    grad_keys, grad_values = pl.pallas_call(
        late_kernel,
        out_shape=(out, out),
        in_specs=[VMEM] * GROUP + [ANY, ANY],
        out_specs=(ANY, ANY),
        input_output_aliases={GROUP: 0, GROUP + 1: 1},
        scratch_shapes=[pltpu.SemaphoreType.DMA((2 * GROUP,))],
        compiler_params=SMALL,
        cost_estimate=pl.CostEstimate(flops=0, bytes_accessed=out.size * 6, transcendentals=0),
        name="late",
    )(*pairs, grad_keys, grad_values)
    return grad_queries, grad_keys, grad_values


def shards(queries, keys, values, grad_out, lengths, image_flags):
    query_rows, key_rows, value_rows, grad_rows = queries[0], keys[0], values[0], grad_out[0]
    row_count = query_rows.shape[0]
    cycle_size = lax.axis_size("ctx")
    samples = lax.axis_size("dp")

    def swap(value, away):
        pairs = [
            (source, source - source % GROUP + (source + away) % GROUP)
            for source in range(cycle_size)
        ]
        return lax.ppermute(value, "ctx", pairs)

    def next_row(value, rows):
        pairs = [(source, (source + rows * GROUP) % cycle_size) for source in range(cycle_size)]
        return lax.ppermute(value, "ctx", pairs)

    def swapped(messages):
        one = swap(messages[0], 1)
        three = swap(messages[2], 3)
        return [one, swap(messages[1], 2), three]

    first_messages, text = first_pack(key_rows, value_rows, lengths, image_flags)
    texts = [text] + [
        lax.ppermute(text, "dp", [(source, (source + away) % samples) for source in range(samples)])
        for away in range(1, samples)
    ]
    total_rows = float(row_count * cycle_size * samples)

    ending = jnp.cumsum(lengths[0])
    bounds = jnp.stack([ending - lengths[0], ending, image_flags[0]])
    bounds = jnp.pad(bounds, ((0, 5), (0, HEAD - bounds.shape[1])))
    key_packs, query_packs, edges = [None] * CHUNKS, [None] * CHUNKS, [None] * CHUNKS
    key_packs[0] = first_messages
    key_packs[1] = pack(key_rows, value_rows, text, 1)
    key_blocks = [swapped(messages) for messages in key_packs]
    edges[0] = make_edge(
        key_rows, value_rows, key_blocks[0], (*texts[1:], key_packs[1][0]), 0, EDGE_COST[0]
    )
    after = edges[0]
    for index in range(CHUNKS):
        query_packs[index] = pack(query_rows, grad_rows, after, index)
        after = query_packs[index][0]
    marks = sides(bounds, after, row_count // 2, cycle_size)
    edges[1] = make_edge(
        key_rows, value_rows, key_blocks[1], (marks[1],), 1, EDGE_COST[1]
    )
    query_blocks = [swapped(messages) for messages in query_packs]
    edges = [next_row(edge, 1) for edge in edges]
    arrays = (query_rows, key_rows, value_rows, grad_rows)
    halves = []
    for chunk in range(CHUNKS):
        *query_grads, main, far = attend(
            texts, marks, arrays,
            key_blocks[chunk], query_blocks[chunk], edges[chunk], chunk, total_rows,
        )
        halves.append((query_grads, main, next_row(far, -1)))
    (first_queries, main, far), (second_queries, last_main, last_far) = halves
    queries = [first_queries[0]] + swapped(first_queries[1:])
    mixed = settle(main, far, extra=second_queries, after=queries[1:])
    pairs = settle(last_main, last_far)
    mixed = [mixed[0]] + swapped(mixed[1:])
    pairs = [pairs[0]] + swapped(pairs[1:])
    grad_queries, grad_keys, grad_values = gathered(queries, mixed, pairs)
    return grad_queries[None], grad_keys[None], grad_values[None]


def solution(mesh):
    in_specs = (
        P("dp", "ctx", None),
        P("dp", "ctx", None),
        P("dp", "ctx", None),
        P("dp", "ctx", None),
        P("dp", None),
        P("dp", None),
    )
    out_specs = (P("dp", "ctx", None), P("dp", "ctx", None), P("dp", "ctx", None))
    return jax.shard_map(shards, mesh=mesh, in_specs=in_specs, out_specs=out_specs, check_vma=False)
```

```python
import functools

import jax
import jax.numpy as jnp
from jax import lax
from jax.experimental import pallas as pl
from jax.experimental.pallas import tpu as pltpu
from jax.sharding import PartitionSpec as P

HEAD = 128
STEPS = 4
GROUP = 4
CHUNKS = 2
LOG2E = 1.4426950408889634
MASKED = -1e30
VMEM = pl.BlockSpec(memory_space=pltpu.VMEM)
ANY = pl.BlockSpec(memory_space=pl.ANY)
LARGE = pltpu.CompilerParams(vmem_limit_bytes=60 * 1024 * 1024)
EDGE_COST = (0, 3000000000)
SETTLE_COST = 0
SMALL = pltpu.CompilerParams(vmem_limit_bytes=10 * 1024 * 1024)


def columns(place, away, chunk, width):
    index = lax.rem(place + GROUP + away, GROUP)
    return pl.ds(pl.multiple_of((index * CHUNKS + chunk) * width, width), width)


def pack_kernel(chunk, first, second, after, one, two, three):
    width = one.shape[2]
    for away, message in ((1, one), (2, two), (3, three)):
        lanes = columns(lax.rem(lax.axis_index("ctx"), GROUP), away, chunk, width)
        message[0] = first[:, lanes]
        message[1] = second[:, lanes]


def first_pack_kernel(first, second, lengths, flags, one, two, three, text, held, sems):
    width = one.shape[2]
    place = lax.rem(lax.axis_index("ctx"), GROUP)
    copies = []
    for away, message in ((1, one), (2, two), (3, three)):
        lanes = columns(place, away, 0, width)
        for part, source in enumerate((first, second)):
            copies.append(
                pltpu.make_async_copy(source.at[:, lanes], message.at[part], sems.at[len(copies)])
            )
    for part, source in enumerate((lengths, flags)):
        copies.append(pltpu.make_async_copy(source, held.at[part], sems.at[len(copies)]))
    for copy in copies:
        copy.start()
    for copy in copies:
        copy.wait()
    text[...] = (held[0] * (1 - held[1])).astype(jnp.float32)


def pack(first, second, after, chunk):
    rows, total = first.shape
    width = total // (GROUP * CHUNKS)
    message = jax.ShapeDtypeStruct((2, rows, width), first.dtype)
    return pl.pallas_call(
        functools.partial(pack_kernel, chunk),
        out_shape=(message,) * (GROUP - 1),
        in_specs=[VMEM, VMEM, ANY],
        out_specs=(VMEM,) * (GROUP - 1),
        compiler_params=SMALL,
        cost_estimate=pl.CostEstimate(flops=0, bytes_accessed=12 * rows * width * 2, transcendentals=0),
        name="pack",
    )(first, second, after)


def first_pack(first, second, lengths, flags):
    rows, total = first.shape
    width = total // (GROUP * CHUNKS)
    message = jax.ShapeDtypeStruct((2, rows, width), first.dtype)
    *messages, text = pl.pallas_call(
        first_pack_kernel,
        out_shape=(message,) * (GROUP - 1) + (jax.ShapeDtypeStruct(lengths.shape, jnp.float32),),
        in_specs=[ANY, ANY, ANY, ANY],
        out_specs=(VMEM,) * GROUP,
        scratch_shapes=[
            pltpu.VMEM((2, *lengths.shape), lengths.dtype),
            pltpu.SemaphoreType.DMA((2 * GROUP,)),
        ],
        compiler_params=LARGE,
        cost_estimate=pl.CostEstimate(flops=0, bytes_accessed=12 * rows * width * 2, transcendentals=0),
        name="first_pack",
    )(first, second, lengths, flags)
    return messages, text


def edge_kernel(chunk, first, second, one, two, three, *refs):
    edge = refs[-1]
    rows = edge.shape[1] // (GROUP - 1)
    width = edge.shape[2]
    place = lax.rem(lax.axis_index("ctx"), GROUP)
    for away, message in enumerate((None, one, two, three)):
        index = lax.rem(place + GROUP - away, GROUP)

        @pl.when(index > 0)
        def put():
            at = pl.ds(pl.multiple_of((index - 1) * rows, rows), rows)
            if message is None:
                lanes = columns(place, 0, chunk, width)
                edge[0, at, :] = first[:, lanes]
                edge[1, at, :] = second[:, lanes]
            else:
                edge[:, at, :] = message[...]


def make_edge(first, second, blocks, afters, chunk, cost):
    _, rows, width = blocks[0].shape
    return pl.pallas_call(
        functools.partial(edge_kernel, chunk),
        out_shape=jax.ShapeDtypeStruct((2, (GROUP - 1) * rows, width), first.dtype),
        in_specs=[VMEM] * 5 + [ANY] * len(afters),
        out_specs=VMEM,
        compiler_params=SMALL,
        cost_estimate=pl.CostEstimate(flops=cost, bytes_accessed=0, transcendentals=0),
        name="edge",
    )(first, second, *blocks, *afters)


def sides_kernel(stretch_rows, cycle_size, bounds_ref, after, limit_ref, text_ref, key_ref):
    rows = 2 * stretch_rows
    device_here = lax.axis_index("ctx")
    start = device_here - lax.rem(device_here, GROUP)
    first = bounds_ref[0:1, :]
    ending = bounds_ref[1:2, :]
    flag = bounds_ref[2:3, :].astype(jnp.float32)
    last = ending.astype(jnp.float32)
    shape = (rows, HEAD)
    offset = lax.broadcasted_iota(jnp.int32, shape, 0)
    for block in range(GROUP):
        device = start + block
        position = jnp.where(
            offset < stretch_rows,
            device * stretch_rows + offset,
            (2 * cycle_size - 2 - device) * stretch_rows + offset,
        )
        inside = (position >= first) & (position < ending)
        image = jnp.sum(jnp.where(inside, flag, 0.0), axis=1, keepdims=True)
        final = jnp.sum(jnp.where(inside, last, 0.0), axis=1, keepdims=True).astype(jnp.int32) - 1
        limit_ref[block] = jnp.where(image > 0.5, final, position)
        text_ref[block] = jnp.broadcast_to(1.0 - image, shape)
        lane = lax.broadcasted_iota(jnp.int32, (8, STEPS * rows), 1)
        step = jnp.zeros_like(lane)
        for edge in range(1, STEPS):
            step = step + (lane >= edge * rows).astype(jnp.int32)
        owner = device - (STEPS - 1) + step
        owner = jnp.where(owner < 0, owner + cycle_size, owner)
        within = lane - step * rows
        key_ref[block] = jnp.where(
            within < stretch_rows,
            owner * stretch_rows + within,
            (2 * cycle_size - 2 - owner) * stretch_rows + within,
        )


def sides(bounds, after, stretch_rows, cycle_size):
    rows = 2 * stretch_rows
    return pl.pallas_call(
        functools.partial(sides_kernel, stretch_rows, cycle_size),
        out_shape=(
            jax.ShapeDtypeStruct((GROUP, rows, HEAD), jnp.int32),
            jax.ShapeDtypeStruct((GROUP, rows, HEAD), jnp.float32),
            jax.ShapeDtypeStruct((GROUP, 8, STEPS * rows), jnp.int32),
        ),
        in_specs=[VMEM, ANY],
        out_specs=(VMEM,) * 3,
        compiler_params=SMALL,
        cost_estimate=pl.CostEstimate(flops=GROUP * rows * HEAD * 8, bytes_accessed=GROUP * rows * HEAD * 8, transcendentals=0),
        name="sides",
    )(bounds, after)


def attend_kernel(
    chunk, total_rows, text_one, text_two, text_three, text_four, limit_ref, text_ref, keypos_ref,
    queries, keys, values, grads, key_one, key_two, key_three, query_one, query_two, query_three,
    edge_ref, *refs,
):
    earlier, refs = refs[: len(refs) - 13], refs[len(refs) - 13 :]
    outs, main_ref, far_ref = refs[:GROUP], refs[GROUP], refs[GROUP + 1]
    key_all, value_all, query_all, grad_all, key_grad, value_grad, query_out = refs[GROUP + 2 :]
    rows, width = queries.shape[0], edge_ref.shape[2]
    edge = (GROUP - 1) * rows
    span = STEPS * rows
    scale = HEAD ** (-0.5)
    place = lax.rem(lax.axis_index("ctx"), GROUP)
    counted = text_one[...] + text_two[...] + text_three[...] + text_four[...]
    factor = total_rows / jnp.sum(counted, axis=1, keepdims=True)
    lanes = columns(place, 0, chunk, width)
    key_all[:edge, :] = edge_ref[0]
    value_all[:edge, :] = edge_ref[1]
    sources = [(keys.at[:, lanes], values.at[:, lanes], queries.at[:, lanes], grads.at[:, lanes])]
    for pair, query_pair in ((key_one, query_one), (key_two, query_two), (key_three, query_three)):
        sources.append((pair.at[0], pair.at[1], query_pair.at[0], query_pair.at[1]))
    for away in range(GROUP):
        start = pl.multiple_of(lax.rem(place + GROUP - away, GROUP) * rows, rows)
        key, value, query, grad = sources[away]
        key_all[pl.ds(edge + start, rows), :] = key[...]
        value_all[pl.ds(edge + start, rows), :] = value[...]
        query_all[pl.ds(start, rows), :] = query[...]
        grad_all[pl.ds(start, rows), :] = grad[...]
    key_grad[...] = jnp.zeros_like(key_grad)
    value_grad[...] = jnp.zeros_like(value_grad)
    for block in range(GROUP):
        at = slice(block * rows, (block + 1) * rows)
        window = slice(block * rows, block * rows + span)
        limit = limit_ref[block]
        allowed = jnp.concatenate(
            [
                keypos_ref[block, 0:1, tile * HEAD : (tile + 1) * HEAD] <= limit
                for tile in range(span // HEAD)
            ],
            axis=1,
        )
        weight = text_ref[block] * factor
        for head in range(width // HEAD):
            lanes = slice(head * HEAD, (head + 1) * HEAD)
            query = query_all[at, lanes]
            grad = (grad_all[at, lanes].astype(jnp.float32) * weight).astype(jnp.bfloat16)
            key = key_all[window, lanes]
            value = value_all[window, lanes]
            scores = lax.dot_general(
                query, key, (((1,), (1,)), ((), ())), preferred_element_type=jnp.float32
            )
            scores = jnp.where(allowed, scores, MASKED)
            largest = jnp.max(scores, axis=1, keepdims=True)
            prob = jnp.exp2((scores - largest) * (scale * LOG2E))
            dprob = lax.dot_general(
                grad, value, (((1,), (1,)), ((), ())), preferred_element_type=jnp.float32
            )
            total = jnp.sum(prob, axis=1, keepdims=True)
            inverse = 1.0 / total
            delta = jnp.sum(prob * dprob, axis=1, keepdims=True) * inverse
            prob = prob * inverse
            dscore = (prob * (dprob - delta)).astype(jnp.bfloat16)
            prob_half = prob.astype(jnp.bfloat16)
            query_out[at, lanes] = (
                jnp.dot(dscore, key, preferred_element_type=jnp.float32) * scale
            ).astype(jnp.bfloat16)
            key_grad[window, lanes] += lax.dot_general(
                dscore, query, (((0,), (0,)), ((), ())), preferred_element_type=jnp.float32
            )
            value_grad[window, lanes] += lax.dot_general(
                prob_half, grad, (((0,), (0,)), ((), ())), preferred_element_type=jnp.float32
            )
    for away, block in enumerate(outs):
        index = lax.rem(place + away, GROUP)
        if earlier:
            block[0] = earlier[away][0]
        block[1 if earlier else 0] = query_out[pl.ds(pl.multiple_of(index * rows, rows), rows), :]
    far_ref[0] = (key_grad[:edge, :] * scale).astype(jnp.bfloat16)
    far_ref[1] = value_grad[:edge, :].astype(jnp.bfloat16)
    main_ref[0] = (key_grad[edge:, :] * scale).astype(jnp.bfloat16)
    main_ref[1] = value_grad[edge:, :].astype(jnp.bfloat16)


def attend(texts, marks, arrays, key_blocks, query_blocks, edge, chunk, total_rows, earlier=()):
    _, rows, width = key_blocks[0].shape
    heads = width // HEAD
    keys = (2 * GROUP - 1) * rows
    pairs = heads * GROUP * rows * STEPS * rows
    return pl.pallas_call(
        functools.partial(attend_kernel, chunk, total_rows),
        out_shape=(
            *[jax.ShapeDtypeStruct((2 if earlier else 1, rows, width), jnp.bfloat16)] * GROUP,
            jax.ShapeDtypeStruct((2, GROUP * rows, width), jnp.bfloat16),
            jax.ShapeDtypeStruct((2, (GROUP - 1) * rows, width), jnp.bfloat16),
        ),
        in_specs=[VMEM] * (len(texts) + 14 + len(earlier)),
        out_specs=(VMEM,) * (GROUP + 2),
        scratch_shapes=[
            pltpu.VMEM((keys, width), jnp.bfloat16),
            pltpu.VMEM((keys, width), jnp.bfloat16),
            pltpu.VMEM((GROUP * rows, width), jnp.bfloat16),
            pltpu.VMEM((GROUP * rows, width), jnp.bfloat16),
            pltpu.VMEM((keys, width), jnp.float32),
            pltpu.VMEM((keys, width), jnp.float32),
            pltpu.VMEM((GROUP * rows, width), jnp.bfloat16),
        ],
        compiler_params=pltpu.CompilerParams(vmem_limit_bytes=24 * 1024 * 1024),
        cost_estimate=pl.CostEstimate(
            flops=4500000000, bytes_accessed=0, transcendentals=0
        ),
        name="attend",
    )(*texts, *marks, *arrays, *key_blocks, *query_blocks, edge, *earlier)


def settle_kernel(main_ref, far_ref, *refs):
    outs = refs[len(refs) - GROUP :]
    rows = outs[0].shape[1]
    place = lax.rem(lax.axis_index("ctx"), GROUP)
    for away, block in enumerate(outs):
        index = lax.rem(place + away, GROUP)
        start = pl.multiple_of(index * rows, rows)

        @pl.when(index == 0)
        def first():
            block[...] = main_ref[:, :rows, :]

        @pl.when(index > 0)
        def later():
            behind = pl.multiple_of(start - rows, rows)
            block[...] = (
                main_ref[:, pl.ds(start, rows), :].astype(jnp.float32)
                + far_ref[:, pl.ds(behind, rows), :].astype(jnp.float32)
            ).astype(jnp.bfloat16)


def settle(main, far, after, cost):
    _, total, width = main.shape
    rows = total // GROUP
    return pl.pallas_call(
        settle_kernel,
        out_shape=(jax.ShapeDtypeStruct((2, rows, width), jnp.bfloat16),) * GROUP,
        in_specs=[VMEM, VMEM] + [ANY] * len(after),
        out_specs=(VMEM,) * GROUP,
        compiler_params=SMALL,
        cost_estimate=pl.CostEstimate(flops=cost, bytes_accessed=main.size * 8, transcendentals=0),
        name="settle",
    )(main, far, *after)


def place_copies(moves, sems):
    copies = []
    for source, target, chunk, away in moves:
        lanes = columns(lax.rem(lax.axis_index("ctx"), GROUP), -away, chunk, source.shape[1])
        copies.append(pltpu.make_async_copy(source, target.at[:, lanes], sems.at[len(copies)]))
    for copy in copies:
        copy.start()
    for copy in copies:
        copy.wait()


def early_kernel(*refs):
    queries, pairs = refs[:GROUP], refs[GROUP : 2 * GROUP]
    query_ref, key_ref, value_ref, sems = refs[2 * GROUP :]
    moves = []
    for away in range(GROUP):
        moves += [
            (queries[away].at[0], query_ref, 0, away),
            (queries[away].at[1], query_ref, 1, away),
            (pairs[away].at[0], key_ref, 0, away),
            (pairs[away].at[1], value_ref, 0, away),
        ]
    place_copies(moves, sems)


def late_kernel(*refs):
    pairs = refs[:GROUP]
    key_ref, value_ref, sems = refs[GROUP + 2 :]
    moves = []
    for away in range(GROUP):
        moves += [
            (pairs[away].at[0], key_ref, 1, away),
            (pairs[away].at[1], value_ref, 1, away),
        ]
    place_copies(moves, sems)


def gathered(queries, mixed, pairs):
    _, rows, width = queries[0].shape
    out = jax.ShapeDtypeStruct((rows, width * CHUNKS * GROUP), jnp.bfloat16)
    grad_queries, grad_keys, grad_values = pl.pallas_call(
        early_kernel,
        out_shape=(out, out, out),
        in_specs=[VMEM] * (2 * GROUP),
        out_specs=(ANY,) * 3,
        scratch_shapes=[pltpu.SemaphoreType.DMA((4 * GROUP,))],
        compiler_params=SMALL,
        cost_estimate=pl.CostEstimate(flops=0, bytes_accessed=out.size * 6, transcendentals=0),
        name="early",
    )(*queries, *mixed)
    grad_keys, grad_values = pl.pallas_call(
        late_kernel,
        out_shape=(out, out),
        in_specs=[VMEM] * GROUP + [ANY, ANY],
        out_specs=(ANY, ANY),
        input_output_aliases={GROUP: 0, GROUP + 1: 1},
        scratch_shapes=[pltpu.SemaphoreType.DMA((2 * GROUP,))],
        compiler_params=SMALL,
        cost_estimate=pl.CostEstimate(flops=0, bytes_accessed=out.size * 6, transcendentals=0),
        name="late",
    )(*pairs, grad_keys, grad_values)
    return grad_queries, grad_keys, grad_values


def shards(queries, keys, values, grad_out, lengths, image_flags):
    query_rows, key_rows, value_rows, grad_rows = queries[0], keys[0], values[0], grad_out[0]
    row_count = query_rows.shape[0]
    cycle_size = lax.axis_size("ctx")
    samples = lax.axis_size("dp")

    def swap(value, away):
        pairs = [
            (source, source - source % GROUP + (source + away) % GROUP)
            for source in range(cycle_size)
        ]
        return lax.ppermute(value, "ctx", pairs)

    def next_row(value, rows):
        pairs = [(source, (source + rows * GROUP) % cycle_size) for source in range(cycle_size)]
        return lax.ppermute(value, "ctx", pairs)

    def swapped(messages):
        one = swap(messages[0], 1)
        three = swap(messages[2], 3)
        return [one, swap(messages[1], 2), three]

    first_messages, text = first_pack(key_rows, value_rows, lengths, image_flags)
    texts = [text] + [
        lax.ppermute(text, "dp", [(source, (source + away) % samples) for source in range(samples)])
        for away in range(1, samples)
    ]
    total_rows = float(row_count * cycle_size * samples)

    ending = jnp.cumsum(lengths[0])
    bounds = jnp.stack([ending - lengths[0], ending, image_flags[0]])
    bounds = jnp.pad(bounds, ((0, 5), (0, HEAD - bounds.shape[1])))
    key_packs, query_packs, edges = [None] * CHUNKS, [None] * CHUNKS, [None] * CHUNKS
    key_packs[0] = first_messages
    key_packs[1] = pack(key_rows, value_rows, text, 1)
    key_blocks = [swapped(messages) for messages in key_packs]
    edges[0] = make_edge(
        key_rows, value_rows, key_blocks[0], (*texts[1:], key_packs[1][0]), 0, EDGE_COST[0]
    )
    after = edges[0]
    for index in range(CHUNKS):
        query_packs[index] = pack(query_rows, grad_rows, after, index)
        after = query_packs[index][0]
    marks = sides(bounds, after, row_count // 2, cycle_size)
    edges[1] = make_edge(
        key_rows, value_rows, key_blocks[1], (marks[1],), 1, EDGE_COST[1]
    )
    query_blocks = [swapped(messages) for messages in query_packs]
    edges = [next_row(edge, 1) for edge in edges]
    arrays = (query_rows, key_rows, value_rows, grad_rows)
    halves = []
    query_grads = ()
    for chunk in range(CHUNKS):
        *query_grads, main, far = attend(
            texts, marks, arrays, key_blocks[chunk], query_blocks[chunk], edges[chunk], chunk,
            total_rows, query_grads,
        )
        halves.append((main, next_row(far, -1)))
    queries = [query_grads[0]] + swapped(query_grads[1:])
    first_pairs = settle(*halves[0], queries[1:], SETTLE_COST)
    last_pairs = settle(*halves[1], first_pairs[:1], 0)
    first_pairs = [first_pairs[0]] + swapped(first_pairs[1:])
    last_pairs = [last_pairs[0]] + swapped(last_pairs[1:])
    grad_queries, grad_keys, grad_values = gathered(queries, first_pairs, last_pairs)
    return grad_queries[None], grad_keys[None], grad_values[None]


def solution(mesh):
    in_specs = (
        P("dp", "ctx", None),
        P("dp", "ctx", None),
        P("dp", "ctx", None),
        P("dp", "ctx", None),
        P("dp", None),
        P("dp", None),
    )
    out_specs = (P("dp", "ctx", None), P("dp", "ctx", None), P("dp", "ctx", None))
    return jax.shard_map(shards, mesh=mesh, in_specs=in_specs, out_specs=out_specs, check_vma=False)
```

```python
import functools

import jax
import jax.numpy as jnp
from jax import lax
from jax.experimental import pallas as pl
from jax.experimental.pallas import tpu as pltpu
from jax.sharding import PartitionSpec as P

HEAD = 128
STEPS = 4
GROUP = 4
CHUNKS = 2
LOG2E = 1.4426950408889634
MASKED = -1e30
VMEM = pl.BlockSpec(memory_space=pltpu.VMEM)
ANY = pl.BlockSpec(memory_space=pl.ANY)
LARGE = pltpu.CompilerParams(vmem_limit_bytes=60 * 1024 * 1024)
EDGE_COST = (0, 3000000000)
SETTLE_COST = 0
SMALL = pltpu.CompilerParams(vmem_limit_bytes=10 * 1024 * 1024)


def columns(place, away, chunk, width):
    index = lax.rem(place + GROUP + away, GROUP)
    return pl.ds(pl.multiple_of((index * CHUNKS + chunk) * width, width), width)


def pack_kernel(chunk, first, second, after, one, two, three):
    width = one.shape[2]
    for away, message in ((1, one), (2, two), (3, three)):
        lanes = columns(lax.rem(lax.axis_index("ctx"), GROUP), away, chunk, width)
        message[0] = first[:, lanes]
        message[1] = second[:, lanes]


def first_pack_kernel(first, second, lengths, flags, one, two, three, text, held, sems):
    width = one.shape[2]
    place = lax.rem(lax.axis_index("ctx"), GROUP)
    copies = []
    for away, message in ((1, one), (2, two), (3, three)):
        lanes = columns(place, away, 0, width)
        for part, source in enumerate((first, second)):
            copies.append(
                pltpu.make_async_copy(source.at[:, lanes], message.at[part], sems.at[len(copies)])
            )
    for part, source in enumerate((lengths, flags)):
        copies.append(pltpu.make_async_copy(source, held.at[part], sems.at[len(copies)]))
    for copy in copies:
        copy.start()
    for copy in copies:
        copy.wait()
    text[...] = (held[0] * (1 - held[1])).astype(jnp.float32)


def pack(first, second, after, chunk):
    rows, total = first.shape
    width = total // (GROUP * CHUNKS)
    message = jax.ShapeDtypeStruct((2, rows, width), first.dtype)
    return pl.pallas_call(
        functools.partial(pack_kernel, chunk),
        out_shape=(message,) * (GROUP - 1),
        in_specs=[VMEM, VMEM, ANY],
        out_specs=(VMEM,) * (GROUP - 1),
        compiler_params=SMALL,
        cost_estimate=pl.CostEstimate(flops=0, bytes_accessed=12 * rows * width * 2, transcendentals=0),
        name="pack",
    )(first, second, after)


def first_pack(first, second, lengths, flags):
    rows, total = first.shape
    width = total // (GROUP * CHUNKS)
    message = jax.ShapeDtypeStruct((2, rows, width), first.dtype)
    *messages, text = pl.pallas_call(
        first_pack_kernel,
        out_shape=(message,) * (GROUP - 1) + (jax.ShapeDtypeStruct(lengths.shape, jnp.float32),),
        in_specs=[ANY, ANY, ANY, ANY],
        out_specs=(VMEM,) * GROUP,
        scratch_shapes=[
            pltpu.VMEM((2, *lengths.shape), lengths.dtype),
            pltpu.SemaphoreType.DMA((2 * GROUP,)),
        ],
        compiler_params=LARGE,
        cost_estimate=pl.CostEstimate(flops=0, bytes_accessed=12 * rows * width * 2, transcendentals=0),
        name="first_pack",
    )(first, second, lengths, flags)
    return messages, text


def edge_kernel(chunk, first, second, one, two, three, *refs):
    edge = refs[-1]
    rows = edge.shape[1] // (GROUP - 1)
    width = edge.shape[2]
    place = lax.rem(lax.axis_index("ctx"), GROUP)
    for away, message in enumerate((None, one, two, three)):
        index = lax.rem(place + GROUP - away, GROUP)

        @pl.when(index > 0)
        def put():
            at = pl.ds(pl.multiple_of((index - 1) * rows, rows), rows)
            if message is None:
                lanes = columns(place, 0, chunk, width)
                edge[0, at, :] = first[:, lanes]
                edge[1, at, :] = second[:, lanes]
            else:
                edge[:, at, :] = message[...]


def make_edge(first, second, blocks, afters, chunk, cost):
    _, rows, width = blocks[0].shape
    return pl.pallas_call(
        functools.partial(edge_kernel, chunk),
        out_shape=jax.ShapeDtypeStruct((2, (GROUP - 1) * rows, width), first.dtype),
        in_specs=[VMEM] * 5 + [ANY] * len(afters),
        out_specs=VMEM,
        compiler_params=SMALL,
        cost_estimate=pl.CostEstimate(flops=cost, bytes_accessed=0, transcendentals=0),
        name="edge",
    )(first, second, *blocks, *afters)


def sides_kernel(stretch_rows, cycle_size, lengths_ref, flags_ref, after, limit_ref, text_ref, key_ref):
    rows = 2 * stretch_rows
    device_here = lax.axis_index("ctx")
    start = device_here - lax.rem(device_here, GROUP)
    segments = lengths_ref.shape[1]
    square = (segments, segments)
    diagonal = lax.broadcasted_iota(jnp.int32, square, 0) == lax.broadcasted_iota(
        jnp.int32, square, 1
    )

    def upright(ref):
        row = jnp.broadcast_to(ref[...].astype(jnp.float32), square)
        return jnp.sum(jnp.where(diagonal, row, 0.0), axis=1, keepdims=True)

    lengths, flags = upright(lengths_ref), upright(flags_ref)
    source = lax.broadcasted_iota(jnp.int32, (segments, HEAD), 0)
    target = lax.broadcasted_iota(jnp.int32, (segments, HEAD), 1)

    def gathered_sum(mask, column):
        return jnp.sum(jnp.where(mask, column, 0.0), axis=0, keepdims=True)

    last = gathered_sum(source <= target, lengths)
    first = gathered_sum(source < target, lengths).astype(jnp.int32)
    flag = gathered_sum(source == target, flags)
    ending = last.astype(jnp.int32)
    shape = (rows, HEAD)
    offset = lax.broadcasted_iota(jnp.int32, shape, 0)
    for block in range(GROUP):
        device = start + block
        position = jnp.where(
            offset < stretch_rows,
            device * stretch_rows + offset,
            (2 * cycle_size - 2 - device) * stretch_rows + offset,
        )
        inside = (position >= first) & (position < ending)
        image = jnp.sum(jnp.where(inside, flag, 0.0), axis=1, keepdims=True)
        final = jnp.sum(jnp.where(inside, last, 0.0), axis=1, keepdims=True).astype(jnp.int32) - 1
        limit_ref[block] = jnp.where(image > 0.5, final, position)
        text_ref[block] = jnp.broadcast_to(1.0 - image, shape)
        lane = lax.broadcasted_iota(jnp.int32, (8, STEPS * rows), 1)
        step = jnp.zeros_like(lane)
        for edge in range(1, STEPS):
            step = step + (lane >= edge * rows).astype(jnp.int32)
        owner = device - (STEPS - 1) + step
        owner = jnp.where(owner < 0, owner + cycle_size, owner)
        within = lane - step * rows
        key_ref[block] = jnp.where(
            within < stretch_rows,
            owner * stretch_rows + within,
            (2 * cycle_size - 2 - owner) * stretch_rows + within,
        )


def sides(lengths, flags, after, stretch_rows, cycle_size):
    rows = 2 * stretch_rows
    return pl.pallas_call(
        functools.partial(sides_kernel, stretch_rows, cycle_size),
        out_shape=(
            jax.ShapeDtypeStruct((GROUP, rows, HEAD), jnp.int32),
            jax.ShapeDtypeStruct((GROUP, rows, HEAD), jnp.float32),
            jax.ShapeDtypeStruct((GROUP, 8, STEPS * rows), jnp.int32),
        ),
        in_specs=[VMEM, VMEM, ANY],
        out_specs=(VMEM,) * 3,
        compiler_params=SMALL,
        cost_estimate=pl.CostEstimate(flops=GROUP * rows * HEAD * 8, bytes_accessed=GROUP * rows * HEAD * 8, transcendentals=0),
        name="sides",
    )(lengths, flags, after)


def attend_kernel(
    chunk, total_rows, text_one, text_two, text_three, text_four, limit_ref, text_ref, keypos_ref,
    queries, keys, values, grads, key_one, key_two, key_three, query_one, query_two, query_three,
    edge_ref, *refs,
):
    earlier, refs = refs[: len(refs) - 13], refs[len(refs) - 13 :]
    outs, main_ref, far_ref = refs[:GROUP], refs[GROUP], refs[GROUP + 1]
    key_all, value_all, query_all, grad_all, key_grad, value_grad, query_out = refs[GROUP + 2 :]
    rows, width = queries.shape[0], edge_ref.shape[2]
    edge = (GROUP - 1) * rows
    span = STEPS * rows
    scale = HEAD ** (-0.5)
    place = lax.rem(lax.axis_index("ctx"), GROUP)
    counted = text_one[...] + text_two[...] + text_three[...] + text_four[...]
    factor = total_rows / jnp.sum(counted, axis=1, keepdims=True)
    lanes = columns(place, 0, chunk, width)
    key_all[:edge, :] = edge_ref[0]
    value_all[:edge, :] = edge_ref[1]
    sources = [(keys.at[:, lanes], values.at[:, lanes], queries.at[:, lanes], grads.at[:, lanes])]
    for pair, query_pair in ((key_one, query_one), (key_two, query_two), (key_three, query_three)):
        sources.append((pair.at[0], pair.at[1], query_pair.at[0], query_pair.at[1]))
    for away in range(GROUP):
        start = pl.multiple_of(lax.rem(place + GROUP - away, GROUP) * rows, rows)
        key, value, query, grad = sources[away]
        key_all[pl.ds(edge + start, rows), :] = key[...]
        value_all[pl.ds(edge + start, rows), :] = value[...]
        query_all[pl.ds(start, rows), :] = query[...]
        grad_all[pl.ds(start, rows), :] = grad[...]
    key_grad[...] = jnp.zeros_like(key_grad)
    value_grad[...] = jnp.zeros_like(value_grad)
    for block in range(GROUP):
        at = slice(block * rows, (block + 1) * rows)
        window = slice(block * rows, block * rows + span)
        limit = limit_ref[block]
        allowed = jnp.concatenate(
            [
                keypos_ref[block, 0:1, tile * HEAD : (tile + 1) * HEAD] <= limit
                for tile in range(span // HEAD)
            ],
            axis=1,
        )
        weight = text_ref[block] * factor
        for head in range(width // HEAD):
            lanes = slice(head * HEAD, (head + 1) * HEAD)
            query = query_all[at, lanes]
            grad = (grad_all[at, lanes].astype(jnp.float32) * weight).astype(jnp.bfloat16)
            key = key_all[window, lanes]
            value = value_all[window, lanes]
            scores = lax.dot_general(
                query, key, (((1,), (1,)), ((), ())), preferred_element_type=jnp.float32
            )
            scores = jnp.where(allowed, scores, MASKED)
            largest = jnp.max(scores, axis=1, keepdims=True)
            prob = jnp.exp2((scores - largest) * (scale * LOG2E))
            dprob = lax.dot_general(
                grad, value, (((1,), (1,)), ((), ())), preferred_element_type=jnp.float32
            )
            total = jnp.sum(prob, axis=1, keepdims=True)
            inverse = 1.0 / total
            delta = jnp.sum(prob * dprob, axis=1, keepdims=True) * inverse
            prob = prob * inverse
            dscore = (prob * (dprob - delta)).astype(jnp.bfloat16)
            prob_half = prob.astype(jnp.bfloat16)
            query_out[at, lanes] = (
                jnp.dot(dscore, key, preferred_element_type=jnp.float32) * scale
            ).astype(jnp.bfloat16)
            key_grad[window, lanes] += lax.dot_general(
                dscore, query, (((0,), (0,)), ((), ())), preferred_element_type=jnp.float32
            )
            value_grad[window, lanes] += lax.dot_general(
                prob_half, grad, (((0,), (0,)), ((), ())), preferred_element_type=jnp.float32
            )
    for away, block in enumerate(outs):
        index = lax.rem(place + away, GROUP)
        if earlier:
            block[0] = earlier[away][0]
        block[1 if earlier else 0] = query_out[pl.ds(pl.multiple_of(index * rows, rows), rows), :]
    far_ref[0] = (key_grad[:edge, :] * scale).astype(jnp.bfloat16)
    far_ref[1] = value_grad[:edge, :].astype(jnp.bfloat16)
    main_ref[0] = (key_grad[edge:, :] * scale).astype(jnp.bfloat16)
    main_ref[1] = value_grad[edge:, :].astype(jnp.bfloat16)


def attend(texts, marks, arrays, key_blocks, query_blocks, edge, chunk, total_rows, earlier=()):
    _, rows, width = key_blocks[0].shape
    heads = width // HEAD
    keys = (2 * GROUP - 1) * rows
    pairs = heads * GROUP * rows * STEPS * rows
    return pl.pallas_call(
        functools.partial(attend_kernel, chunk, total_rows),
        out_shape=(
            *[jax.ShapeDtypeStruct((2 if earlier else 1, rows, width), jnp.bfloat16)] * GROUP,
            jax.ShapeDtypeStruct((2, GROUP * rows, width), jnp.bfloat16),
            jax.ShapeDtypeStruct((2, (GROUP - 1) * rows, width), jnp.bfloat16),
        ),
        in_specs=[VMEM] * (len(texts) + 14 + len(earlier)),
        out_specs=(VMEM,) * (GROUP + 2),
        scratch_shapes=[
            pltpu.VMEM((keys, width), jnp.bfloat16),
            pltpu.VMEM((keys, width), jnp.bfloat16),
            pltpu.VMEM((GROUP * rows, width), jnp.bfloat16),
            pltpu.VMEM((GROUP * rows, width), jnp.bfloat16),
            pltpu.VMEM((keys, width), jnp.float32),
            pltpu.VMEM((keys, width), jnp.float32),
            pltpu.VMEM((GROUP * rows, width), jnp.bfloat16),
        ],
        compiler_params=pltpu.CompilerParams(vmem_limit_bytes=24 * 1024 * 1024),
        cost_estimate=pl.CostEstimate(
            flops=4500000000, bytes_accessed=0, transcendentals=0
        ),
        name="attend",
    )(*texts, *marks, *arrays, *key_blocks, *query_blocks, edge, *earlier)


def settle_kernel(main_ref, far_ref, *refs):
    outs = refs[len(refs) - GROUP :]
    rows = outs[0].shape[1]
    place = lax.rem(lax.axis_index("ctx"), GROUP)
    for away, block in enumerate(outs):
        index = lax.rem(place + away, GROUP)
        start = pl.multiple_of(index * rows, rows)

        @pl.when(index == 0)
        def first():
            block[...] = main_ref[:, :rows, :]

        @pl.when(index > 0)
        def later():
            behind = pl.multiple_of(start - rows, rows)
            block[...] = (
                main_ref[:, pl.ds(start, rows), :].astype(jnp.float32)
                + far_ref[:, pl.ds(behind, rows), :].astype(jnp.float32)
            ).astype(jnp.bfloat16)


def settle(main, far, after, cost):
    _, total, width = main.shape
    rows = total // GROUP
    return pl.pallas_call(
        settle_kernel,
        out_shape=(jax.ShapeDtypeStruct((2, rows, width), jnp.bfloat16),) * GROUP,
        in_specs=[VMEM, VMEM] + [ANY] * len(after),
        out_specs=(VMEM,) * GROUP,
        compiler_params=SMALL,
        cost_estimate=pl.CostEstimate(flops=cost, bytes_accessed=main.size * 8, transcendentals=0),
        name="settle",
    )(main, far, *after)


def place_copies(moves, sems):
    copies = []
    for source, target, chunk, away in moves:
        lanes = columns(lax.rem(lax.axis_index("ctx"), GROUP), -away, chunk, source.shape[1])
        copies.append(pltpu.make_async_copy(source, target.at[:, lanes], sems.at[len(copies)]))
    for copy in copies:
        copy.start()
    for copy in copies:
        copy.wait()


def early_kernel(*refs):
    queries, pairs = refs[:GROUP], refs[GROUP : 2 * GROUP]
    query_ref, key_ref, value_ref, sems = refs[2 * GROUP :]
    moves = []
    for away in range(GROUP):
        moves += [
            (queries[away].at[0], query_ref, 0, away),
            (queries[away].at[1], query_ref, 1, away),
            (pairs[away].at[0], key_ref, 0, away),
            (pairs[away].at[1], value_ref, 0, away),
        ]
    place_copies(moves, sems)


def late_kernel(*refs):
    pairs = refs[:GROUP]
    key_ref, value_ref, sems = refs[GROUP + 2 :]
    moves = []
    for away in range(GROUP):
        moves += [
            (pairs[away].at[0], key_ref, 1, away),
            (pairs[away].at[1], value_ref, 1, away),
        ]
    place_copies(moves, sems)


def gathered(queries, mixed, pairs):
    _, rows, width = queries[0].shape
    out = jax.ShapeDtypeStruct((rows, width * CHUNKS * GROUP), jnp.bfloat16)
    grad_queries, grad_keys, grad_values = pl.pallas_call(
        early_kernel,
        out_shape=(out, out, out),
        in_specs=[VMEM] * (2 * GROUP),
        out_specs=(ANY,) * 3,
        scratch_shapes=[pltpu.SemaphoreType.DMA((4 * GROUP,))],
        compiler_params=SMALL,
        cost_estimate=pl.CostEstimate(flops=0, bytes_accessed=out.size * 6, transcendentals=0),
        name="early",
    )(*queries, *mixed)
    grad_keys, grad_values = pl.pallas_call(
        late_kernel,
        out_shape=(out, out),
        in_specs=[VMEM] * GROUP + [ANY, ANY],
        out_specs=(ANY, ANY),
        input_output_aliases={GROUP: 0, GROUP + 1: 1},
        scratch_shapes=[pltpu.SemaphoreType.DMA((2 * GROUP,))],
        compiler_params=SMALL,
        cost_estimate=pl.CostEstimate(flops=0, bytes_accessed=out.size * 6, transcendentals=0),
        name="late",
    )(*pairs, grad_keys, grad_values)
    return grad_queries, grad_keys, grad_values


def shards(queries, keys, values, grad_out, lengths, image_flags):
    query_rows, key_rows, value_rows, grad_rows = queries[0], keys[0], values[0], grad_out[0]
    row_count = query_rows.shape[0]
    cycle_size = lax.axis_size("ctx")
    samples = lax.axis_size("dp")

    def swap(value, away):
        pairs = [
            (source, source - source % GROUP + (source + away) % GROUP)
            for source in range(cycle_size)
        ]
        return lax.ppermute(value, "ctx", pairs)

    def next_row(value, rows):
        pairs = [(source, (source + rows * GROUP) % cycle_size) for source in range(cycle_size)]
        return lax.ppermute(value, "ctx", pairs)

    def swapped(messages):
        one = swap(messages[0], 1)
        three = swap(messages[2], 3)
        return [one, swap(messages[1], 2), three]

    first_messages, text = first_pack(key_rows, value_rows, lengths, image_flags)
    texts = [text] + [
        lax.ppermute(text, "dp", [(source, (source + away) % samples) for source in range(samples)])
        for away in range(1, samples)
    ]
    total_rows = float(row_count * cycle_size * samples)

    key_packs, query_packs, edges = [None] * CHUNKS, [None] * CHUNKS, [None] * CHUNKS
    key_packs[0] = first_messages
    key_packs[1] = pack(key_rows, value_rows, text, 1)
    key_blocks = [swapped(messages) for messages in key_packs]
    edges[0] = make_edge(
        key_rows, value_rows, key_blocks[0], (*texts[1:], key_packs[1][0]), 0, EDGE_COST[0]
    )
    after = edges[0]
    for index in range(CHUNKS):
        query_packs[index] = pack(query_rows, grad_rows, after, index)
        after = query_packs[index][0]
    marks = sides(lengths, image_flags, after, row_count // 2, cycle_size)
    edges[1] = make_edge(
        key_rows, value_rows, key_blocks[1], (marks[1],), 1, EDGE_COST[1]
    )
    query_blocks = [swapped(messages) for messages in query_packs]
    edges = [next_row(edge, 1) for edge in edges]
    arrays = (query_rows, key_rows, value_rows, grad_rows)
    halves = []
    query_grads = ()
    for chunk in range(CHUNKS):
        *query_grads, main, far = attend(
            texts, marks, arrays, key_blocks[chunk], query_blocks[chunk], edges[chunk], chunk,
            total_rows, query_grads,
        )
        halves.append((main, next_row(far, -1)))
    queries = [query_grads[0]] + swapped(query_grads[1:])
    first_pairs = settle(*halves[0], queries[1:], SETTLE_COST)
    last_pairs = settle(*halves[1], first_pairs[:1], 0)
    first_pairs = [first_pairs[0]] + swapped(first_pairs[1:])
    last_pairs = [last_pairs[0]] + swapped(last_pairs[1:])
    grad_queries, grad_keys, grad_values = gathered(queries, first_pairs, last_pairs)
    return grad_queries[None], grad_keys[None], grad_values[None]


def solution(mesh):
    in_specs = (
        P("dp", "ctx", None),
        P("dp", "ctx", None),
        P("dp", "ctx", None),
        P("dp", "ctx", None),
        P("dp", None),
        P("dp", None),
    )
    out_specs = (P("dp", "ctx", None), P("dp", "ctx", None), P("dp", "ctx", None))
    return jax.shard_map(shards, mesh=mesh, in_specs=in_specs, out_specs=out_specs, check_vma=False)
```

```python
import functools

import jax
import jax.numpy as jnp
from jax import lax
from jax.experimental import pallas as pl
from jax.experimental.pallas import tpu as pltpu
from jax.sharding import PartitionSpec as P

HEAD = 128
STEPS = 4
GROUP = 4
CHUNKS = 2
LOG2E = 1.4426950408889634
MASKED = -1e30
VMEM = pl.BlockSpec(memory_space=pltpu.VMEM)
ANY = pl.BlockSpec(memory_space=pl.ANY)
LARGE = pltpu.CompilerParams(vmem_limit_bytes=60 * 1024 * 1024)
EDGE_COST = (0, 6000000000)
SETTLE_COST = 3000000000
SMALL = pltpu.CompilerParams(vmem_limit_bytes=10 * 1024 * 1024)


def aways():
    core = lax.rem(lax.axis_index("dp"), 2)
    return 0, 1 + 2 * core, 3 - 2 * core, 2


def columns(place, away, chunk, width):
    index = lax.rem(place + GROUP + away, GROUP)
    return pl.ds(pl.multiple_of((index * CHUNKS + chunk) * width, width), width)


def pack_kernel(chunk, first, second, after, one, two, three):
    width = one.shape[2]
    for away, message in zip(aways()[1:], (one, two, three)):
        lanes = columns(lax.rem(lax.axis_index("ctx"), GROUP), away, chunk, width)
        message[0] = first[:, lanes]
        message[1] = second[:, lanes]


def first_pack_kernel(first, second, lengths, flags, one, two, three, text, held, sems):
    width = one.shape[2]
    place = lax.rem(lax.axis_index("ctx"), GROUP)
    copies = []
    for away, message in zip(aways()[1:], (one, two, three)):
        lanes = columns(place, away, 0, width)
        for part, source in enumerate((first, second)):
            copies.append(
                pltpu.make_async_copy(source.at[:, lanes], message.at[part], sems.at[len(copies)])
            )
    for part, source in enumerate((lengths, flags)):
        copies.append(pltpu.make_async_copy(source, held.at[part], sems.at[len(copies)]))
    for copy in copies:
        copy.start()
    for copy in copies:
        copy.wait()
    text[...] = (held[0] * (1 - held[1])).astype(jnp.float32)


def pack(first, second, after, chunk):
    rows, total = first.shape
    width = total // (GROUP * CHUNKS)
    message = jax.ShapeDtypeStruct((2, rows, width), first.dtype)
    return pl.pallas_call(
        functools.partial(pack_kernel, chunk),
        out_shape=(message,) * (GROUP - 1),
        in_specs=[VMEM, VMEM, ANY],
        out_specs=(VMEM,) * (GROUP - 1),
        compiler_params=SMALL,
        cost_estimate=pl.CostEstimate(flops=0, bytes_accessed=12 * rows * width * 2, transcendentals=0),
        name="pack",
    )(first, second, after)


def first_pack(first, second, lengths, flags):
    rows, total = first.shape
    width = total // (GROUP * CHUNKS)
    message = jax.ShapeDtypeStruct((2, rows, width), first.dtype)
    *messages, text = pl.pallas_call(
        first_pack_kernel,
        out_shape=(message,) * (GROUP - 1) + (jax.ShapeDtypeStruct(lengths.shape, jnp.float32),),
        in_specs=[ANY, ANY, ANY, ANY],
        out_specs=(VMEM,) * GROUP,
        scratch_shapes=[
            pltpu.VMEM((2, *lengths.shape), lengths.dtype),
            pltpu.SemaphoreType.DMA((2 * GROUP,)),
        ],
        compiler_params=LARGE,
        cost_estimate=pl.CostEstimate(flops=0, bytes_accessed=12 * rows * width * 2, transcendentals=0),
        name="first_pack",
    )(first, second, lengths, flags)
    return messages, text


def edge_kernel(chunk, first, second, one, two, three, *refs):
    edge = refs[-1]
    rows = edge.shape[1] // (GROUP - 1)
    width = edge.shape[2]
    place = lax.rem(lax.axis_index("ctx"), GROUP)
    for away, message in zip(aways(), (None, one, two, three)):
        index = lax.rem(place + GROUP - away, GROUP)

        @pl.when(index > 0)
        def put():
            at = pl.ds(pl.multiple_of((index - 1) * rows, rows), rows)
            if message is None:
                lanes = columns(place, 0, chunk, width)
                edge[0, at, :] = first[:, lanes]
                edge[1, at, :] = second[:, lanes]
            else:
                edge[:, at, :] = message[...]


def make_edge(first, second, blocks, afters, chunk, cost):
    _, rows, width = blocks[0].shape
    return pl.pallas_call(
        functools.partial(edge_kernel, chunk),
        out_shape=jax.ShapeDtypeStruct((2, (GROUP - 1) * rows, width), first.dtype),
        in_specs=[VMEM] * 5 + [ANY] * len(afters),
        out_specs=VMEM,
        compiler_params=SMALL,
        cost_estimate=pl.CostEstimate(flops=cost, bytes_accessed=0, transcendentals=0),
        name="edge",
    )(first, second, *blocks, *afters)


def sides_kernel(stretch_rows, cycle_size, lengths_ref, flags_ref, after, limit_ref, text_ref, key_ref):
    rows = 2 * stretch_rows
    device_here = lax.axis_index("ctx")
    start = device_here - lax.rem(device_here, GROUP)
    segments = lengths_ref.shape[1]
    square = (segments, segments)
    diagonal = lax.broadcasted_iota(jnp.int32, square, 0) == lax.broadcasted_iota(
        jnp.int32, square, 1
    )

    def upright(ref):
        row = jnp.broadcast_to(ref[...].astype(jnp.float32), square)
        return jnp.sum(jnp.where(diagonal, row, 0.0), axis=1, keepdims=True)

    lengths, flags = upright(lengths_ref), upright(flags_ref)
    source = lax.broadcasted_iota(jnp.int32, (segments, HEAD), 0)
    target = lax.broadcasted_iota(jnp.int32, (segments, HEAD), 1)

    def gathered_sum(mask, column):
        return jnp.sum(jnp.where(mask, column, 0.0), axis=0, keepdims=True)

    last = gathered_sum(source <= target, lengths)
    first = gathered_sum(source < target, lengths).astype(jnp.int32)
    flag = gathered_sum(source == target, flags)
    ending = last.astype(jnp.int32)
    shape = (rows, HEAD)
    offset = lax.broadcasted_iota(jnp.int32, shape, 0)
    for block in range(GROUP):
        device = start + block
        position = jnp.where(
            offset < stretch_rows,
            device * stretch_rows + offset,
            (2 * cycle_size - 2 - device) * stretch_rows + offset,
        )
        inside = (position >= first) & (position < ending)
        image = jnp.sum(jnp.where(inside, flag, 0.0), axis=1, keepdims=True)
        final = jnp.sum(jnp.where(inside, last, 0.0), axis=1, keepdims=True).astype(jnp.int32) - 1
        limit_ref[block] = jnp.where(image > 0.5, final, position)
        text_ref[block] = jnp.broadcast_to(1.0 - image, shape)
        lane = lax.broadcasted_iota(jnp.int32, (8, STEPS * rows), 1)
        step = jnp.zeros_like(lane)
        for edge in range(1, STEPS):
            step = step + (lane >= edge * rows).astype(jnp.int32)
        owner = device - (STEPS - 1) + step
        owner = jnp.where(owner < 0, owner + cycle_size, owner)
        within = lane - step * rows
        key_ref[block] = jnp.where(
            within < stretch_rows,
            owner * stretch_rows + within,
            (2 * cycle_size - 2 - owner) * stretch_rows + within,
        )


def sides(lengths, flags, after, stretch_rows, cycle_size):
    rows = 2 * stretch_rows
    return pl.pallas_call(
        functools.partial(sides_kernel, stretch_rows, cycle_size),
        out_shape=(
            jax.ShapeDtypeStruct((GROUP, rows, HEAD), jnp.int32),
            jax.ShapeDtypeStruct((GROUP, rows, HEAD), jnp.float32),
            jax.ShapeDtypeStruct((GROUP, 8, STEPS * rows), jnp.int32),
        ),
        in_specs=[VMEM, VMEM, ANY],
        out_specs=(VMEM,) * 3,
        compiler_params=SMALL,
        cost_estimate=pl.CostEstimate(flops=GROUP * rows * HEAD * 8, bytes_accessed=GROUP * rows * HEAD * 8, transcendentals=0),
        name="sides",
    )(lengths, flags, after)


def attend_kernel(
    chunk, total_rows, text_one, text_two, text_three, text_four, limit_ref, text_ref, keypos_ref,
    queries, keys, values, grads, key_one, key_two, key_three, query_one, query_two, query_three,
    edge_ref, query_own, query_to_one, query_to_two, query_to_three, main_ref, far_ref,
    key_all, value_all, query_all, grad_all, key_grad, value_grad, query_out,
):
    rows, width = queries.shape[0], edge_ref.shape[2]
    edge = (GROUP - 1) * rows
    span = STEPS * rows
    scale = HEAD ** (-0.5)
    place = lax.rem(lax.axis_index("ctx"), GROUP)
    counted = text_one[...] + text_two[...] + text_three[...] + text_four[...]
    factor = total_rows / jnp.sum(counted, axis=1, keepdims=True)
    lanes = columns(place, 0, chunk, width)
    key_all[:edge, :] = edge_ref[0]
    value_all[:edge, :] = edge_ref[1]
    sources = [(keys.at[:, lanes], values.at[:, lanes], queries.at[:, lanes], grads.at[:, lanes])]
    for pair, query_pair in ((key_one, query_one), (key_two, query_two), (key_three, query_three)):
        sources.append((pair.at[0], pair.at[1], query_pair.at[0], query_pair.at[1]))
    for slot, away in enumerate(aways()):
        start = pl.multiple_of(lax.rem(place + GROUP - away, GROUP) * rows, rows)
        key, value, query, grad = sources[slot]
        key_all[pl.ds(edge + start, rows), :] = key[...]
        value_all[pl.ds(edge + start, rows), :] = value[...]
        query_all[pl.ds(start, rows), :] = query[...]
        grad_all[pl.ds(start, rows), :] = grad[...]
    key_grad[...] = jnp.zeros_like(key_grad)
    value_grad[...] = jnp.zeros_like(value_grad)
    for block in range(GROUP):
        at = slice(block * rows, (block + 1) * rows)
        window = slice(block * rows, block * rows + span)
        limit = limit_ref[block]
        allowed = jnp.concatenate(
            [
                keypos_ref[block, 0:1, tile * HEAD : (tile + 1) * HEAD] <= limit
                for tile in range(span // HEAD)
            ],
            axis=1,
        )
        weight = text_ref[block] * factor
        for head in range(width // HEAD):
            lanes = slice(head * HEAD, (head + 1) * HEAD)
            query = query_all[at, lanes]
            grad = (grad_all[at, lanes].astype(jnp.float32) * weight).astype(jnp.bfloat16)
            key = key_all[window, lanes]
            value = value_all[window, lanes]
            scores = lax.dot_general(
                query, key, (((1,), (1,)), ((), ())), preferred_element_type=jnp.float32
            )
            scores = jnp.where(allowed, scores, MASKED)
            largest = jnp.max(scores, axis=1, keepdims=True)
            prob = jnp.exp2((scores - largest) * (scale * LOG2E))
            dprob = lax.dot_general(
                grad, value, (((1,), (1,)), ((), ())), preferred_element_type=jnp.float32
            )
            total = jnp.sum(prob, axis=1, keepdims=True)
            inverse = 1.0 / total
            delta = jnp.sum(prob * dprob, axis=1, keepdims=True) * inverse
            prob = prob * inverse
            dscore = (prob * (dprob - delta)).astype(jnp.bfloat16)
            prob_half = prob.astype(jnp.bfloat16)
            query_out[at, lanes] = (
                jnp.dot(dscore, key, preferred_element_type=jnp.float32) * scale
            ).astype(jnp.bfloat16)
            key_grad[window, lanes] += lax.dot_general(
                dscore, query, (((0,), (0,)), ((), ())), preferred_element_type=jnp.float32
            )
            value_grad[window, lanes] += lax.dot_general(
                prob_half, grad, (((0,), (0,)), ((), ())), preferred_element_type=jnp.float32
            )
    for away, block in zip(aways(), (query_own, query_to_one, query_to_two, query_to_three)):
        index = lax.rem(place + away, GROUP)
        block[...] = query_out[pl.ds(pl.multiple_of(index * rows, rows), rows), :]
    far_ref[0] = (key_grad[:edge, :] * scale).astype(jnp.bfloat16)
    far_ref[1] = value_grad[:edge, :].astype(jnp.bfloat16)
    main_ref[0] = (key_grad[edge:, :] * scale).astype(jnp.bfloat16)
    main_ref[1] = value_grad[edge:, :].astype(jnp.bfloat16)


def attend(texts, marks, arrays, key_blocks, query_blocks, edge, chunk, total_rows):
    _, rows, width = key_blocks[0].shape
    heads = width // HEAD
    keys = (2 * GROUP - 1) * rows
    pairs = heads * GROUP * rows * STEPS * rows
    return pl.pallas_call(
        functools.partial(attend_kernel, chunk, total_rows),
        out_shape=(
            *[jax.ShapeDtypeStruct((rows, width), jnp.bfloat16)] * GROUP,
            jax.ShapeDtypeStruct((2, GROUP * rows, width), jnp.bfloat16),
            jax.ShapeDtypeStruct((2, (GROUP - 1) * rows, width), jnp.bfloat16),
        ),
        in_specs=[VMEM] * (len(texts) + 14),
        out_specs=(VMEM,) * (GROUP + 2),
        scratch_shapes=[
            pltpu.VMEM((keys, width), jnp.bfloat16),
            pltpu.VMEM((keys, width), jnp.bfloat16),
            pltpu.VMEM((GROUP * rows, width), jnp.bfloat16),
            pltpu.VMEM((GROUP * rows, width), jnp.bfloat16),
            pltpu.VMEM((keys, width), jnp.float32),
            pltpu.VMEM((keys, width), jnp.float32),
            pltpu.VMEM((GROUP * rows, width), jnp.bfloat16),
        ],
        compiler_params=pltpu.CompilerParams(vmem_limit_bytes=24 * 1024 * 1024),
        cost_estimate=pl.CostEstimate(
            flops=4500000000, bytes_accessed=0, transcendentals=0
        ),
        name="attend",
    )(*texts, *marks, *arrays, *key_blocks, *query_blocks, edge)


def settle_kernel(main_ref, far_ref, *refs):
    extra = refs[: len(refs) // GROUP * GROUP - GROUP]
    outs = refs[len(refs) - GROUP :]
    rows = outs[0].shape[1]
    first_kind = 1 if extra else 0
    place = lax.rem(lax.axis_index("ctx"), GROUP)
    for slot, (away, block) in enumerate(zip(aways(), outs)):
        index = lax.rem(place + away, GROUP)
        start = pl.multiple_of(index * rows, rows)
        if extra:
            block[0] = extra[slot][...]

        @pl.when(index == 0)
        def first():
            block[first_kind:] = main_ref[:, :rows, :]

        @pl.when(index > 0)
        def later():
            behind = pl.multiple_of(start - rows, rows)
            block[first_kind:] = (
                main_ref[:, pl.ds(start, rows), :].astype(jnp.float32)
                + far_ref[:, pl.ds(behind, rows), :].astype(jnp.float32)
            ).astype(jnp.bfloat16)


def settle(main, far, extra=(), after=()):
    _, total, width = main.shape
    rows = total // GROUP
    count = 2 + (1 if extra else 0)

    def kernel(main_ref, far_ref, *refs):
        refs = list(refs)
        settle_kernel(main_ref, far_ref, *refs[: len(extra)], *refs[-GROUP:])

    return pl.pallas_call(
        kernel,
        out_shape=(jax.ShapeDtypeStruct((count, rows, width), jnp.bfloat16),) * GROUP,
        in_specs=[VMEM, VMEM] + [VMEM] * len(extra) + [ANY] * len(after),
        out_specs=(VMEM,) * GROUP,
        compiler_params=SMALL,
        cost_estimate=pl.CostEstimate(
            flops=SETTLE_COST if extra else 0, bytes_accessed=main.size * 8, transcendentals=0
        ),
        name="settle",
    )(main, far, *extra, *after)


def place_copies(moves, sems):
    copies = []
    for source, target, chunk, slot in moves:
        lanes = columns(lax.rem(lax.axis_index("ctx"), GROUP), -aways()[slot], chunk, source.shape[1])
        copies.append(pltpu.make_async_copy(source, target.at[:, lanes], sems.at[len(copies)]))
    for copy in copies:
        copy.start()
    for copy in copies:
        copy.wait()


def early_kernel(*refs):
    queries, mixed = refs[:GROUP], refs[GROUP : 2 * GROUP]
    query_ref, key_ref, value_ref, sems = refs[2 * GROUP :]
    moves = []
    for away in range(GROUP):
        moves += [
            (queries[away], query_ref, 0, away),
            (mixed[away].at[0], query_ref, 1, away),
            (mixed[away].at[1], key_ref, 0, away),
            (mixed[away].at[2], value_ref, 0, away),
        ]
    place_copies(moves, sems)


def late_kernel(*refs):
    pairs = refs[:GROUP]
    key_ref, value_ref, sems = refs[GROUP + 2 :]
    moves = []
    for away in range(GROUP):
        moves += [
            (pairs[away].at[0], key_ref, 1, away),
            (pairs[away].at[1], value_ref, 1, away),
        ]
    place_copies(moves, sems)


def gathered(queries, mixed, pairs):
    rows, width = queries[0].shape
    out = jax.ShapeDtypeStruct((rows, width * CHUNKS * GROUP), jnp.bfloat16)
    grad_queries, grad_keys, grad_values = pl.pallas_call(
        early_kernel,
        out_shape=(out, out, out),
        in_specs=[VMEM] * (2 * GROUP),
        out_specs=(ANY,) * 3,
        scratch_shapes=[pltpu.SemaphoreType.DMA((4 * GROUP,))],
        compiler_params=SMALL,
        cost_estimate=pl.CostEstimate(flops=0, bytes_accessed=out.size * 6, transcendentals=0),
        name="early",
    )(*queries, *mixed)
    grad_keys, grad_values = pl.pallas_call(
        late_kernel,
        out_shape=(out, out),
        in_specs=[VMEM] * GROUP + [ANY, ANY],
        out_specs=(ANY, ANY),
        input_output_aliases={GROUP: 0, GROUP + 1: 1},
        scratch_shapes=[pltpu.SemaphoreType.DMA((2 * GROUP,))],
        compiler_params=SMALL,
        cost_estimate=pl.CostEstimate(flops=0, bytes_accessed=out.size * 6, transcendentals=0),
        name="late",
    )(*pairs, grad_keys, grad_values)
    return grad_queries, grad_keys, grad_values


def shards(queries, keys, values, grad_out, lengths, image_flags):
    query_rows, key_rows, value_rows, grad_rows = queries[0], keys[0], values[0], grad_out[0]
    row_count = query_rows.shape[0]
    cycle_size = lax.axis_size("ctx")
    samples = lax.axis_size("dp")

    def swap(value, slot):
        pairs = []
        for sample in range(samples):
            core = sample % 2
            away = (1 + 2 * core, 3 - 2 * core, 2)[slot]
            for source in range(cycle_size):
                target = source - source % GROUP + (source + away) % GROUP
                pairs.append((sample * cycle_size + source, sample * cycle_size + target))
        return lax.ppermute(value, ("dp", "ctx"), pairs)

    def next_row(value, rows):
        pairs = [(source, (source + rows * GROUP) % cycle_size) for source in range(cycle_size)]
        return lax.ppermute(value, "ctx", pairs)

    def swapped(messages):
        return [swap(message, slot) for slot, message in enumerate(messages)]

    first_messages, text = first_pack(key_rows, value_rows, lengths, image_flags)
    texts = [text] + [
        lax.ppermute(text, "dp", [(source, (source + away) % samples) for source in range(samples)])
        for away in range(1, samples)
    ]
    total_rows = float(row_count * cycle_size * samples)

    key_packs, query_packs, edges = [None] * CHUNKS, [None] * CHUNKS, [None] * CHUNKS
    key_packs[0] = first_messages
    key_packs[1] = pack(key_rows, value_rows, text, 1)
    key_blocks = [swapped(messages) for messages in key_packs]
    edges[0] = make_edge(
        key_rows, value_rows, key_blocks[0], (*texts[1:], key_packs[1][0]), 0, EDGE_COST[0]
    )
    after = edges[0]
    for index in range(CHUNKS):
        query_packs[index] = pack(query_rows, grad_rows, after, index)
        after = query_packs[index][0]
    marks = sides(lengths, image_flags, after, row_count // 2, cycle_size)
    edges[1] = make_edge(
        key_rows, value_rows, key_blocks[1], (marks[1],), 1, EDGE_COST[1]
    )
    query_blocks = [swapped(messages) for messages in query_packs]
    edges = [next_row(edge, 1) for edge in edges]
    arrays = (query_rows, key_rows, value_rows, grad_rows)
    halves = []
    for chunk in range(CHUNKS):
        *query_grads, main, far = attend(
            texts, marks, arrays,
            key_blocks[chunk], query_blocks[chunk], edges[chunk], chunk, total_rows,
        )
        halves.append((query_grads, main, next_row(far, -1)))
    (first_queries, main, far), (second_queries, last_main, last_far) = halves
    queries = [first_queries[0]] + swapped(first_queries[1:])
    mixed = settle(main, far, extra=second_queries, after=queries[1:])
    pairs = settle(last_main, last_far)
    mixed = [mixed[0]] + swapped(mixed[1:])
    pairs = [pairs[0]] + swapped(pairs[1:])
    grad_queries, grad_keys, grad_values = gathered(queries, mixed, pairs)
    return grad_queries[None], grad_keys[None], grad_values[None]


def solution(mesh):
    in_specs = (
        P("dp", "ctx", None),
        P("dp", "ctx", None),
        P("dp", "ctx", None),
        P("dp", "ctx", None),
        P("dp", None),
        P("dp", None),
    )
    out_specs = (P("dp", "ctx", None), P("dp", "ctx", None), P("dp", "ctx", None))
    return jax.shard_map(shards, mesh=mesh, in_specs=in_specs, out_specs=out_specs, check_vma=False)
```

```python
import functools

import jax
import jax.numpy as jnp
from jax import lax
from jax.experimental import pallas as pl
from jax.experimental.pallas import tpu as pltpu
from jax.sharding import PartitionSpec as P

HEAD = 128
STEPS = 4
GROUP = 4
CHUNKS = 2
LOG2E = 1.4426950408889634
MASKED = -1e30
VMEM = pl.BlockSpec(memory_space=pltpu.VMEM)
ANY = pl.BlockSpec(memory_space=pl.ANY)
LARGE = pltpu.CompilerParams(vmem_limit_bytes=60 * 1024 * 1024)
EDGE_COST = (0, 6000000000)
SETTLE_COST = 3000000000
SMALL = pltpu.CompilerParams(vmem_limit_bytes=10 * 1024 * 1024)


def aways():
    core = lax.rem(lax.axis_index("dp"), 2)
    return 0, 1 + core, 3 - 2 * core, 2 + core


def columns(place, away, chunk, width):
    index = lax.rem(place + GROUP + away, GROUP)
    return pl.ds(pl.multiple_of((index * CHUNKS + chunk) * width, width), width)


def pack_kernel(chunk, first, second, after, one, two, three):
    width = one.shape[2]
    for away, message in zip(aways()[1:], (one, two, three)):
        lanes = columns(lax.rem(lax.axis_index("ctx"), GROUP), away, chunk, width)
        message[0] = first[:, lanes]
        message[1] = second[:, lanes]


def first_pack_kernel(first, second, lengths, flags, one, two, three, text, held, sems):
    width = one.shape[2]
    place = lax.rem(lax.axis_index("ctx"), GROUP)
    copies = []
    for away, message in zip(aways()[1:], (one, two, three)):
        lanes = columns(place, away, 0, width)
        for part, source in enumerate((first, second)):
            copies.append(
                pltpu.make_async_copy(source.at[:, lanes], message.at[part], sems.at[len(copies)])
            )
    for part, source in enumerate((lengths, flags)):
        copies.append(pltpu.make_async_copy(source, held.at[part], sems.at[len(copies)]))
    for copy in copies:
        copy.start()
    for copy in copies:
        copy.wait()
    text[...] = (held[0] * (1 - held[1])).astype(jnp.float32)


def pack(first, second, after, chunk):
    rows, total = first.shape
    width = total // (GROUP * CHUNKS)
    message = jax.ShapeDtypeStruct((2, rows, width), first.dtype)
    return pl.pallas_call(
        functools.partial(pack_kernel, chunk),
        out_shape=(message,) * (GROUP - 1),
        in_specs=[VMEM, VMEM, ANY],
        out_specs=(VMEM,) * (GROUP - 1),
        compiler_params=SMALL,
        cost_estimate=pl.CostEstimate(flops=0, bytes_accessed=12 * rows * width * 2, transcendentals=0),
        name="pack",
    )(first, second, after)


def first_pack(first, second, lengths, flags):
    rows, total = first.shape
    width = total // (GROUP * CHUNKS)
    message = jax.ShapeDtypeStruct((2, rows, width), first.dtype)
    *messages, text = pl.pallas_call(
        first_pack_kernel,
        out_shape=(message,) * (GROUP - 1) + (jax.ShapeDtypeStruct(lengths.shape, jnp.float32),),
        in_specs=[ANY, ANY, ANY, ANY],
        out_specs=(VMEM,) * GROUP,
        scratch_shapes=[
            pltpu.VMEM((2, *lengths.shape), lengths.dtype),
            pltpu.SemaphoreType.DMA((2 * GROUP,)),
        ],
        compiler_params=LARGE,
        cost_estimate=pl.CostEstimate(flops=0, bytes_accessed=12 * rows * width * 2, transcendentals=0),
        name="first_pack",
    )(first, second, lengths, flags)
    return messages, text


def edge_kernel(chunk, first, second, one, two, three, *refs):
    edge = refs[-1]
    rows = edge.shape[1] // (GROUP - 1)
    width = edge.shape[2]
    place = lax.rem(lax.axis_index("ctx"), GROUP)
    for away, message in zip(aways(), (None, one, two, three)):
        index = lax.rem(place + GROUP - away, GROUP)

        @pl.when(index > 0)
        def put():
            at = pl.ds(pl.multiple_of((index - 1) * rows, rows), rows)
            if message is None:
                lanes = columns(place, 0, chunk, width)
                edge[0, at, :] = first[:, lanes]
                edge[1, at, :] = second[:, lanes]
            else:
                edge[:, at, :] = message[...]


def make_edge(first, second, blocks, afters, chunk, cost):
    _, rows, width = blocks[0].shape
    return pl.pallas_call(
        functools.partial(edge_kernel, chunk),
        out_shape=jax.ShapeDtypeStruct((2, (GROUP - 1) * rows, width), first.dtype),
        in_specs=[VMEM] * 5 + [ANY] * len(afters),
        out_specs=VMEM,
        compiler_params=SMALL,
        cost_estimate=pl.CostEstimate(flops=cost, bytes_accessed=0, transcendentals=0),
        name="edge",
    )(first, second, *blocks, *afters)


def sides_kernel(stretch_rows, cycle_size, lengths_ref, flags_ref, after, limit_ref, text_ref, key_ref):
    rows = 2 * stretch_rows
    device_here = lax.axis_index("ctx")
    start = device_here - lax.rem(device_here, GROUP)
    segments = lengths_ref.shape[1]
    square = (segments, segments)
    diagonal = lax.broadcasted_iota(jnp.int32, square, 0) == lax.broadcasted_iota(
        jnp.int32, square, 1
    )

    def upright(ref):
        row = jnp.broadcast_to(ref[...].astype(jnp.float32), square)
        return jnp.sum(jnp.where(diagonal, row, 0.0), axis=1, keepdims=True)

    lengths, flags = upright(lengths_ref), upright(flags_ref)
    source = lax.broadcasted_iota(jnp.int32, (segments, HEAD), 0)
    target = lax.broadcasted_iota(jnp.int32, (segments, HEAD), 1)

    def gathered_sum(mask, column):
        return jnp.sum(jnp.where(mask, column, 0.0), axis=0, keepdims=True)

    last = gathered_sum(source <= target, lengths)
    first = gathered_sum(source < target, lengths).astype(jnp.int32)
    flag = gathered_sum(source == target, flags)
    ending = last.astype(jnp.int32)
    shape = (rows, HEAD)
    offset = lax.broadcasted_iota(jnp.int32, shape, 0)
    for block in range(GROUP):
        device = start + block
        position = jnp.where(
            offset < stretch_rows,
            device * stretch_rows + offset,
            (2 * cycle_size - 2 - device) * stretch_rows + offset,
        )
        inside = (position >= first) & (position < ending)
        image = jnp.sum(jnp.where(inside, flag, 0.0), axis=1, keepdims=True)
        final = jnp.sum(jnp.where(inside, last, 0.0), axis=1, keepdims=True).astype(jnp.int32) - 1
        limit_ref[block] = jnp.where(image > 0.5, final, position)
        text_ref[block] = jnp.broadcast_to(1.0 - image, shape)
        lane = lax.broadcasted_iota(jnp.int32, (8, STEPS * rows), 1)
        step = jnp.zeros_like(lane)
        for edge in range(1, STEPS):
            step = step + (lane >= edge * rows).astype(jnp.int32)
        owner = device - (STEPS - 1) + step
        owner = jnp.where(owner < 0, owner + cycle_size, owner)
        within = lane - step * rows
        key_ref[block] = jnp.where(
            within < stretch_rows,
            owner * stretch_rows + within,
            (2 * cycle_size - 2 - owner) * stretch_rows + within,
        )


def sides(lengths, flags, after, stretch_rows, cycle_size):
    rows = 2 * stretch_rows
    return pl.pallas_call(
        functools.partial(sides_kernel, stretch_rows, cycle_size),
        out_shape=(
            jax.ShapeDtypeStruct((GROUP, rows, HEAD), jnp.int32),
            jax.ShapeDtypeStruct((GROUP, rows, HEAD), jnp.float32),
            jax.ShapeDtypeStruct((GROUP, 8, STEPS * rows), jnp.int32),
        ),
        in_specs=[VMEM, VMEM, ANY],
        out_specs=(VMEM,) * 3,
        compiler_params=SMALL,
        cost_estimate=pl.CostEstimate(flops=GROUP * rows * HEAD * 8, bytes_accessed=GROUP * rows * HEAD * 8, transcendentals=0),
        name="sides",
    )(lengths, flags, after)


def attend_kernel(
    chunk, total_rows, text_one, text_two, text_three, text_four, limit_ref, text_ref, keypos_ref,
    queries, keys, values, grads, key_one, key_two, key_three, query_one, query_two, query_three,
    edge_ref, query_own, query_to_one, query_to_two, query_to_three, main_ref, far_ref,
    key_all, value_all, query_all, grad_all, key_grad, value_grad, query_out,
):
    rows, width = queries.shape[0], edge_ref.shape[2]
    edge = (GROUP - 1) * rows
    span = STEPS * rows
    scale = HEAD ** (-0.5)
    place = lax.rem(lax.axis_index("ctx"), GROUP)
    counted = text_one[...] + text_two[...] + text_three[...] + text_four[...]
    factor = total_rows / jnp.sum(counted, axis=1, keepdims=True)
    lanes = columns(place, 0, chunk, width)
    key_all[:edge, :] = edge_ref[0]
    value_all[:edge, :] = edge_ref[1]
    sources = [(keys.at[:, lanes], values.at[:, lanes], queries.at[:, lanes], grads.at[:, lanes])]
    for pair, query_pair in ((key_one, query_one), (key_two, query_two), (key_three, query_three)):
        sources.append((pair.at[0], pair.at[1], query_pair.at[0], query_pair.at[1]))
    for slot, away in enumerate(aways()):
        start = pl.multiple_of(lax.rem(place + GROUP - away, GROUP) * rows, rows)
        key, value, query, grad = sources[slot]
        key_all[pl.ds(edge + start, rows), :] = key[...]
        value_all[pl.ds(edge + start, rows), :] = value[...]
        query_all[pl.ds(start, rows), :] = query[...]
        grad_all[pl.ds(start, rows), :] = grad[...]
    key_grad[...] = jnp.zeros_like(key_grad)
    value_grad[...] = jnp.zeros_like(value_grad)
    for block in range(GROUP):
        at = slice(block * rows, (block + 1) * rows)
        window = slice(block * rows, block * rows + span)
        limit = limit_ref[block]
        allowed = jnp.concatenate(
            [
                keypos_ref[block, 0:1, tile * HEAD : (tile + 1) * HEAD] <= limit
                for tile in range(span // HEAD)
            ],
            axis=1,
        )
        weight = text_ref[block] * factor
        for head in range(width // HEAD):
            lanes = slice(head * HEAD, (head + 1) * HEAD)
            query = query_all[at, lanes]
            grad = (grad_all[at, lanes].astype(jnp.float32) * weight).astype(jnp.bfloat16)
            key = key_all[window, lanes]
            value = value_all[window, lanes]
            scores = lax.dot_general(
                query, key, (((1,), (1,)), ((), ())), preferred_element_type=jnp.float32
            )
            scores = jnp.where(allowed, scores, MASKED)
            largest = jnp.max(scores, axis=1, keepdims=True)
            prob = jnp.exp2((scores - largest) * (scale * LOG2E))
            dprob = lax.dot_general(
                grad, value, (((1,), (1,)), ((), ())), preferred_element_type=jnp.float32
            )
            total = jnp.sum(prob, axis=1, keepdims=True)
            inverse = 1.0 / total
            delta = jnp.sum(prob * dprob, axis=1, keepdims=True) * inverse
            prob = prob * inverse
            dscore = (prob * (dprob - delta)).astype(jnp.bfloat16)
            prob_half = prob.astype(jnp.bfloat16)
            query_out[at, lanes] = (
                jnp.dot(dscore, key, preferred_element_type=jnp.float32) * scale
            ).astype(jnp.bfloat16)
            key_grad[window, lanes] += lax.dot_general(
                dscore, query, (((0,), (0,)), ((), ())), preferred_element_type=jnp.float32
            )
            value_grad[window, lanes] += lax.dot_general(
                prob_half, grad, (((0,), (0,)), ((), ())), preferred_element_type=jnp.float32
            )
    for away, block in zip(aways(), (query_own, query_to_one, query_to_two, query_to_three)):
        index = lax.rem(place + away, GROUP)
        block[...] = query_out[pl.ds(pl.multiple_of(index * rows, rows), rows), :]
    far_ref[0] = (key_grad[:edge, :] * scale).astype(jnp.bfloat16)
    far_ref[1] = value_grad[:edge, :].astype(jnp.bfloat16)
    main_ref[0] = (key_grad[edge:, :] * scale).astype(jnp.bfloat16)
    main_ref[1] = value_grad[edge:, :].astype(jnp.bfloat16)


def attend(texts, marks, arrays, key_blocks, query_blocks, edge, chunk, total_rows):
    _, rows, width = key_blocks[0].shape
    heads = width // HEAD
    keys = (2 * GROUP - 1) * rows
    pairs = heads * GROUP * rows * STEPS * rows
    return pl.pallas_call(
        functools.partial(attend_kernel, chunk, total_rows),
        out_shape=(
            *[jax.ShapeDtypeStruct((rows, width), jnp.bfloat16)] * GROUP,
            jax.ShapeDtypeStruct((2, GROUP * rows, width), jnp.bfloat16),
            jax.ShapeDtypeStruct((2, (GROUP - 1) * rows, width), jnp.bfloat16),
        ),
        in_specs=[VMEM] * (len(texts) + 14),
        out_specs=(VMEM,) * (GROUP + 2),
        scratch_shapes=[
            pltpu.VMEM((keys, width), jnp.bfloat16),
            pltpu.VMEM((keys, width), jnp.bfloat16),
            pltpu.VMEM((GROUP * rows, width), jnp.bfloat16),
            pltpu.VMEM((GROUP * rows, width), jnp.bfloat16),
            pltpu.VMEM((keys, width), jnp.float32),
            pltpu.VMEM((keys, width), jnp.float32),
            pltpu.VMEM((GROUP * rows, width), jnp.bfloat16),
        ],
        compiler_params=pltpu.CompilerParams(vmem_limit_bytes=24 * 1024 * 1024),
        cost_estimate=pl.CostEstimate(
            flops=4500000000, bytes_accessed=0, transcendentals=0
        ),
        name="attend",
    )(*texts, *marks, *arrays, *key_blocks, *query_blocks, edge)


def settle_kernel(main_ref, far_ref, *refs):
    extra = refs[: len(refs) // GROUP * GROUP - GROUP]
    outs = refs[len(refs) - GROUP :]
    rows = outs[0].shape[1]
    first_kind = 1 if extra else 0
    place = lax.rem(lax.axis_index("ctx"), GROUP)
    for slot, (away, block) in enumerate(zip(aways(), outs)):
        index = lax.rem(place + away, GROUP)
        start = pl.multiple_of(index * rows, rows)
        if extra:
            block[0] = extra[slot][...]

        @pl.when(index == 0)
        def first():
            block[first_kind:] = main_ref[:, :rows, :]

        @pl.when(index > 0)
        def later():
            behind = pl.multiple_of(start - rows, rows)
            block[first_kind:] = (
                main_ref[:, pl.ds(start, rows), :].astype(jnp.float32)
                + far_ref[:, pl.ds(behind, rows), :].astype(jnp.float32)
            ).astype(jnp.bfloat16)


def settle(main, far, extra=(), after=()):
    _, total, width = main.shape
    rows = total // GROUP
    count = 2 + (1 if extra else 0)

    def kernel(main_ref, far_ref, *refs):
        refs = list(refs)
        settle_kernel(main_ref, far_ref, *refs[: len(extra)], *refs[-GROUP:])

    return pl.pallas_call(
        kernel,
        out_shape=(jax.ShapeDtypeStruct((count, rows, width), jnp.bfloat16),) * GROUP,
        in_specs=[VMEM, VMEM] + [VMEM] * len(extra) + [ANY] * len(after),
        out_specs=(VMEM,) * GROUP,
        compiler_params=SMALL,
        cost_estimate=pl.CostEstimate(
            flops=SETTLE_COST if extra else 0, bytes_accessed=main.size * 8, transcendentals=0
        ),
        name="settle",
    )(main, far, *extra, *after)


def place_copies(moves, sems):
    copies = []
    for source, target, chunk, slot in moves:
        lanes = columns(lax.rem(lax.axis_index("ctx"), GROUP), -aways()[slot], chunk, source.shape[1])
        copies.append(pltpu.make_async_copy(source, target.at[:, lanes], sems.at[len(copies)]))
    for copy in copies:
        copy.start()
    for copy in copies:
        copy.wait()


def early_kernel(*refs):
    queries, mixed = refs[:GROUP], refs[GROUP : 2 * GROUP]
    query_ref, key_ref, value_ref, sems = refs[2 * GROUP :]
    moves = []
    for away in range(GROUP):
        moves += [
            (queries[away], query_ref, 0, away),
            (mixed[away].at[0], query_ref, 1, away),
            (mixed[away].at[1], key_ref, 0, away),
            (mixed[away].at[2], value_ref, 0, away),
        ]
    place_copies(moves, sems)


def late_kernel(*refs):
    pairs = refs[:GROUP]
    key_ref, value_ref, sems = refs[GROUP + 2 :]
    moves = []
    for away in range(GROUP):
        moves += [
            (pairs[away].at[0], key_ref, 1, away),
            (pairs[away].at[1], value_ref, 1, away),
        ]
    place_copies(moves, sems)


def gathered(queries, mixed, pairs):
    rows, width = queries[0].shape
    out = jax.ShapeDtypeStruct((rows, width * CHUNKS * GROUP), jnp.bfloat16)
    grad_queries, grad_keys, grad_values = pl.pallas_call(
        early_kernel,
        out_shape=(out, out, out),
        in_specs=[VMEM] * (2 * GROUP),
        out_specs=(ANY,) * 3,
        scratch_shapes=[pltpu.SemaphoreType.DMA((4 * GROUP,))],
        compiler_params=SMALL,
        cost_estimate=pl.CostEstimate(flops=0, bytes_accessed=out.size * 6, transcendentals=0),
        name="early",
    )(*queries, *mixed)
    grad_keys, grad_values = pl.pallas_call(
        late_kernel,
        out_shape=(out, out),
        in_specs=[VMEM] * GROUP + [ANY, ANY],
        out_specs=(ANY, ANY),
        input_output_aliases={GROUP: 0, GROUP + 1: 1},
        scratch_shapes=[pltpu.SemaphoreType.DMA((2 * GROUP,))],
        compiler_params=SMALL,
        cost_estimate=pl.CostEstimate(flops=0, bytes_accessed=out.size * 6, transcendentals=0),
        name="late",
    )(*pairs, grad_keys, grad_values)
    return grad_queries, grad_keys, grad_values


def shards(queries, keys, values, grad_out, lengths, image_flags):
    query_rows, key_rows, value_rows, grad_rows = queries[0], keys[0], values[0], grad_out[0]
    row_count = query_rows.shape[0]
    cycle_size = lax.axis_size("ctx")
    samples = lax.axis_size("dp")

    def swap(value, slot):
        pairs = []
        for sample in range(samples):
            core = sample % 2
            away = (1 + core, 3 - 2 * core, 2 + core)[slot]
            for source in range(cycle_size):
                target = source - source % GROUP + (source + away) % GROUP
                pairs.append((sample * cycle_size + source, sample * cycle_size + target))
        return lax.ppermute(value, ("dp", "ctx"), pairs)

    def next_row(value, rows):
        pairs = [(source, (source + rows * GROUP) % cycle_size) for source in range(cycle_size)]
        return lax.ppermute(value, "ctx", pairs)

    def swapped(messages):
        return [swap(message, slot) for slot, message in enumerate(messages)]

    first_messages, text = first_pack(key_rows, value_rows, lengths, image_flags)
    texts = [text] + [
        lax.ppermute(text, "dp", [(source, (source + away) % samples) for source in range(samples)])
        for away in range(1, samples)
    ]
    total_rows = float(row_count * cycle_size * samples)

    key_packs, query_packs, edges = [None] * CHUNKS, [None] * CHUNKS, [None] * CHUNKS
    key_packs[0] = first_messages
    key_packs[1] = pack(key_rows, value_rows, text, 1)
    key_blocks = [swapped(messages) for messages in key_packs]
    edges[0] = make_edge(
        key_rows, value_rows, key_blocks[0], (*texts[1:], key_packs[1][0]), 0, EDGE_COST[0]
    )
    after = edges[0]
    for index in range(CHUNKS):
        query_packs[index] = pack(query_rows, grad_rows, after, index)
        after = query_packs[index][0]
    marks = sides(lengths, image_flags, after, row_count // 2, cycle_size)
    edges[1] = make_edge(
        key_rows, value_rows, key_blocks[1], (marks[1],), 1, EDGE_COST[1]
    )
    query_blocks = [swapped(messages) for messages in query_packs]
    edges = [next_row(edge, 1) for edge in edges]
    arrays = (query_rows, key_rows, value_rows, grad_rows)
    halves = []
    for chunk in range(CHUNKS):
        *query_grads, main, far = attend(
            texts, marks, arrays,
            key_blocks[chunk], query_blocks[chunk], edges[chunk], chunk, total_rows,
        )
        halves.append((query_grads, main, next_row(far, -1)))
    (first_queries, main, far), (second_queries, last_main, last_far) = halves
    queries = [first_queries[0]] + swapped(first_queries[1:])
    mixed = settle(main, far, extra=second_queries, after=queries[1:])
    pairs = settle(last_main, last_far)
    mixed = [mixed[0]] + swapped(mixed[1:])
    pairs = [pairs[0]] + swapped(pairs[1:])
    grad_queries, grad_keys, grad_values = gathered(queries, mixed, pairs)
    return grad_queries[None], grad_keys[None], grad_values[None]


def solution(mesh):
    in_specs = (
        P("dp", "ctx", None),
        P("dp", "ctx", None),
        P("dp", "ctx", None),
        P("dp", "ctx", None),
        P("dp", None),
        P("dp", None),
    )
    out_specs = (P("dp", "ctx", None), P("dp", "ctx", None), P("dp", "ctx", None))
    return jax.shard_map(shards, mesh=mesh, in_specs=in_specs, out_specs=out_specs, check_vma=False)
```

```python
import functools

import jax
import jax.numpy as jnp
from jax import lax
from jax.experimental import pallas as pl
from jax.experimental.pallas import tpu as pltpu
from jax.sharding import PartitionSpec as P

HEAD = 128
STEPS = 4
GROUP = 4
CHUNKS = 2
LOG2E = 1.4426950408889634
MASKED = -1e30
VMEM = pl.BlockSpec(memory_space=pltpu.VMEM)
ANY = pl.BlockSpec(memory_space=pl.ANY)
LARGE = pltpu.CompilerParams(vmem_limit_bytes=60 * 1024 * 1024)
EDGE_COST = (0, 6000000000)
SETTLE_COST = 3000000000
SMALL = pltpu.CompilerParams(vmem_limit_bytes=10 * 1024 * 1024)


def aways():
    core = lax.rem(lax.axis_index("dp"), 2)
    return 0, 1 + 2 * core, 3 - 2 * core, 2


def columns(place, away, chunk, width):
    index = lax.rem(place + GROUP + away, GROUP)
    return pl.ds(pl.multiple_of((index * CHUNKS + chunk) * width, width), width)


def pack_kernel(chunk, first, second, after, one, two, three):
    width = one.shape[2]
    for away, message in zip(aways()[1:], (one, two, three)):
        lanes = columns(lax.rem(lax.axis_index("ctx"), GROUP), away, chunk, width)
        message[0] = first[:, lanes]
        message[1] = second[:, lanes]


def first_pack_kernel(first, second, lengths, flags, one, two, three, text, held, sems):
    width = one.shape[2]
    place = lax.rem(lax.axis_index("ctx"), GROUP)
    copies = []
    for away, message in zip(aways()[1:], (one, two, three)):
        lanes = columns(place, away, 0, width)
        for part, source in enumerate((first, second)):
            copies.append(
                pltpu.make_async_copy(source.at[:, lanes], message.at[part], sems.at[len(copies)])
            )
    for part, source in enumerate((lengths, flags)):
        copies.append(pltpu.make_async_copy(source, held.at[part], sems.at[len(copies)]))
    for copy in copies:
        copy.start()
    for copy in copies:
        copy.wait()
    text[...] = (held[0] * (1 - held[1])).astype(jnp.float32)


def pack(first, second, after, chunk):
    rows, total = first.shape
    width = total // (GROUP * CHUNKS)
    message = jax.ShapeDtypeStruct((2, rows, width), first.dtype)
    return pl.pallas_call(
        functools.partial(pack_kernel, chunk),
        out_shape=(message,) * (GROUP - 1),
        in_specs=[VMEM, VMEM, ANY],
        out_specs=(VMEM,) * (GROUP - 1),
        compiler_params=SMALL,
        cost_estimate=pl.CostEstimate(flops=0, bytes_accessed=12 * rows * width * 2, transcendentals=0),
        name="pack",
    )(first, second, after)


def first_pack(first, second, lengths, flags):
    rows, total = first.shape
    width = total // (GROUP * CHUNKS)
    message = jax.ShapeDtypeStruct((2, rows, width), first.dtype)
    *messages, text = pl.pallas_call(
        first_pack_kernel,
        out_shape=(message,) * (GROUP - 1) + (jax.ShapeDtypeStruct(lengths.shape, jnp.float32),),
        in_specs=[ANY, ANY, ANY, ANY],
        out_specs=(VMEM,) * GROUP,
        scratch_shapes=[
            pltpu.VMEM((2, *lengths.shape), lengths.dtype),
            pltpu.SemaphoreType.DMA((2 * GROUP,)),
        ],
        compiler_params=LARGE,
        cost_estimate=pl.CostEstimate(flops=0, bytes_accessed=12 * rows * width * 2, transcendentals=0),
        name="first_pack",
    )(first, second, lengths, flags)
    return messages, text


def edge_kernel(chunk, first, second, one, two, three, *refs):
    edge = refs[-1]
    rows = edge.shape[1] // (GROUP - 1)
    width = edge.shape[2]
    place = lax.rem(lax.axis_index("ctx"), GROUP)
    for away, message in zip(aways(), (None, one, two, three)):
        index = lax.rem(place + GROUP - away, GROUP)

        @pl.when(index > 0)
        def put():
            at = pl.ds(pl.multiple_of((index - 1) * rows, rows), rows)
            if message is None:
                lanes = columns(place, 0, chunk, width)
                edge[0, at, :] = first[:, lanes]
                edge[1, at, :] = second[:, lanes]
            else:
                edge[:, at, :] = message[...]


def make_edge(first, second, blocks, afters, chunk, cost):
    _, rows, width = blocks[0].shape
    return pl.pallas_call(
        functools.partial(edge_kernel, chunk),
        out_shape=jax.ShapeDtypeStruct((2, (GROUP - 1) * rows, width), first.dtype),
        in_specs=[VMEM] * 5 + [ANY] * len(afters),
        out_specs=VMEM,
        compiler_params=SMALL,
        cost_estimate=pl.CostEstimate(flops=cost, bytes_accessed=0, transcendentals=0),
        name="edge",
    )(first, second, *blocks, *afters)


def sides_kernel(stretch_rows, cycle_size, lengths_ref, flags_ref, after, limit_ref, text_ref, key_ref):
    rows = 2 * stretch_rows
    device_here = lax.axis_index("ctx")
    start = device_here - lax.rem(device_here, GROUP)
    segments = lengths_ref.shape[1]
    square = (segments, segments)
    diagonal = lax.broadcasted_iota(jnp.int32, square, 0) == lax.broadcasted_iota(
        jnp.int32, square, 1
    )

    def upright(ref):
        row = jnp.broadcast_to(ref[...].astype(jnp.float32), square)
        return jnp.sum(jnp.where(diagonal, row, 0.0), axis=1, keepdims=True)

    lengths, flags = upright(lengths_ref), upright(flags_ref)
    source = lax.broadcasted_iota(jnp.int32, (segments, HEAD), 0)
    target = lax.broadcasted_iota(jnp.int32, (segments, HEAD), 1)

    def gathered_sum(mask, column):
        return jnp.sum(jnp.where(mask, column, 0.0), axis=0, keepdims=True)

    last = gathered_sum(source <= target, lengths)
    first = gathered_sum(source < target, lengths).astype(jnp.int32)
    flag = gathered_sum(source == target, flags)
    ending = last.astype(jnp.int32)
    shape = (rows, HEAD)
    offset = lax.broadcasted_iota(jnp.int32, shape, 0)
    for block in range(GROUP):
        device = start + block
        position = jnp.where(
            offset < stretch_rows,
            device * stretch_rows + offset,
            (2 * cycle_size - 2 - device) * stretch_rows + offset,
        )
        inside = (position >= first) & (position < ending)
        image = jnp.sum(jnp.where(inside, flag, 0.0), axis=1, keepdims=True)
        final = jnp.sum(jnp.where(inside, last, 0.0), axis=1, keepdims=True).astype(jnp.int32) - 1
        limit_ref[block] = jnp.where(image > 0.5, final, position)
        text_ref[block] = jnp.broadcast_to(1.0 - image, shape)
        lane = lax.broadcasted_iota(jnp.int32, (8, STEPS * rows), 1)
        step = jnp.zeros_like(lane)
        for edge in range(1, STEPS):
            step = step + (lane >= edge * rows).astype(jnp.int32)
        owner = device - (STEPS - 1) + step
        owner = jnp.where(owner < 0, owner + cycle_size, owner)
        within = lane - step * rows
        key_ref[block] = jnp.where(
            within < stretch_rows,
            owner * stretch_rows + within,
            (2 * cycle_size - 2 - owner) * stretch_rows + within,
        )


def sides(lengths, flags, after, stretch_rows, cycle_size):
    rows = 2 * stretch_rows
    return pl.pallas_call(
        functools.partial(sides_kernel, stretch_rows, cycle_size),
        out_shape=(
            jax.ShapeDtypeStruct((GROUP, rows, HEAD), jnp.int32),
            jax.ShapeDtypeStruct((GROUP, rows, HEAD), jnp.float32),
            jax.ShapeDtypeStruct((GROUP, 8, STEPS * rows), jnp.int32),
        ),
        in_specs=[VMEM, VMEM, ANY],
        out_specs=(VMEM,) * 3,
        compiler_params=SMALL,
        cost_estimate=pl.CostEstimate(flops=GROUP * rows * HEAD * 8, bytes_accessed=GROUP * rows * HEAD * 8, transcendentals=0),
        name="sides",
    )(lengths, flags, after)


def attend_kernel(
    chunk, total_rows, text_one, text_two, text_three, text_four, limit_ref, text_ref, keypos_ref,
    queries, keys, values, grads, key_one, key_two, key_three, query_one, query_two, query_three,
    edge_ref, query_own, query_to_one, query_to_two, query_to_three, main_ref, far_ref,
    key_all, value_all, query_all, grad_all, key_grad, value_grad, query_out,
):
    rows, width = queries.shape[0], edge_ref.shape[2]
    edge = (GROUP - 1) * rows
    span = STEPS * rows
    scale = HEAD ** (-0.5)
    place = lax.rem(lax.axis_index("ctx"), GROUP)
    counted = text_one[...] + text_two[...] + text_three[...] + text_four[...]
    factor = total_rows / jnp.sum(counted, axis=1, keepdims=True)
    lanes = columns(place, 0, chunk, width)
    key_all[:edge, :] = edge_ref[0]
    value_all[:edge, :] = edge_ref[1]
    sources = [(keys.at[:, lanes], values.at[:, lanes], queries.at[:, lanes], grads.at[:, lanes])]
    for pair, query_pair in ((key_one, query_one), (key_two, query_two), (key_three, query_three)):
        sources.append((pair.at[0], pair.at[1], query_pair.at[0], query_pair.at[1]))
    for slot, away in enumerate(aways()):
        start = pl.multiple_of(lax.rem(place + GROUP - away, GROUP) * rows, rows)
        key, value, query, grad = sources[slot]
        key_all[pl.ds(edge + start, rows), :] = key[...]
        value_all[pl.ds(edge + start, rows), :] = value[...]
        query_all[pl.ds(start, rows), :] = query[...]
        grad_all[pl.ds(start, rows), :] = grad[...]
    for block in range(GROUP):
        at = slice(block * rows, (block + 1) * rows)
        window = slice(block * rows, block * rows + span)
        limit = limit_ref[block]
        allowed = jnp.concatenate(
            [
                keypos_ref[block, 0:1, tile * HEAD : (tile + 1) * HEAD] <= limit
                for tile in range(span // HEAD)
            ],
            axis=1,
        )
        weight = text_ref[block] * factor
        for head in range(width // HEAD):
            lanes = slice(head * HEAD, (head + 1) * HEAD)
            query = query_all[at, lanes]
            grad = (grad_all[at, lanes].astype(jnp.float32) * weight).astype(jnp.bfloat16)
            key = key_all[window, lanes]
            value = value_all[window, lanes]
            scores = lax.dot_general(
                query, key, (((1,), (1,)), ((), ())), preferred_element_type=jnp.float32
            )
            scores = jnp.where(allowed, scores, MASKED)
            largest = jnp.max(scores, axis=1, keepdims=True)
            prob = jnp.exp2((scores - largest) * (scale * LOG2E))
            dprob = lax.dot_general(
                grad, value, (((1,), (1,)), ((), ())), preferred_element_type=jnp.float32
            )
            total = jnp.sum(prob, axis=1, keepdims=True)
            inverse = 1.0 / total
            delta = jnp.sum(prob * dprob, axis=1, keepdims=True) * inverse
            prob = prob * inverse
            dscore = (prob * (dprob - delta)).astype(jnp.bfloat16)
            prob_half = prob.astype(jnp.bfloat16)
            query_out[at, lanes] = (
                jnp.dot(dscore, key, preferred_element_type=jnp.float32) * scale
            ).astype(jnp.bfloat16)
            for kind, (left, right, held, scaling) in enumerate(
                ((dscore, query, key_grad, scale), (prob_half, grad, value_grad, 1.0))
            ):
                term = lax.dot_general(
                    left, right, (((0,), (0,)), ((), ())), preferred_element_type=jnp.float32
                )
                for step in range(STEPS):
                    index = block + step
                    here = slice(index * rows, (index + 1) * rows)
                    part = term[step * rows : (step + 1) * rows]
                    if block > 0 and step < STEPS - 1:
                        part = part + held[here, lanes]
                    if step > 0 and block < GROUP - 1:
                        held[here, lanes] = part
                    elif index < GROUP - 1:
                        far_ref[kind, here, lanes] = (part * scaling).astype(jnp.bfloat16)
                    else:
                        there = slice((index - GROUP + 1) * rows, (index - GROUP + 2) * rows)
                        main_ref[kind, there, lanes] = (part * scaling).astype(jnp.bfloat16)
    for away, block in zip(aways(), (query_own, query_to_one, query_to_two, query_to_three)):
        index = lax.rem(place + away, GROUP)
        block[...] = query_out[pl.ds(pl.multiple_of(index * rows, rows), rows), :]


def attend(texts, marks, arrays, key_blocks, query_blocks, edge, chunk, total_rows):
    _, rows, width = key_blocks[0].shape
    heads = width // HEAD
    keys = (2 * GROUP - 1) * rows
    pairs = heads * GROUP * rows * STEPS * rows
    return pl.pallas_call(
        functools.partial(attend_kernel, chunk, total_rows),
        out_shape=(
            *[jax.ShapeDtypeStruct((rows, width), jnp.bfloat16)] * GROUP,
            jax.ShapeDtypeStruct((2, GROUP * rows, width), jnp.bfloat16),
            jax.ShapeDtypeStruct((2, (GROUP - 1) * rows, width), jnp.bfloat16),
        ),
        in_specs=[VMEM] * (len(texts) + 14),
        out_specs=(VMEM,) * (GROUP + 2),
        scratch_shapes=[
            pltpu.VMEM((keys, width), jnp.bfloat16),
            pltpu.VMEM((keys, width), jnp.bfloat16),
            pltpu.VMEM((GROUP * rows, width), jnp.bfloat16),
            pltpu.VMEM((GROUP * rows, width), jnp.bfloat16),
            pltpu.VMEM((keys, width), jnp.float32),
            pltpu.VMEM((keys, width), jnp.float32),
            pltpu.VMEM((GROUP * rows, width), jnp.bfloat16),
        ],
        compiler_params=pltpu.CompilerParams(vmem_limit_bytes=24 * 1024 * 1024),
        cost_estimate=pl.CostEstimate(
            flops=4500000000, bytes_accessed=0, transcendentals=0
        ),
        name="attend",
    )(*texts, *marks, *arrays, *key_blocks, *query_blocks, edge)


def settle_kernel(main_ref, far_ref, *refs):
    extra = refs[: len(refs) // GROUP * GROUP - GROUP]
    outs = refs[len(refs) - GROUP :]
    rows = outs[0].shape[1]
    first_kind = 1 if extra else 0
    place = lax.rem(lax.axis_index("ctx"), GROUP)
    for slot, (away, block) in enumerate(zip(aways(), outs)):
        index = lax.rem(place + away, GROUP)
        start = pl.multiple_of(index * rows, rows)
        if extra:
            block[0] = extra[slot][...]

        @pl.when(index == 0)
        def first():
            block[first_kind:] = main_ref[:, :rows, :]

        @pl.when(index > 0)
        def later():
            behind = pl.multiple_of(start - rows, rows)
            block[first_kind:] = (
                main_ref[:, pl.ds(start, rows), :].astype(jnp.float32)
                + far_ref[:, pl.ds(behind, rows), :].astype(jnp.float32)
            ).astype(jnp.bfloat16)


def settle(main, far, extra=(), after=()):
    _, total, width = main.shape
    rows = total // GROUP
    count = 2 + (1 if extra else 0)

    def kernel(main_ref, far_ref, *refs):
        refs = list(refs)
        settle_kernel(main_ref, far_ref, *refs[: len(extra)], *refs[-GROUP:])

    return pl.pallas_call(
        kernel,
        out_shape=(jax.ShapeDtypeStruct((count, rows, width), jnp.bfloat16),) * GROUP,
        in_specs=[VMEM, VMEM] + [VMEM] * len(extra) + [ANY] * len(after),
        out_specs=(VMEM,) * GROUP,
        compiler_params=SMALL,
        cost_estimate=pl.CostEstimate(
            flops=SETTLE_COST if extra else 0, bytes_accessed=main.size * 8, transcendentals=0
        ),
        name="settle",
    )(main, far, *extra, *after)


def place_copies(moves, sems):
    copies = []
    for source, target, chunk, slot in moves:
        lanes = columns(lax.rem(lax.axis_index("ctx"), GROUP), -aways()[slot], chunk, source.shape[1])
        copies.append(pltpu.make_async_copy(source, target.at[:, lanes], sems.at[len(copies)]))
    for copy in copies:
        copy.start()
    for copy in copies:
        copy.wait()


def early_kernel(*refs):
    queries, mixed = refs[:GROUP], refs[GROUP : 2 * GROUP]
    query_ref, key_ref, value_ref, sems = refs[2 * GROUP :]
    moves = []
    for away in range(GROUP):
        moves += [
            (queries[away], query_ref, 0, away),
            (mixed[away].at[0], query_ref, 1, away),
            (mixed[away].at[1], key_ref, 0, away),
            (mixed[away].at[2], value_ref, 0, away),
        ]
    place_copies(moves, sems)


def late_kernel(*refs):
    pairs = refs[:GROUP]
    key_ref, value_ref, sems = refs[GROUP + 2 :]
    moves = []
    for away in range(GROUP):
        moves += [
            (pairs[away].at[0], key_ref, 1, away),
            (pairs[away].at[1], value_ref, 1, away),
        ]
    place_copies(moves, sems)


def gathered(queries, mixed, pairs):
    rows, width = queries[0].shape
    out = jax.ShapeDtypeStruct((rows, width * CHUNKS * GROUP), jnp.bfloat16)
    grad_queries, grad_keys, grad_values = pl.pallas_call(
        early_kernel,
        out_shape=(out, out, out),
        in_specs=[VMEM] * (2 * GROUP),
        out_specs=(ANY,) * 3,
        scratch_shapes=[pltpu.SemaphoreType.DMA((4 * GROUP,))],
        compiler_params=SMALL,
        cost_estimate=pl.CostEstimate(flops=0, bytes_accessed=out.size * 6, transcendentals=0),
        name="early",
    )(*queries, *mixed)
    grad_keys, grad_values = pl.pallas_call(
        late_kernel,
        out_shape=(out, out),
        in_specs=[VMEM] * GROUP + [ANY, ANY],
        out_specs=(ANY, ANY),
        input_output_aliases={GROUP: 0, GROUP + 1: 1},
        scratch_shapes=[pltpu.SemaphoreType.DMA((2 * GROUP,))],
        compiler_params=SMALL,
        cost_estimate=pl.CostEstimate(flops=0, bytes_accessed=out.size * 6, transcendentals=0),
        name="late",
    )(*pairs, grad_keys, grad_values)
    return grad_queries, grad_keys, grad_values


def shards(queries, keys, values, grad_out, lengths, image_flags):
    query_rows, key_rows, value_rows, grad_rows = queries[0], keys[0], values[0], grad_out[0]
    row_count = query_rows.shape[0]
    cycle_size = lax.axis_size("ctx")
    samples = lax.axis_size("dp")

    def swap(value, slot):
        pairs = []
        for sample in range(samples):
            core = sample % 2
            away = (1 + 2 * core, 3 - 2 * core, 2)[slot]
            for source in range(cycle_size):
                target = source - source % GROUP + (source + away) % GROUP
                pairs.append((sample * cycle_size + source, sample * cycle_size + target))
        return lax.ppermute(value, ("dp", "ctx"), pairs)

    def next_row(value, rows):
        pairs = [(source, (source + rows * GROUP) % cycle_size) for source in range(cycle_size)]
        return lax.ppermute(value, "ctx", pairs)

    def swapped(messages):
        return [swap(message, slot) for slot, message in enumerate(messages)]

    first_messages, text = first_pack(key_rows, value_rows, lengths, image_flags)
    texts = [text] + [
        lax.ppermute(text, "dp", [(source, (source + away) % samples) for source in range(samples)])
        for away in range(1, samples)
    ]
    total_rows = float(row_count * cycle_size * samples)

    key_packs, query_packs, edges = [None] * CHUNKS, [None] * CHUNKS, [None] * CHUNKS
    key_packs[0] = first_messages
    key_packs[1] = pack(key_rows, value_rows, text, 1)
    key_blocks = [swapped(messages) for messages in key_packs]
    edges[0] = make_edge(
        key_rows, value_rows, key_blocks[0], (*texts[1:], key_packs[1][0]), 0, EDGE_COST[0]
    )
    after = edges[0]
    for index in range(CHUNKS):
        query_packs[index] = pack(query_rows, grad_rows, after, index)
        after = query_packs[index][0]
    marks = sides(lengths, image_flags, after, row_count // 2, cycle_size)
    edges[1] = make_edge(
        key_rows, value_rows, key_blocks[1], (marks[1],), 1, EDGE_COST[1]
    )
    query_blocks = [swapped(messages) for messages in query_packs]
    edges = [next_row(edge, 1) for edge in edges]
    arrays = (query_rows, key_rows, value_rows, grad_rows)
    halves = []
    for chunk in range(CHUNKS):
        *query_grads, main, far = attend(
            texts, marks, arrays,
            key_blocks[chunk], query_blocks[chunk], edges[chunk], chunk, total_rows,
        )
        halves.append((query_grads, main, next_row(far, -1)))
    (first_queries, main, far), (second_queries, last_main, last_far) = halves
    queries = [first_queries[0]] + swapped(first_queries[1:])
    mixed = settle(main, far, extra=second_queries, after=queries[1:])
    pairs = settle(last_main, last_far)
    mixed = [mixed[0]] + swapped(mixed[1:])
    pairs = [pairs[0]] + swapped(pairs[1:])
    grad_queries, grad_keys, grad_values = gathered(queries, mixed, pairs)
    return grad_queries[None], grad_keys[None], grad_values[None]


def solution(mesh):
    in_specs = (
        P("dp", "ctx", None),
        P("dp", "ctx", None),
        P("dp", "ctx", None),
        P("dp", "ctx", None),
        P("dp", None),
        P("dp", None),
    )
    out_specs = (P("dp", "ctx", None), P("dp", "ctx", None), P("dp", "ctx", None))
    return jax.shard_map(shards, mesh=mesh, in_specs=in_specs, out_specs=out_specs, check_vma=False)
```

```python
import functools

import jax
import jax.numpy as jnp
from jax import lax
from jax.experimental import pallas as pl
from jax.experimental.pallas import tpu as pltpu
from jax.sharding import PartitionSpec as P

HEAD = 128
STEPS = 4
GROUP = 4
CHUNKS = 2
LOG2E = 1.4426950408889634
MASKED = -1e30
VMEM = pl.BlockSpec(memory_space=pltpu.VMEM)
ANY = pl.BlockSpec(memory_space=pl.ANY)
LARGE = pltpu.CompilerParams(vmem_limit_bytes=60 * 1024 * 1024)
EDGE_COST = (0, 6000000000)
SETTLE_COST = 3000000000
SMALL = pltpu.CompilerParams(vmem_limit_bytes=10 * 1024 * 1024)


def aways():
    core = lax.rem(lax.axis_index("dp"), 2)
    return 0, 1 + 2 * core, 3 - 2 * core, 2


def columns(place, away, chunk, width):
    index = lax.rem(place + GROUP + away, GROUP)
    return pl.ds(pl.multiple_of((index * CHUNKS + chunk) * width, width), width)


def pack_kernel(chunk, first, second, after, one, two, three):
    width = one.shape[2]
    for away, message in zip(aways()[1:], (one, two, three)):
        lanes = columns(lax.rem(lax.axis_index("ctx"), GROUP), away, chunk, width)
        message[0] = first[:, lanes]
        message[1] = second[:, lanes]


def first_pack_kernel(first, second, lengths, flags, one, two, three, text, held, sems):
    width = one.shape[2]
    place = lax.rem(lax.axis_index("ctx"), GROUP)
    copies = []
    for away, message in zip(aways()[1:], (one, two, three)):
        lanes = columns(place, away, 0, width)
        for part, source in enumerate((first, second)):
            copies.append(
                pltpu.make_async_copy(source.at[:, lanes], message.at[part], sems.at[len(copies)])
            )
    for part, source in enumerate((lengths, flags)):
        copies.append(pltpu.make_async_copy(source, held.at[part], sems.at[len(copies)]))
    for copy in copies:
        copy.start()
    for copy in copies:
        copy.wait()
    text[...] = (held[0] * (1 - held[1])).astype(jnp.float32)


def pack(first, second, after, chunk):
    rows, total = first.shape
    width = total // (GROUP * CHUNKS)
    message = jax.ShapeDtypeStruct((2, rows, width), first.dtype)
    return pl.pallas_call(
        functools.partial(pack_kernel, chunk),
        out_shape=(message,) * (GROUP - 1),
        in_specs=[VMEM, VMEM, ANY],
        out_specs=(VMEM,) * (GROUP - 1),
        compiler_params=SMALL,
        cost_estimate=pl.CostEstimate(flops=0, bytes_accessed=12 * rows * width * 2, transcendentals=0),
        name="pack",
    )(first, second, after)


def first_pack(first, second, lengths, flags):
    rows, total = first.shape
    width = total // (GROUP * CHUNKS)
    message = jax.ShapeDtypeStruct((2, rows, width), first.dtype)
    *messages, text = pl.pallas_call(
        first_pack_kernel,
        out_shape=(message,) * (GROUP - 1) + (jax.ShapeDtypeStruct(lengths.shape, jnp.float32),),
        in_specs=[ANY, ANY, ANY, ANY],
        out_specs=(VMEM,) * GROUP,
        scratch_shapes=[
            pltpu.VMEM((2, *lengths.shape), lengths.dtype),
            pltpu.SemaphoreType.DMA((2 * GROUP,)),
        ],
        compiler_params=LARGE,
        cost_estimate=pl.CostEstimate(flops=0, bytes_accessed=12 * rows * width * 2, transcendentals=0),
        name="first_pack",
    )(first, second, lengths, flags)
    return messages, text


def edge_kernel(chunk, first, second, one, two, three, *refs):
    edge = refs[-1]
    rows = edge.shape[1] // (GROUP - 1)
    width = edge.shape[2]
    place = lax.rem(lax.axis_index("ctx"), GROUP)
    for away, message in zip(aways(), (None, one, two, three)):
        index = lax.rem(place + GROUP - away, GROUP)

        @pl.when(index > 0)
        def put():
            at = pl.ds(pl.multiple_of((index - 1) * rows, rows), rows)
            if message is None:
                lanes = columns(place, 0, chunk, width)
                edge[0, at, :] = first[:, lanes]
                edge[1, at, :] = second[:, lanes]
            else:
                edge[:, at, :] = message[...]


def make_edge(first, second, blocks, afters, chunk, cost):
    _, rows, width = blocks[0].shape
    return pl.pallas_call(
        functools.partial(edge_kernel, chunk),
        out_shape=jax.ShapeDtypeStruct((2, (GROUP - 1) * rows, width), first.dtype),
        in_specs=[VMEM] * 5 + [ANY] * len(afters),
        out_specs=VMEM,
        compiler_params=SMALL,
        cost_estimate=pl.CostEstimate(flops=cost, bytes_accessed=0, transcendentals=0),
        name="edge",
    )(first, second, *blocks, *afters)


def sides_kernel(stretch_rows, cycle_size, lengths_ref, flags_ref, after, limit_ref, text_ref, key_ref):
    rows = 2 * stretch_rows
    device_here = lax.axis_index("ctx")
    start = device_here - lax.rem(device_here, GROUP)
    segments = lengths_ref.shape[1]
    square = (segments, segments)
    diagonal = lax.broadcasted_iota(jnp.int32, square, 0) == lax.broadcasted_iota(
        jnp.int32, square, 1
    )

    def upright(ref):
        row = jnp.broadcast_to(ref[...].astype(jnp.float32), square)
        return jnp.sum(jnp.where(diagonal, row, 0.0), axis=1, keepdims=True)

    lengths, flags = upright(lengths_ref), upright(flags_ref)
    source = lax.broadcasted_iota(jnp.int32, (segments, HEAD), 0)
    target = lax.broadcasted_iota(jnp.int32, (segments, HEAD), 1)

    def gathered_sum(mask, column):
        return jnp.sum(jnp.where(mask, column, 0.0), axis=0, keepdims=True)

    last = gathered_sum(source <= target, lengths)
    first = gathered_sum(source < target, lengths).astype(jnp.int32)
    flag = gathered_sum(source == target, flags)
    ending = last.astype(jnp.int32)
    shape = (rows, HEAD)
    offset = lax.broadcasted_iota(jnp.int32, shape, 0)
    for block in range(GROUP):
        device = start + block
        position = jnp.where(
            offset < stretch_rows,
            device * stretch_rows + offset,
            (2 * cycle_size - 2 - device) * stretch_rows + offset,
        )
        inside = (position >= first) & (position < ending)
        image = jnp.sum(jnp.where(inside, flag, 0.0), axis=1, keepdims=True)
        final = jnp.sum(jnp.where(inside, last, 0.0), axis=1, keepdims=True).astype(jnp.int32) - 1
        limit_ref[block] = jnp.where(image > 0.5, final, position)
        text_ref[block] = jnp.broadcast_to(1.0 - image, shape)
        lane = lax.broadcasted_iota(jnp.int32, (8, STEPS * rows), 1)
        step = jnp.zeros_like(lane)
        for edge in range(1, STEPS):
            step = step + (lane >= edge * rows).astype(jnp.int32)
        owner = device - (STEPS - 1) + step
        owner = jnp.where(owner < 0, owner + cycle_size, owner)
        within = lane - step * rows
        key_ref[block] = jnp.where(
            within < stretch_rows,
            owner * stretch_rows + within,
            (2 * cycle_size - 2 - owner) * stretch_rows + within,
        )


def sides(lengths, flags, after, stretch_rows, cycle_size):
    rows = 2 * stretch_rows
    return pl.pallas_call(
        functools.partial(sides_kernel, stretch_rows, cycle_size),
        out_shape=(
            jax.ShapeDtypeStruct((GROUP, rows, HEAD), jnp.int32),
            jax.ShapeDtypeStruct((GROUP, rows, HEAD), jnp.float32),
            jax.ShapeDtypeStruct((GROUP, 8, STEPS * rows), jnp.int32),
        ),
        in_specs=[VMEM, VMEM, ANY],
        out_specs=(VMEM,) * 3,
        compiler_params=SMALL,
        cost_estimate=pl.CostEstimate(flops=GROUP * rows * HEAD * 8, bytes_accessed=GROUP * rows * HEAD * 8, transcendentals=0),
        name="sides",
    )(lengths, flags, after)


def attend_kernel(
    chunk, total_rows, text_one, text_two, text_three, text_four, limit_ref, text_ref, keypos_ref,
    queries, keys, values, grads, key_one, key_two, key_three, query_one, query_two, query_three,
    edge_ref, query_own, query_to_one, query_to_two, query_to_three, main_ref, far_ref,
    key_all, value_all, query_all, grad_all, key_grad, value_grad, query_out,
):
    rows, width = queries.shape[0], edge_ref.shape[2]
    edge = (GROUP - 1) * rows
    span = STEPS * rows
    scale = HEAD ** (-0.5)
    place = lax.rem(lax.axis_index("ctx"), GROUP)
    counted = text_one[...] + text_two[...] + text_three[...] + text_four[...]
    factor = total_rows / jnp.sum(counted, axis=1, keepdims=True)
    lanes = columns(place, 0, chunk, width)
    key_all[:edge, :] = edge_ref[0]
    value_all[:edge, :] = edge_ref[1]
    sources = [(keys.at[:, lanes], values.at[:, lanes], queries.at[:, lanes], grads.at[:, lanes])]
    for pair, query_pair in ((key_one, query_one), (key_two, query_two), (key_three, query_three)):
        sources.append((pair.at[0], pair.at[1], query_pair.at[0], query_pair.at[1]))
    for slot, away in enumerate(aways()):
        start = pl.multiple_of(lax.rem(place + GROUP - away, GROUP) * rows, rows)
        key, value, query, grad = sources[slot]
        key_all[pl.ds(edge + start, rows), :] = key[...]
        value_all[pl.ds(edge + start, rows), :] = value[...]
        query_all[pl.ds(start, rows), :] = query[...]
        grad_all[pl.ds(start, rows), :] = grad[...]
    for block in range(GROUP):
        at = slice(block * rows, (block + 1) * rows)
        window = slice(block * rows, block * rows + span)
        limit = limit_ref[block]
        allowed = jnp.concatenate(
            [
                keypos_ref[block, 0:1, tile * HEAD : (tile + 1) * HEAD] <= limit
                for tile in range(span // HEAD)
            ],
            axis=1,
        )
        weight = text_ref[block] * factor
        for head in range(width // HEAD):
            lanes = slice(head * HEAD, (head + 1) * HEAD)
            query = query_all[at, lanes]
            grad = (grad_all[at, lanes].astype(jnp.float32) * weight).astype(jnp.bfloat16)
            key = key_all[window, lanes]
            value = value_all[window, lanes]
            scores = lax.dot_general(
                query, key, (((1,), (1,)), ((), ())), preferred_element_type=jnp.float32
            )
            scores = jnp.where(allowed, scores, MASKED)
            largest = jnp.max(scores, axis=1, keepdims=True)
            prob = jnp.exp2((scores - largest) * (scale * LOG2E))
            dprob = lax.dot_general(
                grad, value, (((1,), (1,)), ((), ())), preferred_element_type=jnp.float32
            )
            total = jnp.sum(prob, axis=1, keepdims=True)
            inverse = 1.0 / total
            delta = jnp.sum(prob * dprob, axis=1, keepdims=True) * inverse
            prob = prob * inverse
            dscore = (prob * (dprob - delta)).astype(jnp.bfloat16)
            prob_half = prob.astype(jnp.bfloat16)
            query_out[at, lanes] = (
                jnp.dot(dscore, key, preferred_element_type=jnp.float32) * scale
            ).astype(jnp.bfloat16)
            for kind, (left, right, held, scaling) in enumerate(
                ((dscore, query, key_grad, scale), (prob_half, grad, value_grad, 1.0))
            ):
                term = lax.dot_general(
                    right, left, (((0,), (0,)), ((), ())), preferred_element_type=jnp.float32
                ).T
                for step in range(STEPS):
                    index = block + step
                    here = slice(index * rows, (index + 1) * rows)
                    part = term[step * rows : (step + 1) * rows]
                    if block > 0 and step < STEPS - 1:
                        part = part + held[here, lanes]
                    if step > 0 and block < GROUP - 1:
                        held[here, lanes] = part
                    elif index < GROUP - 1:
                        far_ref[kind, here, lanes] = (part * scaling).astype(jnp.bfloat16)
                    else:
                        there = slice((index - GROUP + 1) * rows, (index - GROUP + 2) * rows)
                        main_ref[kind, there, lanes] = (part * scaling).astype(jnp.bfloat16)
    for away, block in zip(aways(), (query_own, query_to_one, query_to_two, query_to_three)):
        index = lax.rem(place + away, GROUP)
        block[...] = query_out[pl.ds(pl.multiple_of(index * rows, rows), rows), :]


def attend(texts, marks, arrays, key_blocks, query_blocks, edge, chunk, total_rows):
    _, rows, width = key_blocks[0].shape
    heads = width // HEAD
    keys = (2 * GROUP - 1) * rows
    pairs = heads * GROUP * rows * STEPS * rows
    return pl.pallas_call(
        functools.partial(attend_kernel, chunk, total_rows),
        out_shape=(
            *[jax.ShapeDtypeStruct((rows, width), jnp.bfloat16)] * GROUP,
            jax.ShapeDtypeStruct((2, GROUP * rows, width), jnp.bfloat16),
            jax.ShapeDtypeStruct((2, (GROUP - 1) * rows, width), jnp.bfloat16),
        ),
        in_specs=[VMEM] * (len(texts) + 14),
        out_specs=(VMEM,) * (GROUP + 2),
        scratch_shapes=[
            pltpu.VMEM((keys, width), jnp.bfloat16),
            pltpu.VMEM((keys, width), jnp.bfloat16),
            pltpu.VMEM((GROUP * rows, width), jnp.bfloat16),
            pltpu.VMEM((GROUP * rows, width), jnp.bfloat16),
            pltpu.VMEM((keys, width), jnp.float32),
            pltpu.VMEM((keys, width), jnp.float32),
            pltpu.VMEM((GROUP * rows, width), jnp.bfloat16),
        ],
        compiler_params=pltpu.CompilerParams(vmem_limit_bytes=24 * 1024 * 1024),
        cost_estimate=pl.CostEstimate(
            flops=4500000000, bytes_accessed=0, transcendentals=0
        ),
        name="attend",
    )(*texts, *marks, *arrays, *key_blocks, *query_blocks, edge)


def settle_kernel(main_ref, far_ref, *refs):
    extra = refs[: len(refs) // GROUP * GROUP - GROUP]
    outs = refs[len(refs) - GROUP :]
    rows = outs[0].shape[1]
    first_kind = 1 if extra else 0
    place = lax.rem(lax.axis_index("ctx"), GROUP)
    for slot, (away, block) in enumerate(zip(aways(), outs)):
        index = lax.rem(place + away, GROUP)
        start = pl.multiple_of(index * rows, rows)
        if extra:
            block[0] = extra[slot][...]

        @pl.when(index == 0)
        def first():
            block[first_kind:] = main_ref[:, :rows, :]

        @pl.when(index > 0)
        def later():
            behind = pl.multiple_of(start - rows, rows)
            block[first_kind:] = (
                main_ref[:, pl.ds(start, rows), :].astype(jnp.float32)
                + far_ref[:, pl.ds(behind, rows), :].astype(jnp.float32)
            ).astype(jnp.bfloat16)


def settle(main, far, extra=(), after=()):
    _, total, width = main.shape
    rows = total // GROUP
    count = 2 + (1 if extra else 0)

    def kernel(main_ref, far_ref, *refs):
        refs = list(refs)
        settle_kernel(main_ref, far_ref, *refs[: len(extra)], *refs[-GROUP:])

    return pl.pallas_call(
        kernel,
        out_shape=(jax.ShapeDtypeStruct((count, rows, width), jnp.bfloat16),) * GROUP,
        in_specs=[VMEM, VMEM] + [VMEM] * len(extra) + [ANY] * len(after),
        out_specs=(VMEM,) * GROUP,
        compiler_params=SMALL,
        cost_estimate=pl.CostEstimate(
            flops=SETTLE_COST if extra else 0, bytes_accessed=main.size * 8, transcendentals=0
        ),
        name="settle",
    )(main, far, *extra, *after)


def place_copies(moves, sems):
    copies = []
    for source, target, chunk, slot in moves:
        lanes = columns(lax.rem(lax.axis_index("ctx"), GROUP), -aways()[slot], chunk, source.shape[1])
        copies.append(pltpu.make_async_copy(source, target.at[:, lanes], sems.at[len(copies)]))
    for copy in copies:
        copy.start()
    for copy in copies:
        copy.wait()


def early_kernel(*refs):
    queries, mixed = refs[:GROUP], refs[GROUP : 2 * GROUP]
    query_ref, key_ref, value_ref, sems = refs[2 * GROUP :]
    moves = []
    for away in range(GROUP):
        moves += [
            (queries[away], query_ref, 0, away),
            (mixed[away].at[0], query_ref, 1, away),
            (mixed[away].at[1], key_ref, 0, away),
            (mixed[away].at[2], value_ref, 0, away),
        ]
    place_copies(moves, sems)


def late_kernel(*refs):
    pairs = refs[:GROUP]
    key_ref, value_ref, sems = refs[GROUP + 2 :]
    moves = []
    for away in range(GROUP):
        moves += [
            (pairs[away].at[0], key_ref, 1, away),
            (pairs[away].at[1], value_ref, 1, away),
        ]
    place_copies(moves, sems)


def gathered(queries, mixed, pairs):
    rows, width = queries[0].shape
    out = jax.ShapeDtypeStruct((rows, width * CHUNKS * GROUP), jnp.bfloat16)
    grad_queries, grad_keys, grad_values = pl.pallas_call(
        early_kernel,
        out_shape=(out, out, out),
        in_specs=[VMEM] * (2 * GROUP),
        out_specs=(ANY,) * 3,
        scratch_shapes=[pltpu.SemaphoreType.DMA((4 * GROUP,))],
        compiler_params=SMALL,
        cost_estimate=pl.CostEstimate(flops=0, bytes_accessed=out.size * 6, transcendentals=0),
        name="early",
    )(*queries, *mixed)
    grad_keys, grad_values = pl.pallas_call(
        late_kernel,
        out_shape=(out, out),
        in_specs=[VMEM] * GROUP + [ANY, ANY],
        out_specs=(ANY, ANY),
        input_output_aliases={GROUP: 0, GROUP + 1: 1},
        scratch_shapes=[pltpu.SemaphoreType.DMA((2 * GROUP,))],
        compiler_params=SMALL,
        cost_estimate=pl.CostEstimate(flops=0, bytes_accessed=out.size * 6, transcendentals=0),
        name="late",
    )(*pairs, grad_keys, grad_values)
    return grad_queries, grad_keys, grad_values


def shards(queries, keys, values, grad_out, lengths, image_flags):
    query_rows, key_rows, value_rows, grad_rows = queries[0], keys[0], values[0], grad_out[0]
    row_count = query_rows.shape[0]
    cycle_size = lax.axis_size("ctx")
    samples = lax.axis_size("dp")

    def swap(value, slot):
        pairs = []
        for sample in range(samples):
            core = sample % 2
            away = (1 + 2 * core, 3 - 2 * core, 2)[slot]
            for source in range(cycle_size):
                target = source - source % GROUP + (source + away) % GROUP
                pairs.append((sample * cycle_size + source, sample * cycle_size + target))
        return lax.ppermute(value, ("dp", "ctx"), pairs)

    def next_row(value, rows):
        pairs = [(source, (source + rows * GROUP) % cycle_size) for source in range(cycle_size)]
        return lax.ppermute(value, "ctx", pairs)

    def swapped(messages):
        return [swap(message, slot) for slot, message in enumerate(messages)]

    first_messages, text = first_pack(key_rows, value_rows, lengths, image_flags)
    texts = [text] + [
        lax.ppermute(text, "dp", [(source, (source + away) % samples) for source in range(samples)])
        for away in range(1, samples)
    ]
    total_rows = float(row_count * cycle_size * samples)

    key_packs, query_packs, edges = [None] * CHUNKS, [None] * CHUNKS, [None] * CHUNKS
    key_packs[0] = first_messages
    key_packs[1] = pack(key_rows, value_rows, text, 1)
    key_blocks = [swapped(messages) for messages in key_packs]
    edges[0] = make_edge(
        key_rows, value_rows, key_blocks[0], (*texts[1:], key_packs[1][0]), 0, EDGE_COST[0]
    )
    after = edges[0]
    for index in range(CHUNKS):
        query_packs[index] = pack(query_rows, grad_rows, after, index)
        after = query_packs[index][0]
    marks = sides(lengths, image_flags, after, row_count // 2, cycle_size)
    edges[1] = make_edge(
        key_rows, value_rows, key_blocks[1], (marks[1],), 1, EDGE_COST[1]
    )
    query_blocks = [swapped(messages) for messages in query_packs]
    edges = [next_row(edge, 1) for edge in edges]
    arrays = (query_rows, key_rows, value_rows, grad_rows)
    halves = []
    for chunk in range(CHUNKS):
        *query_grads, main, far = attend(
            texts, marks, arrays,
            key_blocks[chunk], query_blocks[chunk], edges[chunk], chunk, total_rows,
        )
        halves.append((query_grads, main, next_row(far, -1)))
    (first_queries, main, far), (second_queries, last_main, last_far) = halves
    queries = [first_queries[0]] + swapped(first_queries[1:])
    mixed = settle(main, far, extra=second_queries, after=queries[1:])
    pairs = settle(last_main, last_far)
    mixed = [mixed[0]] + swapped(mixed[1:])
    pairs = [pairs[0]] + swapped(pairs[1:])
    grad_queries, grad_keys, grad_values = gathered(queries, mixed, pairs)
    return grad_queries[None], grad_keys[None], grad_values[None]


def solution(mesh):
    in_specs = (
        P("dp", "ctx", None),
        P("dp", "ctx", None),
        P("dp", "ctx", None),
        P("dp", "ctx", None),
        P("dp", None),
        P("dp", None),
    )
    out_specs = (P("dp", "ctx", None), P("dp", "ctx", None), P("dp", "ctx", None))
    return jax.shard_map(shards, mesh=mesh, in_specs=in_specs, out_specs=out_specs, check_vma=False)
```

```python
import functools

import jax
import jax.numpy as jnp
from jax import lax
from jax.experimental import pallas as pl
from jax.experimental.pallas import tpu as pltpu
from jax.sharding import PartitionSpec as P

HEAD = 128
STEPS = 4
GROUP = 4
CHUNKS = 2
LOG2E = 1.4426950408889634
MASKED = -1e30
VMEM = pl.BlockSpec(memory_space=pltpu.VMEM)
ANY = pl.BlockSpec(memory_space=pl.ANY)
LARGE = pltpu.CompilerParams(vmem_limit_bytes=60 * 1024 * 1024)
EDGE_COST = (0, 6000000000)
SETTLE_COST = 3000000000
SMALL = pltpu.CompilerParams(vmem_limit_bytes=10 * 1024 * 1024)


def aways():
    core = lax.rem(lax.axis_index("dp"), 2)
    return 0, 2, 1 + 2 * core, 3 - 2 * core


def columns(place, away, chunk, width):
    index = lax.rem(place + GROUP + away, GROUP)
    return pl.ds(pl.multiple_of((index * CHUNKS + chunk) * width, width), width)


def pack_kernel(chunk, first, second, after, one, two, three):
    width = one.shape[2]
    for away, message in zip(aways()[1:], (one, two, three)):
        lanes = columns(lax.rem(lax.axis_index("ctx"), GROUP), away, chunk, width)
        message[0] = first[:, lanes]
        message[1] = second[:, lanes]


def first_pack_kernel(first, second, lengths, flags, one, two, three, text, held, sems):
    width = one.shape[2]
    place = lax.rem(lax.axis_index("ctx"), GROUP)
    copies = []
    for away, message in zip(aways()[1:], (one, two, three)):
        lanes = columns(place, away, 0, width)
        for part, source in enumerate((first, second)):
            copies.append(
                pltpu.make_async_copy(source.at[:, lanes], message.at[part], sems.at[len(copies)])
            )
    for part, source in enumerate((lengths, flags)):
        copies.append(pltpu.make_async_copy(source, held.at[part], sems.at[len(copies)]))
    for copy in copies:
        copy.start()
    for copy in copies:
        copy.wait()
    text[...] = (held[0] * (1 - held[1])).astype(jnp.float32)


def pack(first, second, after, chunk):
    rows, total = first.shape
    width = total // (GROUP * CHUNKS)
    message = jax.ShapeDtypeStruct((2, rows, width), first.dtype)
    return pl.pallas_call(
        functools.partial(pack_kernel, chunk),
        out_shape=(message,) * (GROUP - 1),
        in_specs=[VMEM, VMEM, ANY],
        out_specs=(VMEM,) * (GROUP - 1),
        compiler_params=SMALL,
        cost_estimate=pl.CostEstimate(flops=0, bytes_accessed=12 * rows * width * 2, transcendentals=0),
        name="pack",
    )(first, second, after)


def first_pack(first, second, lengths, flags):
    rows, total = first.shape
    width = total // (GROUP * CHUNKS)
    message = jax.ShapeDtypeStruct((2, rows, width), first.dtype)
    *messages, text = pl.pallas_call(
        first_pack_kernel,
        out_shape=(message,) * (GROUP - 1) + (jax.ShapeDtypeStruct(lengths.shape, jnp.float32),),
        in_specs=[ANY, ANY, ANY, ANY],
        out_specs=(VMEM,) * GROUP,
        scratch_shapes=[
            pltpu.VMEM((2, *lengths.shape), lengths.dtype),
            pltpu.SemaphoreType.DMA((2 * GROUP,)),
        ],
        compiler_params=LARGE,
        cost_estimate=pl.CostEstimate(flops=0, bytes_accessed=12 * rows * width * 2, transcendentals=0),
        name="first_pack",
    )(first, second, lengths, flags)
    return messages, text


def edge_kernel(chunk, first, second, one, two, three, *refs):
    edge = refs[-1]
    rows = edge.shape[1] // (GROUP - 1)
    width = edge.shape[2]
    place = lax.rem(lax.axis_index("ctx"), GROUP)
    for away, message in zip(aways(), (None, one, two, three)):
        index = lax.rem(place + GROUP - away, GROUP)

        @pl.when(index > 0)
        def put():
            at = pl.ds(pl.multiple_of((index - 1) * rows, rows), rows)
            if message is None:
                lanes = columns(place, 0, chunk, width)
                edge[0, at, :] = first[:, lanes]
                edge[1, at, :] = second[:, lanes]
            else:
                edge[:, at, :] = message[...]


def make_edge(first, second, blocks, afters, chunk, cost):
    _, rows, width = blocks[0].shape
    return pl.pallas_call(
        functools.partial(edge_kernel, chunk),
        out_shape=jax.ShapeDtypeStruct((2, (GROUP - 1) * rows, width), first.dtype),
        in_specs=[VMEM] * 5 + [ANY] * len(afters),
        out_specs=VMEM,
        compiler_params=SMALL,
        cost_estimate=pl.CostEstimate(flops=cost, bytes_accessed=0, transcendentals=0),
        name="edge",
    )(first, second, *blocks, *afters)


def sides_kernel(stretch_rows, cycle_size, lengths_ref, flags_ref, after, limit_ref, text_ref, key_ref):
    rows = 2 * stretch_rows
    device_here = lax.axis_index("ctx")
    start = device_here - lax.rem(device_here, GROUP)
    segments = lengths_ref.shape[1]
    square = (segments, segments)
    diagonal = lax.broadcasted_iota(jnp.int32, square, 0) == lax.broadcasted_iota(
        jnp.int32, square, 1
    )

    def upright(ref):
        row = jnp.broadcast_to(ref[...].astype(jnp.float32), square)
        return jnp.sum(jnp.where(diagonal, row, 0.0), axis=1, keepdims=True)

    lengths, flags = upright(lengths_ref), upright(flags_ref)
    source = lax.broadcasted_iota(jnp.int32, (segments, HEAD), 0)
    target = lax.broadcasted_iota(jnp.int32, (segments, HEAD), 1)

    def gathered_sum(mask, column):
        return jnp.sum(jnp.where(mask, column, 0.0), axis=0, keepdims=True)

    last = gathered_sum(source <= target, lengths)
    first = gathered_sum(source < target, lengths).astype(jnp.int32)
    flag = gathered_sum(source == target, flags)
    ending = last.astype(jnp.int32)
    shape = (rows, HEAD)
    offset = lax.broadcasted_iota(jnp.int32, shape, 0)
    for block in range(GROUP):
        device = start + block
        position = jnp.where(
            offset < stretch_rows,
            device * stretch_rows + offset,
            (2 * cycle_size - 2 - device) * stretch_rows + offset,
        )
        inside = (position >= first) & (position < ending)
        image = jnp.sum(jnp.where(inside, flag, 0.0), axis=1, keepdims=True)
        final = jnp.sum(jnp.where(inside, last, 0.0), axis=1, keepdims=True).astype(jnp.int32) - 1
        limit_ref[block] = jnp.where(image > 0.5, final, position)
        text_ref[block] = jnp.broadcast_to(1.0 - image, shape)
        lane = lax.broadcasted_iota(jnp.int32, (8, STEPS * rows), 1)
        step = jnp.zeros_like(lane)
        for edge in range(1, STEPS):
            step = step + (lane >= edge * rows).astype(jnp.int32)
        owner = device - (STEPS - 1) + step
        owner = jnp.where(owner < 0, owner + cycle_size, owner)
        within = lane - step * rows
        key_ref[block] = jnp.where(
            within < stretch_rows,
            owner * stretch_rows + within,
            (2 * cycle_size - 2 - owner) * stretch_rows + within,
        )


def sides(lengths, flags, after, stretch_rows, cycle_size):
    rows = 2 * stretch_rows
    return pl.pallas_call(
        functools.partial(sides_kernel, stretch_rows, cycle_size),
        out_shape=(
            jax.ShapeDtypeStruct((GROUP, rows, HEAD), jnp.int32),
            jax.ShapeDtypeStruct((GROUP, rows, HEAD), jnp.float32),
            jax.ShapeDtypeStruct((GROUP, 8, STEPS * rows), jnp.int32),
        ),
        in_specs=[VMEM, VMEM, ANY],
        out_specs=(VMEM,) * 3,
        compiler_params=SMALL,
        cost_estimate=pl.CostEstimate(flops=GROUP * rows * HEAD * 8, bytes_accessed=GROUP * rows * HEAD * 8, transcendentals=0),
        name="sides",
    )(lengths, flags, after)


def attend_kernel(
    chunk, total_rows, text_one, text_two, text_three, text_four, limit_ref, text_ref, keypos_ref,
    queries, keys, values, grads, key_one, key_two, key_three, query_one, query_two, query_three,
    edge_ref, query_own, query_to_one, query_to_two, query_to_three, main_ref, far_ref,
    key_all, value_all, query_all, grad_all, key_grad, value_grad, query_out,
):
    rows, width = queries.shape[0], edge_ref.shape[2]
    edge = (GROUP - 1) * rows
    span = STEPS * rows
    scale = HEAD ** (-0.5)
    place = lax.rem(lax.axis_index("ctx"), GROUP)
    counted = text_one[...] + text_two[...] + text_three[...] + text_four[...]
    factor = total_rows / jnp.sum(counted, axis=1, keepdims=True)
    lanes = columns(place, 0, chunk, width)
    key_all[:edge, :] = edge_ref[0]
    value_all[:edge, :] = edge_ref[1]
    sources = [(keys.at[:, lanes], values.at[:, lanes], queries.at[:, lanes], grads.at[:, lanes])]
    for pair, query_pair in ((key_one, query_one), (key_two, query_two), (key_three, query_three)):
        sources.append((pair.at[0], pair.at[1], query_pair.at[0], query_pair.at[1]))
    for slot, away in enumerate(aways()):
        start = pl.multiple_of(lax.rem(place + GROUP - away, GROUP) * rows, rows)
        key, value, query, grad = sources[slot]
        key_all[pl.ds(edge + start, rows), :] = key[...]
        value_all[pl.ds(edge + start, rows), :] = value[...]
        query_all[pl.ds(start, rows), :] = query[...]
        grad_all[pl.ds(start, rows), :] = grad[...]
    for block in range(GROUP):
        at = slice(block * rows, (block + 1) * rows)
        window = slice(block * rows, block * rows + span)
        limit = limit_ref[block]
        allowed = jnp.concatenate(
            [
                keypos_ref[block, 0:1, tile * HEAD : (tile + 1) * HEAD] <= limit
                for tile in range(span // HEAD)
            ],
            axis=1,
        )
        weight = text_ref[block] * factor
        for head in range(width // HEAD):
            lanes = slice(head * HEAD, (head + 1) * HEAD)
            query = query_all[at, lanes]
            grad = (grad_all[at, lanes].astype(jnp.float32) * weight).astype(jnp.bfloat16)
            key = key_all[window, lanes]
            value = value_all[window, lanes]
            scores = lax.dot_general(
                query, key, (((1,), (1,)), ((), ())), preferred_element_type=jnp.float32
            )
            scores = jnp.where(allowed, scores, MASKED)
            largest = jnp.max(scores, axis=1, keepdims=True)
            prob = jnp.exp2((scores - largest) * (scale * LOG2E))
            dprob = lax.dot_general(
                grad, value, (((1,), (1,)), ((), ())), preferred_element_type=jnp.float32
            )
            total = jnp.sum(prob, axis=1, keepdims=True)
            inverse = 1.0 / total
            delta = jnp.sum(prob * dprob, axis=1, keepdims=True) * inverse
            prob = prob * inverse
            dscore = (prob * (dprob - delta)).astype(jnp.bfloat16)
            prob_half = prob.astype(jnp.bfloat16)
            query_out[at, lanes] = (
                jnp.dot(dscore, key, preferred_element_type=jnp.float32) * scale
            ).astype(jnp.bfloat16)
            for kind, (left, right, held, scaling) in enumerate(
                ((dscore, query, key_grad, scale), (prob_half, grad, value_grad, 1.0))
            ):
                term = lax.dot_general(
                    right, left, (((0,), (0,)), ((), ())), preferred_element_type=jnp.float32
                ).T
                for step in range(STEPS):
                    index = block + step
                    here = slice(index * rows, (index + 1) * rows)
                    part = term[step * rows : (step + 1) * rows]
                    if block > 0 and step < STEPS - 1:
                        part = part + held[here, lanes]
                    if step > 0 and block < GROUP - 1:
                        held[here, lanes] = part
                    elif index < GROUP - 1:
                        far_ref[kind, here, lanes] = (part * scaling).astype(jnp.bfloat16)
                    else:
                        there = slice((index - GROUP + 1) * rows, (index - GROUP + 2) * rows)
                        main_ref[kind, there, lanes] = (part * scaling).astype(jnp.bfloat16)
    for away, block in zip(aways(), (query_own, query_to_one, query_to_two, query_to_three)):
        index = lax.rem(place + away, GROUP)
        block[...] = query_out[pl.ds(pl.multiple_of(index * rows, rows), rows), :]


def attend(texts, marks, arrays, key_blocks, query_blocks, edge, chunk, total_rows):
    _, rows, width = key_blocks[0].shape
    heads = width // HEAD
    keys = (2 * GROUP - 1) * rows
    pairs = heads * GROUP * rows * STEPS * rows
    return pl.pallas_call(
        functools.partial(attend_kernel, chunk, total_rows),
        out_shape=(
            *[jax.ShapeDtypeStruct((rows, width), jnp.bfloat16)] * GROUP,
            jax.ShapeDtypeStruct((2, GROUP * rows, width), jnp.bfloat16),
            jax.ShapeDtypeStruct((2, (GROUP - 1) * rows, width), jnp.bfloat16),
        ),
        in_specs=[VMEM] * (len(texts) + 14),
        out_specs=(VMEM,) * (GROUP + 2),
        scratch_shapes=[
            pltpu.VMEM((keys, width), jnp.bfloat16),
            pltpu.VMEM((keys, width), jnp.bfloat16),
            pltpu.VMEM((GROUP * rows, width), jnp.bfloat16),
            pltpu.VMEM((GROUP * rows, width), jnp.bfloat16),
            pltpu.VMEM((keys, width), jnp.float32),
            pltpu.VMEM((keys, width), jnp.float32),
            pltpu.VMEM((GROUP * rows, width), jnp.bfloat16),
        ],
        compiler_params=pltpu.CompilerParams(vmem_limit_bytes=24 * 1024 * 1024),
        cost_estimate=pl.CostEstimate(
            flops=4500000000, bytes_accessed=0, transcendentals=0
        ),
        name="attend",
    )(*texts, *marks, *arrays, *key_blocks, *query_blocks, edge)


def settle_kernel(main_ref, far_ref, *refs):
    extra = refs[: len(refs) // GROUP * GROUP - GROUP]
    outs = refs[len(refs) - GROUP :]
    rows = outs[0].shape[1]
    first_kind = 1 if extra else 0
    place = lax.rem(lax.axis_index("ctx"), GROUP)
    for slot, (away, block) in enumerate(zip(aways(), outs)):
        index = lax.rem(place + away, GROUP)
        start = pl.multiple_of(index * rows, rows)
        if extra:
            block[0] = extra[slot][...]

        @pl.when(index == 0)
        def first():
            block[first_kind:] = main_ref[:, :rows, :]

        @pl.when(index > 0)
        def later():
            behind = pl.multiple_of(start - rows, rows)
            block[first_kind:] = (
                main_ref[:, pl.ds(start, rows), :].astype(jnp.float32)
                + far_ref[:, pl.ds(behind, rows), :].astype(jnp.float32)
            ).astype(jnp.bfloat16)


def settle(main, far, extra=(), after=()):
    _, total, width = main.shape
    rows = total // GROUP
    count = 2 + (1 if extra else 0)

    def kernel(main_ref, far_ref, *refs):
        refs = list(refs)
        settle_kernel(main_ref, far_ref, *refs[: len(extra)], *refs[-GROUP:])

    return pl.pallas_call(
        kernel,
        out_shape=(jax.ShapeDtypeStruct((count, rows, width), jnp.bfloat16),) * GROUP,
        in_specs=[VMEM, VMEM] + [VMEM] * len(extra) + [ANY] * len(after),
        out_specs=(VMEM,) * GROUP,
        compiler_params=SMALL,
        cost_estimate=pl.CostEstimate(
            flops=SETTLE_COST if extra else 0, bytes_accessed=main.size * 8, transcendentals=0
        ),
        name="settle",
    )(main, far, *extra, *after)


def place_copies(moves, sems):
    copies = []
    for source, target, chunk, slot in moves:
        lanes = columns(lax.rem(lax.axis_index("ctx"), GROUP), -aways()[slot], chunk, source.shape[1])
        copies.append(pltpu.make_async_copy(source, target.at[:, lanes], sems.at[len(copies)]))
    for copy in copies:
        copy.start()
    for copy in copies:
        copy.wait()


def early_kernel(*refs):
    queries, mixed = refs[:GROUP], refs[GROUP : 2 * GROUP]
    query_ref, key_ref, value_ref, sems = refs[2 * GROUP :]
    moves = []
    for away in range(GROUP):
        moves += [
            (queries[away], query_ref, 0, away),
            (mixed[away].at[0], query_ref, 1, away),
            (mixed[away].at[1], key_ref, 0, away),
            (mixed[away].at[2], value_ref, 0, away),
        ]
    place_copies(moves, sems)


def late_kernel(*refs):
    pairs = refs[:GROUP]
    key_ref, value_ref, sems = refs[GROUP + 2 :]
    moves = []
    for away in range(GROUP):
        moves += [
            (pairs[away].at[0], key_ref, 1, away),
            (pairs[away].at[1], value_ref, 1, away),
        ]
    place_copies(moves, sems)


def gathered(queries, mixed, pairs):
    rows, width = queries[0].shape
    out = jax.ShapeDtypeStruct((rows, width * CHUNKS * GROUP), jnp.bfloat16)
    grad_queries, grad_keys, grad_values = pl.pallas_call(
        early_kernel,
        out_shape=(out, out, out),
        in_specs=[VMEM] * (2 * GROUP),
        out_specs=(ANY,) * 3,
        scratch_shapes=[pltpu.SemaphoreType.DMA((4 * GROUP,))],
        compiler_params=SMALL,
        cost_estimate=pl.CostEstimate(flops=0, bytes_accessed=out.size * 6, transcendentals=0),
        name="early",
    )(*queries, *mixed)
    grad_keys, grad_values = pl.pallas_call(
        late_kernel,
        out_shape=(out, out),
        in_specs=[VMEM] * GROUP + [ANY, ANY],
        out_specs=(ANY, ANY),
        input_output_aliases={GROUP: 0, GROUP + 1: 1},
        scratch_shapes=[pltpu.SemaphoreType.DMA((2 * GROUP,))],
        compiler_params=SMALL,
        cost_estimate=pl.CostEstimate(flops=0, bytes_accessed=out.size * 6, transcendentals=0),
        name="late",
    )(*pairs, grad_keys, grad_values)
    return grad_queries, grad_keys, grad_values


def shards(queries, keys, values, grad_out, lengths, image_flags):
    query_rows, key_rows, value_rows, grad_rows = queries[0], keys[0], values[0], grad_out[0]
    row_count = query_rows.shape[0]
    cycle_size = lax.axis_size("ctx")
    samples = lax.axis_size("dp")

    def swap(value, slot):
        pairs = []
        for sample in range(samples):
            core = sample % 2
            away = (2, 1 + 2 * core, 3 - 2 * core)[slot]
            for source in range(cycle_size):
                target = source - source % GROUP + (source + away) % GROUP
                pairs.append((sample * cycle_size + source, sample * cycle_size + target))
        return lax.ppermute(value, ("dp", "ctx"), pairs)

    def next_row(value, rows):
        pairs = [(source, (source + rows * GROUP) % cycle_size) for source in range(cycle_size)]
        return lax.ppermute(value, "ctx", pairs)

    def swapped(messages):
        return [swap(message, slot) for slot, message in enumerate(messages)]

    first_messages, text = first_pack(key_rows, value_rows, lengths, image_flags)
    texts = [text] + [
        lax.ppermute(text, "dp", [(source, (source + away) % samples) for source in range(samples)])
        for away in range(1, samples)
    ]
    total_rows = float(row_count * cycle_size * samples)

    key_packs, query_packs, edges = [None] * CHUNKS, [None] * CHUNKS, [None] * CHUNKS
    key_packs[0] = first_messages
    key_packs[1] = pack(key_rows, value_rows, text, 1)
    key_blocks = [swapped(messages) for messages in key_packs]
    edges[0] = make_edge(
        key_rows, value_rows, key_blocks[0], (*texts[1:], key_packs[1][0]), 0, EDGE_COST[0]
    )
    after = edges[0]
    for index in range(CHUNKS):
        query_packs[index] = pack(query_rows, grad_rows, after, index)
        after = query_packs[index][0]
    marks = sides(lengths, image_flags, after, row_count // 2, cycle_size)
    edges[1] = make_edge(
        key_rows, value_rows, key_blocks[1], (marks[1],), 1, EDGE_COST[1]
    )
    query_blocks = [swapped(messages) for messages in query_packs]
    edges = [next_row(edge, 1) for edge in edges]
    arrays = (query_rows, key_rows, value_rows, grad_rows)
    halves = []
    for chunk in range(CHUNKS):
        *query_grads, main, far = attend(
            texts, marks, arrays,
            key_blocks[chunk], query_blocks[chunk], edges[chunk], chunk, total_rows,
        )
        halves.append((query_grads, main, next_row(far, -1)))
    (first_queries, main, far), (second_queries, last_main, last_far) = halves
    queries = [first_queries[0]] + swapped(first_queries[1:])
    mixed = settle(main, far, extra=second_queries, after=queries[1:])
    pairs = settle(last_main, last_far)
    mixed = [mixed[0]] + swapped(mixed[1:])
    pairs = [pairs[0]] + swapped(pairs[1:])
    grad_queries, grad_keys, grad_values = gathered(queries, mixed, pairs)
    return grad_queries[None], grad_keys[None], grad_values[None]


def solution(mesh):
    in_specs = (
        P("dp", "ctx", None),
        P("dp", "ctx", None),
        P("dp", "ctx", None),
        P("dp", "ctx", None),
        P("dp", None),
        P("dp", None),
    )
    out_specs = (P("dp", "ctx", None), P("dp", "ctx", None), P("dp", "ctx", None))
    return jax.shard_map(shards, mesh=mesh, in_specs=in_specs, out_specs=out_specs, check_vma=False)
```

```python
import functools

import jax
import jax.numpy as jnp
from jax import lax
from jax.experimental import pallas as pl
from jax.experimental.pallas import tpu as pltpu
from jax.sharding import PartitionSpec as P

HEAD = 128
STEPS = 4
GROUP = 4
CHUNKS = 2
LOG2E = 1.4426950408889634
MASKED = -1e30
VMEM = pl.BlockSpec(memory_space=pltpu.VMEM)
ANY = pl.BlockSpec(memory_space=pl.ANY)
LARGE = pltpu.CompilerParams(vmem_limit_bytes=60 * 1024 * 1024)
EDGE_COST = (0, 6000000000)
SETTLE_COST = 3000000000
SMALL = pltpu.CompilerParams(vmem_limit_bytes=10 * 1024 * 1024)


def aways(turned=False):
    core = lax.rem(lax.axis_index("dp"), 2)
    if turned:
        return 0, 2, 1 + 2 * core, 3 - 2 * core
    return 0, 1 + 2 * core, 3 - 2 * core, 2


def columns(place, away, chunk, width):
    index = lax.rem(place + GROUP + away, GROUP)
    return pl.ds(pl.multiple_of((index * CHUNKS + chunk) * width, width), width)


def pack_kernel(chunk, turned, first, second, after, one, two, three):
    width = one.shape[2]
    for away, message in zip(aways(turned)[1:], (one, two, three)):
        lanes = columns(lax.rem(lax.axis_index("ctx"), GROUP), away, chunk, width)
        message[0] = first[:, lanes]
        message[1] = second[:, lanes]


def first_pack_kernel(first, second, lengths, flags, one, two, three, text, held, sems):
    width = one.shape[2]
    place = lax.rem(lax.axis_index("ctx"), GROUP)
    copies = []
    for away, message in zip(aways()[1:], (one, two, three)):
        lanes = columns(place, away, 0, width)
        for part, source in enumerate((first, second)):
            copies.append(
                pltpu.make_async_copy(source.at[:, lanes], message.at[part], sems.at[len(copies)])
            )
    for part, source in enumerate((lengths, flags)):
        copies.append(pltpu.make_async_copy(source, held.at[part], sems.at[len(copies)]))
    for copy in copies:
        copy.start()
    for copy in copies:
        copy.wait()
    text[...] = (held[0] * (1 - held[1])).astype(jnp.float32)


def pack(first, second, after, chunk, turned=False):
    rows, total = first.shape
    width = total // (GROUP * CHUNKS)
    message = jax.ShapeDtypeStruct((2, rows, width), first.dtype)
    return pl.pallas_call(
        functools.partial(pack_kernel, chunk, turned),
        out_shape=(message,) * (GROUP - 1),
        in_specs=[VMEM, VMEM, ANY],
        out_specs=(VMEM,) * (GROUP - 1),
        compiler_params=SMALL,
        cost_estimate=pl.CostEstimate(flops=0, bytes_accessed=12 * rows * width * 2, transcendentals=0),
        name="pack",
    )(first, second, after)


def first_pack(first, second, lengths, flags):
    rows, total = first.shape
    width = total // (GROUP * CHUNKS)
    message = jax.ShapeDtypeStruct((2, rows, width), first.dtype)
    *messages, text = pl.pallas_call(
        first_pack_kernel,
        out_shape=(message,) * (GROUP - 1) + (jax.ShapeDtypeStruct(lengths.shape, jnp.float32),),
        in_specs=[ANY, ANY, ANY, ANY],
        out_specs=(VMEM,) * GROUP,
        scratch_shapes=[
            pltpu.VMEM((2, *lengths.shape), lengths.dtype),
            pltpu.SemaphoreType.DMA((2 * GROUP,)),
        ],
        compiler_params=LARGE,
        cost_estimate=pl.CostEstimate(flops=0, bytes_accessed=12 * rows * width * 2, transcendentals=0),
        name="first_pack",
    )(first, second, lengths, flags)
    return messages, text


def edge_kernel(chunk, turned, first, second, one, two, three, *refs):
    edge = refs[-1]
    rows = edge.shape[1] // (GROUP - 1)
    width = edge.shape[2]
    place = lax.rem(lax.axis_index("ctx"), GROUP)
    for away, message in zip(aways(turned), (None, one, two, three)):
        index = lax.rem(place + GROUP - away, GROUP)

        @pl.when(index > 0)
        def put():
            at = pl.ds(pl.multiple_of((index - 1) * rows, rows), rows)
            if message is None:
                lanes = columns(place, 0, chunk, width)
                edge[0, at, :] = first[:, lanes]
                edge[1, at, :] = second[:, lanes]
            else:
                edge[:, at, :] = message[...]


def make_edge(first, second, blocks, afters, chunk, cost, turned=False):
    _, rows, width = blocks[0].shape
    return pl.pallas_call(
        functools.partial(edge_kernel, chunk, turned),
        out_shape=jax.ShapeDtypeStruct((2, (GROUP - 1) * rows, width), first.dtype),
        in_specs=[VMEM] * 5 + [ANY] * len(afters),
        out_specs=VMEM,
        compiler_params=SMALL,
        cost_estimate=pl.CostEstimate(flops=cost, bytes_accessed=0, transcendentals=0),
        name="edge",
    )(first, second, *blocks, *afters)


def sides_kernel(stretch_rows, cycle_size, lengths_ref, flags_ref, after, limit_ref, text_ref, key_ref):
    rows = 2 * stretch_rows
    device_here = lax.axis_index("ctx")
    start = device_here - lax.rem(device_here, GROUP)
    segments = lengths_ref.shape[1]
    square = (segments, segments)
    diagonal = lax.broadcasted_iota(jnp.int32, square, 0) == lax.broadcasted_iota(
        jnp.int32, square, 1
    )

    def upright(ref):
        row = jnp.broadcast_to(ref[...].astype(jnp.float32), square)
        return jnp.sum(jnp.where(diagonal, row, 0.0), axis=1, keepdims=True)

    lengths, flags = upright(lengths_ref), upright(flags_ref)
    source = lax.broadcasted_iota(jnp.int32, (segments, HEAD), 0)
    target = lax.broadcasted_iota(jnp.int32, (segments, HEAD), 1)

    def gathered_sum(mask, column):
        return jnp.sum(jnp.where(mask, column, 0.0), axis=0, keepdims=True)

    last = gathered_sum(source <= target, lengths)
    first = gathered_sum(source < target, lengths).astype(jnp.int32)
    flag = gathered_sum(source == target, flags)
    ending = last.astype(jnp.int32)
    shape = (rows, HEAD)
    offset = lax.broadcasted_iota(jnp.int32, shape, 0)
    for block in range(GROUP):
        device = start + block
        position = jnp.where(
            offset < stretch_rows,
            device * stretch_rows + offset,
            (2 * cycle_size - 2 - device) * stretch_rows + offset,
        )
        inside = (position >= first) & (position < ending)
        image = jnp.sum(jnp.where(inside, flag, 0.0), axis=1, keepdims=True)
        final = jnp.sum(jnp.where(inside, last, 0.0), axis=1, keepdims=True).astype(jnp.int32) - 1
        limit_ref[block] = jnp.where(image > 0.5, final, position)
        text_ref[block] = jnp.broadcast_to(1.0 - image, shape)
        lane = lax.broadcasted_iota(jnp.int32, (8, STEPS * rows), 1)
        step = jnp.zeros_like(lane)
        for edge in range(1, STEPS):
            step = step + (lane >= edge * rows).astype(jnp.int32)
        owner = device - (STEPS - 1) + step
        owner = jnp.where(owner < 0, owner + cycle_size, owner)
        within = lane - step * rows
        key_ref[block] = jnp.where(
            within < stretch_rows,
            owner * stretch_rows + within,
            (2 * cycle_size - 2 - owner) * stretch_rows + within,
        )


def sides(lengths, flags, after, stretch_rows, cycle_size):
    rows = 2 * stretch_rows
    return pl.pallas_call(
        functools.partial(sides_kernel, stretch_rows, cycle_size),
        out_shape=(
            jax.ShapeDtypeStruct((GROUP, rows, HEAD), jnp.int32),
            jax.ShapeDtypeStruct((GROUP, rows, HEAD), jnp.float32),
            jax.ShapeDtypeStruct((GROUP, 8, STEPS * rows), jnp.int32),
        ),
        in_specs=[VMEM, VMEM, ANY],
        out_specs=(VMEM,) * 3,
        compiler_params=SMALL,
        cost_estimate=pl.CostEstimate(flops=GROUP * rows * HEAD * 8, bytes_accessed=GROUP * rows * HEAD * 8, transcendentals=0),
        name="sides",
    )(lengths, flags, after)


def attend_kernel(
    chunk, turned, total_rows, text_one, text_two, text_three, text_four, limit_ref, text_ref, keypos_ref,
    queries, keys, values, grads, key_one, key_two, key_three, query_one, query_two, query_three,
    edge_ref, query_own, query_to_one, query_to_two, query_to_three, main_ref, far_ref,
    key_all, value_all, query_all, grad_all, key_grad, value_grad, query_out,
):
    rows, width = queries.shape[0], edge_ref.shape[2]
    edge = (GROUP - 1) * rows
    span = STEPS * rows
    scale = HEAD ** (-0.5)
    place = lax.rem(lax.axis_index("ctx"), GROUP)
    counted = text_one[...] + text_two[...] + text_three[...] + text_four[...]
    factor = total_rows / jnp.sum(counted, axis=1, keepdims=True)
    lanes = columns(place, 0, chunk, width)
    key_all[:edge, :] = edge_ref[0]
    value_all[:edge, :] = edge_ref[1]
    for order, pairs, targets, offset in (
        (aways(turned), (key_one, key_two, key_three), (key_all, value_all), edge),
        (aways(), (query_one, query_two, query_three), (query_all, grad_all), 0),
    ):
        owns = (keys, values) if offset else (queries, grads)
        for slot, away in enumerate(order):
            start = pl.multiple_of(lax.rem(place + GROUP - away, GROUP) * rows, rows)
            for part, target in enumerate(targets):
                block = owns[part][:, lanes] if slot == 0 else pairs[slot - 1][part]
                target[pl.ds(offset + start, rows), :] = block
    for block in range(GROUP):
        at = slice(block * rows, (block + 1) * rows)
        window = slice(block * rows, block * rows + span)
        limit = limit_ref[block]
        allowed = jnp.concatenate(
            [
                keypos_ref[block, 0:1, tile * HEAD : (tile + 1) * HEAD] <= limit
                for tile in range(span // HEAD)
            ],
            axis=1,
        )
        weight = text_ref[block] * factor
        for head in range(width // HEAD):
            lanes = slice(head * HEAD, (head + 1) * HEAD)
            query = query_all[at, lanes]
            grad = (grad_all[at, lanes].astype(jnp.float32) * weight).astype(jnp.bfloat16)
            key = key_all[window, lanes]
            value = value_all[window, lanes]
            scores = lax.dot_general(
                query, key, (((1,), (1,)), ((), ())), preferred_element_type=jnp.float32
            )
            scores = jnp.where(allowed, scores, MASKED)
            largest = jnp.max(scores, axis=1, keepdims=True)
            prob = jnp.exp2((scores - largest) * (scale * LOG2E))
            dprob = lax.dot_general(
                grad, value, (((1,), (1,)), ((), ())), preferred_element_type=jnp.float32
            )
            total = jnp.sum(prob, axis=1, keepdims=True)
            inverse = 1.0 / total
            delta = jnp.sum(prob * dprob, axis=1, keepdims=True) * inverse
            prob = prob * inverse
            dscore = (prob * (dprob - delta)).astype(jnp.bfloat16)
            prob_half = prob.astype(jnp.bfloat16)
            query_out[at, lanes] = (
                jnp.dot(dscore, key, preferred_element_type=jnp.float32) * scale
            ).astype(jnp.bfloat16)
            for kind, (left, right, held, scaling) in enumerate(
                ((dscore, query, key_grad, scale), (prob_half, grad, value_grad, 1.0))
            ):
                term = lax.dot_general(
                    right, left, (((0,), (0,)), ((), ())), preferred_element_type=jnp.float32
                ).T
                for step in range(STEPS):
                    index = block + step
                    here = slice(index * rows, (index + 1) * rows)
                    part = term[step * rows : (step + 1) * rows]
                    if block > 0 and step < STEPS - 1:
                        part = part + held[here, lanes]
                    if step > 0 and block < GROUP - 1:
                        held[here, lanes] = part
                    elif index < GROUP - 1:
                        far_ref[kind, here, lanes] = (part * scaling).astype(jnp.bfloat16)
                    else:
                        there = slice((index - GROUP + 1) * rows, (index - GROUP + 2) * rows)
                        main_ref[kind, there, lanes] = (part * scaling).astype(jnp.bfloat16)
    for away, block in zip(aways(), (query_own, query_to_one, query_to_two, query_to_three)):
        index = lax.rem(place + away, GROUP)
        block[...] = query_out[pl.ds(pl.multiple_of(index * rows, rows), rows), :]


def attend(texts, marks, arrays, key_blocks, query_blocks, edge, chunk, turned, total_rows):
    _, rows, width = key_blocks[0].shape
    heads = width // HEAD
    keys = (2 * GROUP - 1) * rows
    pairs = heads * GROUP * rows * STEPS * rows
    return pl.pallas_call(
        functools.partial(attend_kernel, chunk, turned, total_rows),
        out_shape=(
            *[jax.ShapeDtypeStruct((rows, width), jnp.bfloat16)] * GROUP,
            jax.ShapeDtypeStruct((2, GROUP * rows, width), jnp.bfloat16),
            jax.ShapeDtypeStruct((2, (GROUP - 1) * rows, width), jnp.bfloat16),
        ),
        in_specs=[VMEM] * (len(texts) + 14),
        out_specs=(VMEM,) * (GROUP + 2),
        scratch_shapes=[
            pltpu.VMEM((keys, width), jnp.bfloat16),
            pltpu.VMEM((keys, width), jnp.bfloat16),
            pltpu.VMEM((GROUP * rows, width), jnp.bfloat16),
            pltpu.VMEM((GROUP * rows, width), jnp.bfloat16),
            pltpu.VMEM((keys, width), jnp.float32),
            pltpu.VMEM((keys, width), jnp.float32),
            pltpu.VMEM((GROUP * rows, width), jnp.bfloat16),
        ],
        compiler_params=pltpu.CompilerParams(vmem_limit_bytes=24 * 1024 * 1024),
        cost_estimate=pl.CostEstimate(
            flops=4500000000, bytes_accessed=0, transcendentals=0
        ),
        name="attend",
    )(*texts, *marks, *arrays, *key_blocks, *query_blocks, edge)


def settle_kernel(main_ref, far_ref, *refs):
    extra = refs[: len(refs) // GROUP * GROUP - GROUP]
    outs = refs[len(refs) - GROUP :]
    rows = outs[0].shape[1]
    first_kind = 1 if extra else 0
    place = lax.rem(lax.axis_index("ctx"), GROUP)
    for slot, (away, block) in enumerate(zip(aways(), outs)):
        index = lax.rem(place + away, GROUP)
        start = pl.multiple_of(index * rows, rows)
        if extra:
            block[0] = extra[slot][...]

        @pl.when(index == 0)
        def first():
            block[first_kind:] = main_ref[:, :rows, :]

        @pl.when(index > 0)
        def later():
            behind = pl.multiple_of(start - rows, rows)
            block[first_kind:] = (
                main_ref[:, pl.ds(start, rows), :].astype(jnp.float32)
                + far_ref[:, pl.ds(behind, rows), :].astype(jnp.float32)
            ).astype(jnp.bfloat16)


def settle(main, far, extra=(), after=()):
    _, total, width = main.shape
    rows = total // GROUP
    count = 2 + (1 if extra else 0)

    def kernel(main_ref, far_ref, *refs):
        refs = list(refs)
        settle_kernel(main_ref, far_ref, *refs[: len(extra)], *refs[-GROUP:])

    return pl.pallas_call(
        kernel,
        out_shape=(jax.ShapeDtypeStruct((count, rows, width), jnp.bfloat16),) * GROUP,
        in_specs=[VMEM, VMEM] + [VMEM] * len(extra) + [ANY] * len(after),
        out_specs=(VMEM,) * GROUP,
        compiler_params=SMALL,
        cost_estimate=pl.CostEstimate(
            flops=SETTLE_COST if extra else 0, bytes_accessed=main.size * 8, transcendentals=0
        ),
        name="settle",
    )(main, far, *extra, *after)


def place_copies(moves, sems):
    copies = []
    for source, target, chunk, slot in moves:
        lanes = columns(lax.rem(lax.axis_index("ctx"), GROUP), -aways()[slot], chunk, source.shape[1])
        copies.append(pltpu.make_async_copy(source, target.at[:, lanes], sems.at[len(copies)]))
    for copy in copies:
        copy.start()
    for copy in copies:
        copy.wait()


def early_kernel(*refs):
    queries, mixed = refs[:GROUP], refs[GROUP : 2 * GROUP]
    query_ref, key_ref, value_ref, sems = refs[2 * GROUP :]
    moves = []
    for away in range(GROUP):
        moves += [
            (queries[away], query_ref, 0, away),
            (mixed[away].at[0], query_ref, 1, away),
            (mixed[away].at[1], key_ref, 0, away),
            (mixed[away].at[2], value_ref, 0, away),
        ]
    place_copies(moves, sems)


def late_kernel(*refs):
    pairs = refs[:GROUP]
    key_ref, value_ref, sems = refs[GROUP + 2 :]
    moves = []
    for away in range(GROUP):
        moves += [
            (pairs[away].at[0], key_ref, 1, away),
            (pairs[away].at[1], value_ref, 1, away),
        ]
    place_copies(moves, sems)


def gathered(queries, mixed, pairs):
    rows, width = queries[0].shape
    out = jax.ShapeDtypeStruct((rows, width * CHUNKS * GROUP), jnp.bfloat16)
    grad_queries, grad_keys, grad_values = pl.pallas_call(
        early_kernel,
        out_shape=(out, out, out),
        in_specs=[VMEM] * (2 * GROUP),
        out_specs=(ANY,) * 3,
        scratch_shapes=[pltpu.SemaphoreType.DMA((4 * GROUP,))],
        compiler_params=SMALL,
        cost_estimate=pl.CostEstimate(flops=0, bytes_accessed=out.size * 6, transcendentals=0),
        name="early",
    )(*queries, *mixed)
    grad_keys, grad_values = pl.pallas_call(
        late_kernel,
        out_shape=(out, out),
        in_specs=[VMEM] * GROUP + [ANY, ANY],
        out_specs=(ANY, ANY),
        input_output_aliases={GROUP: 0, GROUP + 1: 1},
        scratch_shapes=[pltpu.SemaphoreType.DMA((2 * GROUP,))],
        compiler_params=SMALL,
        cost_estimate=pl.CostEstimate(flops=0, bytes_accessed=out.size * 6, transcendentals=0),
        name="late",
    )(*pairs, grad_keys, grad_values)
    return grad_queries, grad_keys, grad_values


def shards(queries, keys, values, grad_out, lengths, image_flags):
    query_rows, key_rows, value_rows, grad_rows = queries[0], keys[0], values[0], grad_out[0]
    row_count = query_rows.shape[0]
    cycle_size = lax.axis_size("ctx")
    samples = lax.axis_size("dp")

    def swap(value, slot, turned):
        pairs = []
        for sample in range(samples):
            core = sample % 2
            order = (1 + 2 * core, 3 - 2 * core, 2)
            away = (order[-1:] + order[:-1])[slot] if turned else order[slot]
            for source in range(cycle_size):
                target = source - source % GROUP + (source + away) % GROUP
                pairs.append((sample * cycle_size + source, sample * cycle_size + target))
        return lax.ppermute(value, ("dp", "ctx"), pairs)

    def next_row(value, rows):
        pairs = [(source, (source + rows * GROUP) % cycle_size) for source in range(cycle_size)]
        return lax.ppermute(value, "ctx", pairs)

    def swapped(messages, turned=False):
        return [swap(message, slot, turned) for slot, message in enumerate(messages)]

    first_messages, text = first_pack(key_rows, value_rows, lengths, image_flags)
    texts = [text] + [
        lax.ppermute(text, "dp", [(source, (source + away) % samples) for source in range(samples)])
        for away in range(1, samples)
    ]
    total_rows = float(row_count * cycle_size * samples)

    key_packs, query_packs, edges = [None] * CHUNKS, [None] * CHUNKS, [None] * CHUNKS
    key_packs[0] = first_messages
    key_packs[1] = pack(key_rows, value_rows, text, 1, True)
    key_blocks = [swapped(messages, chunk == 1) for chunk, messages in enumerate(key_packs)]
    edges[0] = make_edge(
        key_rows, value_rows, key_blocks[0], (*texts[1:], key_packs[1][0]), 0, EDGE_COST[0]
    )
    after = edges[0]
    for index in range(CHUNKS):
        query_packs[index] = pack(query_rows, grad_rows, after, index)
        after = query_packs[index][0]
    marks = sides(lengths, image_flags, after, row_count // 2, cycle_size)
    edges[1] = make_edge(
        key_rows, value_rows, key_blocks[1], (marks[1],), 1, EDGE_COST[1], True
    )
    query_blocks = [swapped(messages) for messages in query_packs]
    edges = [next_row(edge, 1) for edge in edges]
    arrays = (query_rows, key_rows, value_rows, grad_rows)
    halves = []
    for chunk in range(CHUNKS):
        *query_grads, main, far = attend(
            texts, marks, arrays,
            key_blocks[chunk], query_blocks[chunk], edges[chunk], chunk, chunk == 1, total_rows,
        )
        halves.append((query_grads, main, next_row(far, -1)))
    (first_queries, main, far), (second_queries, last_main, last_far) = halves
    queries = [first_queries[0]] + swapped(first_queries[1:])
    mixed = settle(main, far, extra=second_queries, after=queries[1:])
    pairs = settle(last_main, last_far)
    mixed = [mixed[0]] + swapped(mixed[1:])
    pairs = [pairs[0]] + swapped(pairs[1:])
    grad_queries, grad_keys, grad_values = gathered(queries, mixed, pairs)
    return grad_queries[None], grad_keys[None], grad_values[None]


def solution(mesh):
    in_specs = (
        P("dp", "ctx", None),
        P("dp", "ctx", None),
        P("dp", "ctx", None),
        P("dp", "ctx", None),
        P("dp", None),
        P("dp", None),
    )
    out_specs = (P("dp", "ctx", None), P("dp", "ctx", None), P("dp", "ctx", None))
    return jax.shard_map(shards, mesh=mesh, in_specs=in_specs, out_specs=out_specs, check_vma=False)
```

```python
import functools

import jax
import jax.numpy as jnp
from jax import lax
from jax.experimental import pallas as pl
from jax.experimental.pallas import tpu as pltpu
from jax.sharding import PartitionSpec as P

HEAD = 128
STEPS = 4
GROUP = 4
CHUNKS = 2
LOG2E = 1.4426950408889634
MASKED = -1e30
VMEM = pl.BlockSpec(memory_space=pltpu.VMEM)
ANY = pl.BlockSpec(memory_space=pl.ANY)
LARGE = pltpu.CompilerParams(vmem_limit_bytes=60 * 1024 * 1024)
EDGE_COST = (0, 6000000000)
SETTLE_COST = 3000000000
SMALL = pltpu.CompilerParams(vmem_limit_bytes=10 * 1024 * 1024)


def aways():
    core = lax.rem(lax.axis_index("dp"), 2)
    return 0, 1 + 2 * core, 3 - 2 * core, 2


def columns(place, away, chunk, width):
    index = lax.rem(place + GROUP + away, GROUP)
    return pl.ds(pl.multiple_of((index * CHUNKS + chunk) * width, width), width)


def pack_kernel(chunk, first, second, after, one, two, three):
    width = one.shape[2]
    for away, message in zip(aways()[1:], (one, two, three)):
        lanes = columns(lax.rem(lax.axis_index("ctx"), GROUP), away, chunk, width)
        message[0] = first[:, lanes]
        message[1] = second[:, lanes]


def first_pack_kernel(first, second, lengths, flags, one, two, three, text, held, sems):
    width = one.shape[2]
    place = lax.rem(lax.axis_index("ctx"), GROUP)
    copies = []
    for away, message in zip(aways()[1:], (one, two, three)):
        lanes = columns(place, away, 0, width)
        for part, source in enumerate((first, second)):
            copies.append(
                pltpu.make_async_copy(source.at[:, lanes], message.at[part], sems.at[len(copies)])
            )
    for part, source in enumerate((lengths, flags)):
        copies.append(pltpu.make_async_copy(source, held.at[part], sems.at[len(copies)]))
    for copy in copies:
        copy.start()
    for copy in copies:
        copy.wait()
    text[...] = (held[0] * (1 - held[1])).astype(jnp.float32)


def pack(first, second, after, chunk):
    rows, total = first.shape
    width = total // (GROUP * CHUNKS)
    message = jax.ShapeDtypeStruct((2, rows, width), first.dtype)
    return pl.pallas_call(
        functools.partial(pack_kernel, chunk),
        out_shape=(message,) * (GROUP - 1),
        in_specs=[VMEM, VMEM, ANY],
        out_specs=(VMEM,) * (GROUP - 1),
        compiler_params=SMALL,
        cost_estimate=pl.CostEstimate(flops=0, bytes_accessed=12 * rows * width * 2, transcendentals=0),
        name="pack",
    )(first, second, after)


def first_pack(first, second, lengths, flags):
    rows, total = first.shape
    width = total // (GROUP * CHUNKS)
    message = jax.ShapeDtypeStruct((2, rows, width), first.dtype)
    *messages, text = pl.pallas_call(
        first_pack_kernel,
        out_shape=(message,) * (GROUP - 1) + (jax.ShapeDtypeStruct(lengths.shape, jnp.float32),),
        in_specs=[ANY, ANY, ANY, ANY],
        out_specs=(VMEM,) * GROUP,
        scratch_shapes=[
            pltpu.VMEM((2, *lengths.shape), lengths.dtype),
            pltpu.SemaphoreType.DMA((2 * GROUP,)),
        ],
        compiler_params=LARGE,
        cost_estimate=pl.CostEstimate(flops=0, bytes_accessed=12 * rows * width * 2, transcendentals=0),
        name="first_pack",
    )(first, second, lengths, flags)
    return messages, text


def edge_kernel(chunk, first, second, one, two, three, *refs):
    edge = refs[-1]
    rows = edge.shape[1] // (GROUP - 1)
    width = edge.shape[2]
    place = lax.rem(lax.axis_index("ctx"), GROUP)
    for away, message in zip(aways(), (None, one, two, three)):
        index = lax.rem(place + GROUP - away, GROUP)

        @pl.when(index > 0)
        def put():
            at = pl.ds(pl.multiple_of((index - 1) * rows, rows), rows)
            if message is None:
                lanes = columns(place, 0, chunk, width)
                edge[0, at, :] = first[:, lanes]
                edge[1, at, :] = second[:, lanes]
            else:
                edge[:, at, :] = message[...]


def make_edge(first, second, blocks, afters, chunk, cost):
    _, rows, width = blocks[0].shape
    return pl.pallas_call(
        functools.partial(edge_kernel, chunk),
        out_shape=jax.ShapeDtypeStruct((2, (GROUP - 1) * rows, width), first.dtype),
        in_specs=[VMEM] * 5 + [ANY] * len(afters),
        out_specs=VMEM,
        compiler_params=SMALL,
        cost_estimate=pl.CostEstimate(flops=cost, bytes_accessed=0, transcendentals=0),
        name="edge",
    )(first, second, *blocks, *afters)


def sides_kernel(stretch_rows, cycle_size, lengths_ref, flags_ref, after, limit_ref, text_ref, key_ref):
    rows = 2 * stretch_rows
    device_here = lax.axis_index("ctx")
    start = device_here - lax.rem(device_here, GROUP)
    segments = lengths_ref.shape[1]
    square = (segments, segments)
    diagonal = lax.broadcasted_iota(jnp.int32, square, 0) == lax.broadcasted_iota(
        jnp.int32, square, 1
    )

    def upright(ref):
        row = jnp.broadcast_to(ref[...].astype(jnp.float32), square)
        return jnp.sum(jnp.where(diagonal, row, 0.0), axis=1, keepdims=True)

    lengths, flags = upright(lengths_ref), upright(flags_ref)
    source = lax.broadcasted_iota(jnp.int32, (segments, HEAD), 0)
    target = lax.broadcasted_iota(jnp.int32, (segments, HEAD), 1)

    def gathered_sum(mask, column):
        return jnp.sum(jnp.where(mask, column, 0.0), axis=0, keepdims=True)

    last = gathered_sum(source <= target, lengths)
    first = gathered_sum(source < target, lengths).astype(jnp.int32)
    flag = gathered_sum(source == target, flags)
    ending = last.astype(jnp.int32)
    shape = (rows, HEAD)
    offset = lax.broadcasted_iota(jnp.int32, shape, 0)
    for block in range(GROUP):
        device = start + block
        position = jnp.where(
            offset < stretch_rows,
            device * stretch_rows + offset,
            (2 * cycle_size - 2 - device) * stretch_rows + offset,
        )
        inside = (position >= first) & (position < ending)
        image = jnp.sum(jnp.where(inside, flag, 0.0), axis=1, keepdims=True)
        final = jnp.sum(jnp.where(inside, last, 0.0), axis=1, keepdims=True).astype(jnp.int32) - 1
        limit_ref[block] = jnp.where(image > 0.5, final, position)
        text_ref[block] = jnp.broadcast_to(1.0 - image, shape)
        lane = lax.broadcasted_iota(jnp.int32, (8, STEPS * rows), 1)
        step = jnp.zeros_like(lane)
        for edge in range(1, STEPS):
            step = step + (lane >= edge * rows).astype(jnp.int32)
        owner = device - (STEPS - 1) + step
        owner = jnp.where(owner < 0, owner + cycle_size, owner)
        within = lane - step * rows
        key_ref[block] = jnp.where(
            within < stretch_rows,
            owner * stretch_rows + within,
            (2 * cycle_size - 2 - owner) * stretch_rows + within,
        )


def sides(lengths, flags, after, stretch_rows, cycle_size):
    rows = 2 * stretch_rows
    return pl.pallas_call(
        functools.partial(sides_kernel, stretch_rows, cycle_size),
        out_shape=(
            jax.ShapeDtypeStruct((GROUP, rows, HEAD), jnp.int32),
            jax.ShapeDtypeStruct((GROUP, rows, HEAD), jnp.float32),
            jax.ShapeDtypeStruct((GROUP, 8, STEPS * rows), jnp.int32),
        ),
        in_specs=[VMEM, VMEM, ANY],
        out_specs=(VMEM,) * 3,
        compiler_params=SMALL,
        cost_estimate=pl.CostEstimate(flops=GROUP * rows * HEAD * 8, bytes_accessed=GROUP * rows * HEAD * 8, transcendentals=0),
        name="sides",
    )(lengths, flags, after)


def attend_kernel(
    chunk, total_rows, text_one, text_two, text_three, text_four, limit_ref, text_ref, keypos_ref,
    queries, keys, values, grads, key_one, key_two, key_three, query_one, query_two, query_three,
    edge_ref, query_own, query_to_one, query_to_two, query_to_three, main_ref, far_ref,
    key_all, value_all, query_all, grad_all, key_grad, value_grad, query_out,
):
    rows, width = queries.shape[0], edge_ref.shape[2]
    edge = (GROUP - 1) * rows
    span = STEPS * rows
    scale = HEAD ** (-0.5)
    place = lax.rem(lax.axis_index("ctx"), GROUP)
    counted = text_one[...] + text_two[...] + text_three[...] + text_four[...]
    factor = total_rows / jnp.sum(counted, axis=1, keepdims=True)
    lanes = columns(place, 0, chunk, width)
    key_all[:edge, :] = edge_ref[0]
    value_all[:edge, :] = edge_ref[1]
    sources = [(keys.at[:, lanes], values.at[:, lanes], queries.at[:, lanes], grads.at[:, lanes])]
    for pair, query_pair in ((key_one, query_one), (key_two, query_two), (key_three, query_three)):
        sources.append((pair.at[0], pair.at[1], query_pair.at[0], query_pair.at[1]))
    for slot, away in enumerate(aways()):
        start = pl.multiple_of(lax.rem(place + GROUP - away, GROUP) * rows, rows)
        key, value, query, grad = sources[slot]
        key_all[pl.ds(edge + start, rows), :] = key[...]
        value_all[pl.ds(edge + start, rows), :] = value[...]
        query_all[pl.ds(start, rows), :] = query[...]
        grad_all[pl.ds(start, rows), :] = grad[...]
    for block in range(GROUP):
        at = slice(block * rows, (block + 1) * rows)
        window = slice(block * rows, block * rows + span)
        limit = limit_ref[block]
        allowed = jnp.concatenate(
            [
                keypos_ref[block, 0:1, tile * HEAD : (tile + 1) * HEAD] <= limit
                for tile in range(span // HEAD)
            ],
            axis=1,
        )
        weight = text_ref[block] * factor
        for head in range(width // HEAD):
            lanes = slice(head * HEAD, (head + 1) * HEAD)
            query = query_all[at, lanes]
            grad = (grad_all[at, lanes].astype(jnp.float32) * weight).astype(jnp.bfloat16)
            key = key_all[window, lanes]
            value = value_all[window, lanes]
            scores = lax.dot_general(
                query, key, (((1,), (1,)), ((), ())), preferred_element_type=jnp.float32
            )
            scores = jnp.where(allowed, scores, MASKED)
            largest = jnp.max(scores, axis=1, keepdims=True)
            prob = jnp.exp2((scores - largest) * (scale * LOG2E))
            dprob = lax.dot_general(
                grad, value, (((1,), (1,)), ((), ())), preferred_element_type=jnp.float32
            )
            total = jnp.sum(prob, axis=1, keepdims=True)
            inverse = 1.0 / total
            delta = jnp.sum(prob * dprob, axis=1, keepdims=True) * inverse
            prob = prob * inverse
            dscore = (prob * (dprob - delta)).astype(jnp.bfloat16)
            prob_half = prob.astype(jnp.bfloat16)
            query_out[at, lanes] = (
                lax.dot_general(
                    key, dscore, (((0,), (1,)), ((), ())), preferred_element_type=jnp.float32
                ).T
                * scale
            ).astype(jnp.bfloat16)
            for kind, (left, right, held, scaling) in enumerate(
                ((dscore, query, key_grad, scale), (prob_half, grad, value_grad, 1.0))
            ):
                term = lax.dot_general(
                    right, left, (((0,), (0,)), ((), ())), preferred_element_type=jnp.float32
                ).T
                for step in range(STEPS):
                    index = block + step
                    here = slice(index * rows, (index + 1) * rows)
                    part = term[step * rows : (step + 1) * rows]
                    if block > 0 and step < STEPS - 1:
                        part = part + held[here, lanes]
                    if step > 0 and block < GROUP - 1:
                        held[here, lanes] = part
                    elif index < GROUP - 1:
                        far_ref[kind, here, lanes] = (part * scaling).astype(jnp.bfloat16)
                    else:
                        there = slice((index - GROUP + 1) * rows, (index - GROUP + 2) * rows)
                        main_ref[kind, there, lanes] = (part * scaling).astype(jnp.bfloat16)
    for away, block in zip(aways(), (query_own, query_to_one, query_to_two, query_to_three)):
        index = lax.rem(place + away, GROUP)
        block[...] = query_out[pl.ds(pl.multiple_of(index * rows, rows), rows), :]


def attend(texts, marks, arrays, key_blocks, query_blocks, edge, chunk, total_rows):
    _, rows, width = key_blocks[0].shape
    heads = width // HEAD
    keys = (2 * GROUP - 1) * rows
    pairs = heads * GROUP * rows * STEPS * rows
    return pl.pallas_call(
        functools.partial(attend_kernel, chunk, total_rows),
        out_shape=(
            *[jax.ShapeDtypeStruct((rows, width), jnp.bfloat16)] * GROUP,
            jax.ShapeDtypeStruct((2, GROUP * rows, width), jnp.bfloat16),
            jax.ShapeDtypeStruct((2, (GROUP - 1) * rows, width), jnp.bfloat16),
        ),
        in_specs=[VMEM] * (len(texts) + 14),
        out_specs=(VMEM,) * (GROUP + 2),
        scratch_shapes=[
            pltpu.VMEM((keys, width), jnp.bfloat16),
            pltpu.VMEM((keys, width), jnp.bfloat16),
            pltpu.VMEM((GROUP * rows, width), jnp.bfloat16),
            pltpu.VMEM((GROUP * rows, width), jnp.bfloat16),
            pltpu.VMEM((keys, width), jnp.float32),
            pltpu.VMEM((keys, width), jnp.float32),
            pltpu.VMEM((GROUP * rows, width), jnp.bfloat16),
        ],
        compiler_params=pltpu.CompilerParams(vmem_limit_bytes=24 * 1024 * 1024),
        cost_estimate=pl.CostEstimate(
            flops=4500000000, bytes_accessed=0, transcendentals=0
        ),
        name="attend",
    )(*texts, *marks, *arrays, *key_blocks, *query_blocks, edge)


def settle_kernel(main_ref, far_ref, *refs):
    extra = refs[: len(refs) // GROUP * GROUP - GROUP]
    outs = refs[len(refs) - GROUP :]
    rows = outs[0].shape[1]
    first_kind = 1 if extra else 0
    place = lax.rem(lax.axis_index("ctx"), GROUP)
    for slot, (away, block) in enumerate(zip(aways(), outs)):
        index = lax.rem(place + away, GROUP)
        start = pl.multiple_of(index * rows, rows)
        if extra:
            block[0] = extra[slot][...]

        @pl.when(index == 0)
        def first():
            block[first_kind:] = main_ref[:, :rows, :]

        @pl.when(index > 0)
        def later():
            behind = pl.multiple_of(start - rows, rows)
            block[first_kind:] = (
                main_ref[:, pl.ds(start, rows), :].astype(jnp.float32)
                + far_ref[:, pl.ds(behind, rows), :].astype(jnp.float32)
            ).astype(jnp.bfloat16)


def settle(main, far, extra=(), after=()):
    _, total, width = main.shape
    rows = total // GROUP
    count = 2 + (1 if extra else 0)

    def kernel(main_ref, far_ref, *refs):
        refs = list(refs)
        settle_kernel(main_ref, far_ref, *refs[: len(extra)], *refs[-GROUP:])

    return pl.pallas_call(
        kernel,
        out_shape=(jax.ShapeDtypeStruct((count, rows, width), jnp.bfloat16),) * GROUP,
        in_specs=[VMEM, VMEM] + [VMEM] * len(extra) + [ANY] * len(after),
        out_specs=(VMEM,) * GROUP,
        compiler_params=SMALL,
        cost_estimate=pl.CostEstimate(
            flops=SETTLE_COST if extra else 0, bytes_accessed=main.size * 8, transcendentals=0
        ),
        name="settle",
    )(main, far, *extra, *after)


def place_copies(moves, sems):
    copies = []
    for source, target, chunk, slot in moves:
        lanes = columns(lax.rem(lax.axis_index("ctx"), GROUP), -aways()[slot], chunk, source.shape[1])
        copies.append(pltpu.make_async_copy(source, target.at[:, lanes], sems.at[len(copies)]))
    for copy in copies:
        copy.start()
    for copy in copies:
        copy.wait()


def early_kernel(*refs):
    queries, mixed = refs[:GROUP], refs[GROUP : 2 * GROUP]
    query_ref, key_ref, value_ref, sems = refs[2 * GROUP :]
    moves = []
    for away in range(GROUP):
        moves += [
            (queries[away], query_ref, 0, away),
            (mixed[away].at[0], query_ref, 1, away),
            (mixed[away].at[1], key_ref, 0, away),
            (mixed[away].at[2], value_ref, 0, away),
        ]
    place_copies(moves, sems)


def late_kernel(*refs):
    pairs = refs[:GROUP]
    key_ref, value_ref, sems = refs[GROUP + 2 :]
    moves = []
    for away in range(GROUP):
        moves += [
            (pairs[away].at[0], key_ref, 1, away),
            (pairs[away].at[1], value_ref, 1, away),
        ]
    place_copies(moves, sems)


def gathered(queries, mixed, pairs):
    rows, width = queries[0].shape
    out = jax.ShapeDtypeStruct((rows, width * CHUNKS * GROUP), jnp.bfloat16)
    grad_queries, grad_keys, grad_values = pl.pallas_call(
        early_kernel,
        out_shape=(out, out, out),
        in_specs=[VMEM] * (2 * GROUP),
        out_specs=(ANY,) * 3,
        scratch_shapes=[pltpu.SemaphoreType.DMA((4 * GROUP,))],
        compiler_params=SMALL,
        cost_estimate=pl.CostEstimate(flops=0, bytes_accessed=out.size * 6, transcendentals=0),
        name="early",
    )(*queries, *mixed)
    grad_keys, grad_values = pl.pallas_call(
        late_kernel,
        out_shape=(out, out),
        in_specs=[VMEM] * GROUP + [ANY, ANY],
        out_specs=(ANY, ANY),
        input_output_aliases={GROUP: 0, GROUP + 1: 1},
        scratch_shapes=[pltpu.SemaphoreType.DMA((2 * GROUP,))],
        compiler_params=SMALL,
        cost_estimate=pl.CostEstimate(flops=0, bytes_accessed=out.size * 6, transcendentals=0),
        name="late",
    )(*pairs, grad_keys, grad_values)
    return grad_queries, grad_keys, grad_values


def shards(queries, keys, values, grad_out, lengths, image_flags):
    query_rows, key_rows, value_rows, grad_rows = queries[0], keys[0], values[0], grad_out[0]
    row_count = query_rows.shape[0]
    cycle_size = lax.axis_size("ctx")
    samples = lax.axis_size("dp")

    def swap(value, slot):
        pairs = []
        for sample in range(samples):
            core = sample % 2
            away = (1 + 2 * core, 3 - 2 * core, 2)[slot]
            for source in range(cycle_size):
                target = source - source % GROUP + (source + away) % GROUP
                pairs.append((sample * cycle_size + source, sample * cycle_size + target))
        return lax.ppermute(value, ("dp", "ctx"), pairs)

    def next_row(value, rows):
        pairs = [(source, (source + rows * GROUP) % cycle_size) for source in range(cycle_size)]
        return lax.ppermute(value, "ctx", pairs)

    def swapped(messages):
        return [swap(message, slot) for slot, message in enumerate(messages)]

    first_messages, text = first_pack(key_rows, value_rows, lengths, image_flags)
    texts = [text] + [
        lax.ppermute(text, "dp", [(source, (source + away) % samples) for source in range(samples)])
        for away in range(1, samples)
    ]
    total_rows = float(row_count * cycle_size * samples)

    key_packs, query_packs, edges = [None] * CHUNKS, [None] * CHUNKS, [None] * CHUNKS
    key_packs[0] = first_messages
    key_packs[1] = pack(key_rows, value_rows, text, 1)
    key_blocks = [swapped(messages) for messages in key_packs]
    edges[0] = make_edge(
        key_rows, value_rows, key_blocks[0], (*texts[1:], key_packs[1][0]), 0, EDGE_COST[0]
    )
    after = edges[0]
    for index in range(CHUNKS):
        query_packs[index] = pack(query_rows, grad_rows, after, index)
        after = query_packs[index][0]
    marks = sides(lengths, image_flags, after, row_count // 2, cycle_size)
    edges[1] = make_edge(
        key_rows, value_rows, key_blocks[1], (marks[1],), 1, EDGE_COST[1]
    )
    query_blocks = [swapped(messages) for messages in query_packs]
    edges = [next_row(edge, 1) for edge in edges]
    arrays = (query_rows, key_rows, value_rows, grad_rows)
    halves = []
    for chunk in range(CHUNKS):
        *query_grads, main, far = attend(
            texts, marks, arrays,
            key_blocks[chunk], query_blocks[chunk], edges[chunk], chunk, total_rows,
        )
        halves.append((query_grads, main, next_row(far, -1)))
    (first_queries, main, far), (second_queries, last_main, last_far) = halves
    queries = [first_queries[0]] + swapped(first_queries[1:])
    mixed = settle(main, far, extra=second_queries, after=queries[1:])
    pairs = settle(last_main, last_far)
    mixed = [mixed[0]] + swapped(mixed[1:])
    pairs = [pairs[0]] + swapped(pairs[1:])
    grad_queries, grad_keys, grad_values = gathered(queries, mixed, pairs)
    return grad_queries[None], grad_keys[None], grad_values[None]


def solution(mesh):
    in_specs = (
        P("dp", "ctx", None),
        P("dp", "ctx", None),
        P("dp", "ctx", None),
        P("dp", "ctx", None),
        P("dp", None),
        P("dp", None),
    )
    out_specs = (P("dp", "ctx", None), P("dp", "ctx", None), P("dp", "ctx", None))
    return jax.shard_map(shards, mesh=mesh, in_specs=in_specs, out_specs=out_specs, check_vma=False)
```

```python
import functools

import jax
import jax.numpy as jnp
from jax import lax
from jax.experimental import pallas as pl
from jax.experimental.pallas import tpu as pltpu
from jax.sharding import PartitionSpec as P

HEAD = 128
STEPS = 4
GROUP = 4
CHUNKS = 2
LOG2E = 1.4426950408889634
MASKED = -1e30
VMEM = pl.BlockSpec(memory_space=pltpu.VMEM)
ANY = pl.BlockSpec(memory_space=pl.ANY)
LARGE = pltpu.CompilerParams(vmem_limit_bytes=60 * 1024 * 1024)
EDGE_COST = (0, 3000000000)
SETTLE_COST = 3000000000
SMALL = pltpu.CompilerParams(vmem_limit_bytes=10 * 1024 * 1024)


def aways():
    core = lax.rem(lax.axis_index("dp"), 2)
    return 0, 1 + 2 * core, 3 - 2 * core, 2


def columns(place, away, chunk, width):
    index = lax.rem(place + GROUP + away, GROUP)
    return pl.ds(pl.multiple_of((index * CHUNKS + chunk) * width, width), width)


def pack_kernel(chunk, first, second, after, one, two, three):
    width = one.shape[2]
    for away, message in zip(aways()[1:], (one, two, three)):
        lanes = columns(lax.rem(lax.axis_index("ctx"), GROUP), away, chunk, width)
        message[0] = first[:, lanes]
        message[1] = second[:, lanes]


def first_pack_kernel(first, second, lengths, flags, one, two, three, text, held, sems):
    width = one.shape[2]
    place = lax.rem(lax.axis_index("ctx"), GROUP)
    copies = []
    for away, message in zip(aways()[1:], (one, two, three)):
        lanes = columns(place, away, 0, width)
        for part, source in enumerate((first, second)):
            copies.append(
                pltpu.make_async_copy(source.at[:, lanes], message.at[part], sems.at[len(copies)])
            )
    for part, source in enumerate((lengths, flags)):
        copies.append(pltpu.make_async_copy(source, held.at[part], sems.at[len(copies)]))
    for copy in copies:
        copy.start()
    for copy in copies:
        copy.wait()
    text[...] = (held[0] * (1 - held[1])).astype(jnp.float32)


def pack(first, second, after, chunk):
    rows, total = first.shape
    width = total // (GROUP * CHUNKS)
    message = jax.ShapeDtypeStruct((2, rows, width), first.dtype)
    return pl.pallas_call(
        functools.partial(pack_kernel, chunk),
        out_shape=(message,) * (GROUP - 1),
        in_specs=[VMEM, VMEM, ANY],
        out_specs=(VMEM,) * (GROUP - 1),
        compiler_params=SMALL,
        cost_estimate=pl.CostEstimate(flops=0, bytes_accessed=12 * rows * width * 2, transcendentals=0),
        name="pack",
    )(first, second, after)


def first_pack(first, second, lengths, flags):
    rows, total = first.shape
    width = total // (GROUP * CHUNKS)
    message = jax.ShapeDtypeStruct((2, rows, width), first.dtype)
    *messages, text = pl.pallas_call(
        first_pack_kernel,
        out_shape=(message,) * (GROUP - 1) + (jax.ShapeDtypeStruct(lengths.shape, jnp.float32),),
        in_specs=[ANY, ANY, ANY, ANY],
        out_specs=(VMEM,) * GROUP,
        scratch_shapes=[
            pltpu.VMEM((2, *lengths.shape), lengths.dtype),
            pltpu.SemaphoreType.DMA((2 * GROUP,)),
        ],
        compiler_params=LARGE,
        cost_estimate=pl.CostEstimate(flops=0, bytes_accessed=12 * rows * width * 2, transcendentals=0),
        name="first_pack",
    )(first, second, lengths, flags)
    return messages, text


def edge_kernel(chunk, first, second, one, two, three, *refs):
    edge = refs[-1]
    rows = edge.shape[1] // (GROUP - 1)
    width = edge.shape[2]
    place = lax.rem(lax.axis_index("ctx"), GROUP)
    for away, message in zip(aways(), (None, one, two, three)):
        index = lax.rem(place + GROUP - away, GROUP)

        @pl.when(index > 0)
        def put():
            at = pl.ds(pl.multiple_of((index - 1) * rows, rows), rows)
            if message is None:
                lanes = columns(place, 0, chunk, width)
                edge[0, at, :] = first[:, lanes]
                edge[1, at, :] = second[:, lanes]
            else:
                edge[:, at, :] = message[...]


def make_edge(first, second, blocks, afters, chunk, cost):
    _, rows, width = blocks[0].shape
    return pl.pallas_call(
        functools.partial(edge_kernel, chunk),
        out_shape=jax.ShapeDtypeStruct((2, (GROUP - 1) * rows, width), first.dtype),
        in_specs=[VMEM] * 5 + [ANY] * len(afters),
        out_specs=VMEM,
        compiler_params=SMALL,
        cost_estimate=pl.CostEstimate(flops=cost, bytes_accessed=0, transcendentals=0),
        name="edge",
    )(first, second, *blocks, *afters)


def sides_kernel(stretch_rows, cycle_size, lengths_ref, flags_ref, after, limit_ref, text_ref, key_ref):
    rows = 2 * stretch_rows
    device_here = lax.axis_index("ctx")
    start = device_here - lax.rem(device_here, GROUP)
    segments = lengths_ref.shape[1]
    square = (segments, segments)
    diagonal = lax.broadcasted_iota(jnp.int32, square, 0) == lax.broadcasted_iota(
        jnp.int32, square, 1
    )

    def upright(ref):
        row = jnp.broadcast_to(ref[...].astype(jnp.float32), square)
        return jnp.sum(jnp.where(diagonal, row, 0.0), axis=1, keepdims=True)

    lengths, flags = upright(lengths_ref), upright(flags_ref)
    source = lax.broadcasted_iota(jnp.int32, (segments, HEAD), 0)
    target = lax.broadcasted_iota(jnp.int32, (segments, HEAD), 1)

    def gathered_sum(mask, column):
        return jnp.sum(jnp.where(mask, column, 0.0), axis=0, keepdims=True)

    last = gathered_sum(source <= target, lengths)
    first = gathered_sum(source < target, lengths).astype(jnp.int32)
    flag = gathered_sum(source == target, flags)
    ending = last.astype(jnp.int32)
    shape = (rows, HEAD)
    offset = lax.broadcasted_iota(jnp.int32, shape, 0)
    for block in range(GROUP):
        device = start + block
        position = jnp.where(
            offset < stretch_rows,
            device * stretch_rows + offset,
            (2 * cycle_size - 2 - device) * stretch_rows + offset,
        )
        inside = (position >= first) & (position < ending)
        image = jnp.sum(jnp.where(inside, flag, 0.0), axis=1, keepdims=True)
        final = jnp.sum(jnp.where(inside, last, 0.0), axis=1, keepdims=True).astype(jnp.int32) - 1
        limit_ref[block] = jnp.where(image > 0.5, final, position)
        text_ref[block] = jnp.broadcast_to(1.0 - image, shape)
        lane = lax.broadcasted_iota(jnp.int32, (8, STEPS * rows), 1)
        step = jnp.zeros_like(lane)
        for edge in range(1, STEPS):
            step = step + (lane >= edge * rows).astype(jnp.int32)
        owner = device - (STEPS - 1) + step
        owner = jnp.where(owner < 0, owner + cycle_size, owner)
        within = lane - step * rows
        key_ref[block] = jnp.where(
            within < stretch_rows,
            owner * stretch_rows + within,
            (2 * cycle_size - 2 - owner) * stretch_rows + within,
        )


def sides(lengths, flags, after, stretch_rows, cycle_size):
    rows = 2 * stretch_rows
    return pl.pallas_call(
        functools.partial(sides_kernel, stretch_rows, cycle_size),
        out_shape=(
            jax.ShapeDtypeStruct((GROUP, rows, HEAD), jnp.int32),
            jax.ShapeDtypeStruct((GROUP, rows, HEAD), jnp.float32),
            jax.ShapeDtypeStruct((GROUP, 8, STEPS * rows), jnp.int32),
        ),
        in_specs=[VMEM, VMEM, ANY],
        out_specs=(VMEM,) * 3,
        compiler_params=SMALL,
        cost_estimate=pl.CostEstimate(flops=GROUP * rows * HEAD * 8, bytes_accessed=GROUP * rows * HEAD * 8, transcendentals=0),
        name="sides",
    )(lengths, flags, after)


def attend_kernel(
    chunk, total_rows, text_one, text_two, text_three, text_four, limit_ref, text_ref, keypos_ref,
    queries, keys, values, grads, key_one, key_two, key_three, query_one, query_two, query_three,
    edge_ref, query_own, query_to_one, query_to_two, query_to_three, main_ref, far_ref,
    key_all, value_all, query_all, grad_all, key_grad, value_grad, query_out,
):
    rows, width = queries.shape[0], edge_ref.shape[2]
    edge = (GROUP - 1) * rows
    span = STEPS * rows
    scale = HEAD ** (-0.5)
    place = lax.rem(lax.axis_index("ctx"), GROUP)
    counted = text_one[...] + text_two[...] + text_three[...] + text_four[...]
    factor = total_rows / jnp.sum(counted, axis=1, keepdims=True)
    lanes = columns(place, 0, chunk, width)
    key_all[:edge, :] = edge_ref[0]
    value_all[:edge, :] = edge_ref[1]
    sources = [(keys.at[:, lanes], values.at[:, lanes], queries.at[:, lanes], grads.at[:, lanes])]
    for pair, query_pair in ((key_one, query_one), (key_two, query_two), (key_three, query_three)):
        sources.append((pair.at[0], pair.at[1], query_pair.at[0], query_pair.at[1]))
    for slot, away in enumerate(aways()):
        start = pl.multiple_of(lax.rem(place + GROUP - away, GROUP) * rows, rows)
        key, value, query, grad = sources[slot]
        key_all[pl.ds(edge + start, rows), :] = key[...]
        value_all[pl.ds(edge + start, rows), :] = value[...]
        query_all[pl.ds(start, rows), :] = query[...]
        grad_all[pl.ds(start, rows), :] = grad[...]
    for block in range(GROUP):
        at = slice(block * rows, (block + 1) * rows)
        window = slice(block * rows, block * rows + span)
        limit = limit_ref[block]
        allowed = jnp.concatenate(
            [
                keypos_ref[block, 0:1, tile * HEAD : (tile + 1) * HEAD] <= limit
                for tile in range(span // HEAD)
            ],
            axis=1,
        )
        weight = text_ref[block] * factor
        for head in range(width // HEAD):
            lanes = slice(head * HEAD, (head + 1) * HEAD)
            query = query_all[at, lanes]
            grad = (grad_all[at, lanes].astype(jnp.float32) * weight).astype(jnp.bfloat16)
            key = key_all[window, lanes]
            value = value_all[window, lanes]
            scores = lax.dot_general(
                query, key, (((1,), (1,)), ((), ())), preferred_element_type=jnp.float32
            )
            scores = jnp.where(allowed, scores, MASKED)
            largest = jnp.max(scores, axis=1, keepdims=True)
            prob = jnp.exp2((scores - largest) * (scale * LOG2E))
            dprob = lax.dot_general(
                grad, value, (((1,), (1,)), ((), ())), preferred_element_type=jnp.float32
            )
            total = jnp.sum(prob, axis=1, keepdims=True)
            inverse = 1.0 / total
            delta = jnp.sum(prob * dprob, axis=1, keepdims=True) * inverse
            prob = prob * inverse
            dscore = (prob * (dprob - delta)).astype(jnp.bfloat16)
            prob_half = prob.astype(jnp.bfloat16)
            query_out[at, lanes] = (
                jnp.dot(dscore, key, preferred_element_type=jnp.float32) * scale
            ).astype(jnp.bfloat16)
            for kind, (left, right, held, scaling) in enumerate(
                ((dscore, query, key_grad, scale), (prob_half, grad, value_grad, 1.0))
            ):
                term = lax.dot_general(
                    right, left, (((0,), (0,)), ((), ())), preferred_element_type=jnp.float32
                ).T
                for step in range(STEPS):
                    index = block + step
                    here = slice(index * rows, (index + 1) * rows)
                    part = term[step * rows : (step + 1) * rows]
                    if block > 0 and step < STEPS - 1:
                        part = part + held[here, lanes]
                    if step > 0 and block < GROUP - 1:
                        held[here, lanes] = part
                    elif index < GROUP - 1:
                        far_ref[kind, here, lanes] = (part * scaling).astype(jnp.bfloat16)
                    else:
                        there = slice((index - GROUP + 1) * rows, (index - GROUP + 2) * rows)
                        main_ref[kind, there, lanes] = (part * scaling).astype(jnp.bfloat16)
    for away, block in zip(aways(), (query_own, query_to_one, query_to_two, query_to_three)):
        index = lax.rem(place + away, GROUP)
        block[...] = query_out[pl.ds(pl.multiple_of(index * rows, rows), rows), :]


def attend(texts, marks, arrays, key_blocks, query_blocks, edge, chunk, total_rows):
    _, rows, width = key_blocks[0].shape
    heads = width // HEAD
    keys = (2 * GROUP - 1) * rows
    pairs = heads * GROUP * rows * STEPS * rows
    return pl.pallas_call(
        functools.partial(attend_kernel, chunk, total_rows),
        out_shape=(
            *[jax.ShapeDtypeStruct((rows, width), jnp.bfloat16)] * GROUP,
            jax.ShapeDtypeStruct((2, GROUP * rows, width), jnp.bfloat16),
            jax.ShapeDtypeStruct((2, (GROUP - 1) * rows, width), jnp.bfloat16),
        ),
        in_specs=[VMEM] * (len(texts) + 14),
        out_specs=(VMEM,) * (GROUP + 2),
        scratch_shapes=[
            pltpu.VMEM((keys, width), jnp.bfloat16),
            pltpu.VMEM((keys, width), jnp.bfloat16),
            pltpu.VMEM((GROUP * rows, width), jnp.bfloat16),
            pltpu.VMEM((GROUP * rows, width), jnp.bfloat16),
            pltpu.VMEM((keys, width), jnp.float32),
            pltpu.VMEM((keys, width), jnp.float32),
            pltpu.VMEM((GROUP * rows, width), jnp.bfloat16),
        ],
        compiler_params=pltpu.CompilerParams(vmem_limit_bytes=24 * 1024 * 1024),
        cost_estimate=pl.CostEstimate(
            flops=4500000000, bytes_accessed=0, transcendentals=0
        ),
        name="attend",
    )(*texts, *marks, *arrays, *key_blocks, *query_blocks, edge)


def settle_kernel(main_ref, far_ref, *refs):
    extra = refs[: len(refs) // GROUP * GROUP - GROUP]
    outs = refs[len(refs) - GROUP :]
    rows = outs[0].shape[1]
    first_kind = 1 if extra else 0
    place = lax.rem(lax.axis_index("ctx"), GROUP)
    for slot, (away, block) in enumerate(zip(aways(), outs)):
        index = lax.rem(place + away, GROUP)
        start = pl.multiple_of(index * rows, rows)
        if extra:
            block[0] = extra[slot][...]

        @pl.when(index == 0)
        def first():
            block[first_kind:] = main_ref[:, :rows, :]

        @pl.when(index > 0)
        def later():
            behind = pl.multiple_of(start - rows, rows)
            block[first_kind:] = (
                main_ref[:, pl.ds(start, rows), :].astype(jnp.float32)
                + far_ref[:, pl.ds(behind, rows), :].astype(jnp.float32)
            ).astype(jnp.bfloat16)


def settle(main, far, extra=(), after=()):
    _, total, width = main.shape
    rows = total // GROUP
    count = 2 + (1 if extra else 0)

    def kernel(main_ref, far_ref, *refs):
        refs = list(refs)
        settle_kernel(main_ref, far_ref, *refs[: len(extra)], *refs[-GROUP:])

    return pl.pallas_call(
        kernel,
        out_shape=(jax.ShapeDtypeStruct((count, rows, width), jnp.bfloat16),) * GROUP,
        in_specs=[VMEM, VMEM] + [VMEM] * len(extra) + [ANY] * len(after),
        out_specs=(VMEM,) * GROUP,
        compiler_params=SMALL,
        cost_estimate=pl.CostEstimate(
            flops=SETTLE_COST if extra else 0, bytes_accessed=main.size * 8, transcendentals=0
        ),
        name="settle",
    )(main, far, *extra, *after)


def place_copies(moves, sems):
    copies = []
    for source, target, chunk, slot in moves:
        lanes = columns(lax.rem(lax.axis_index("ctx"), GROUP), -aways()[slot], chunk, source.shape[1])
        copies.append(pltpu.make_async_copy(source, target.at[:, lanes], sems.at[len(copies)]))
    for copy in copies:
        copy.start()
    for copy in copies:
        copy.wait()


def early_kernel(*refs):
    queries, mixed = refs[:GROUP], refs[GROUP : 2 * GROUP]
    query_ref, key_ref, value_ref, sems = refs[2 * GROUP :]
    moves = []
    for away in range(GROUP):
        moves += [
            (queries[away], query_ref, 0, away),
            (mixed[away].at[0], query_ref, 1, away),
            (mixed[away].at[1], key_ref, 0, away),
            (mixed[away].at[2], value_ref, 0, away),
        ]
    place_copies(moves, sems)


def late_kernel(*refs):
    pairs = refs[:GROUP]
    key_ref, value_ref, sems = refs[GROUP + 2 :]
    moves = []
    for away in range(GROUP):
        moves += [
            (pairs[away].at[0], key_ref, 1, away),
            (pairs[away].at[1], value_ref, 1, away),
        ]
    place_copies(moves, sems)


def gathered(queries, mixed, pairs):
    rows, width = queries[0].shape
    out = jax.ShapeDtypeStruct((rows, width * CHUNKS * GROUP), jnp.bfloat16)
    grad_queries, grad_keys, grad_values = pl.pallas_call(
        early_kernel,
        out_shape=(out, out, out),
        in_specs=[VMEM] * (2 * GROUP),
        out_specs=(ANY,) * 3,
        scratch_shapes=[pltpu.SemaphoreType.DMA((4 * GROUP,))],
        compiler_params=SMALL,
        cost_estimate=pl.CostEstimate(flops=0, bytes_accessed=out.size * 6, transcendentals=0),
        name="early",
    )(*queries, *mixed)
    grad_keys, grad_values = pl.pallas_call(
        late_kernel,
        out_shape=(out, out),
        in_specs=[VMEM] * GROUP + [ANY, ANY],
        out_specs=(ANY, ANY),
        input_output_aliases={GROUP: 0, GROUP + 1: 1},
        scratch_shapes=[pltpu.SemaphoreType.DMA((2 * GROUP,))],
        compiler_params=SMALL,
        cost_estimate=pl.CostEstimate(flops=0, bytes_accessed=out.size * 6, transcendentals=0),
        name="late",
    )(*pairs, grad_keys, grad_values)
    return grad_queries, grad_keys, grad_values


def shards(queries, keys, values, grad_out, lengths, image_flags):
    query_rows, key_rows, value_rows, grad_rows = queries[0], keys[0], values[0], grad_out[0]
    row_count = query_rows.shape[0]
    cycle_size = lax.axis_size("ctx")
    samples = lax.axis_size("dp")

    def swap(value, slot):
        pairs = []
        for sample in range(samples):
            core = sample % 2
            away = (1 + 2 * core, 3 - 2 * core, 2)[slot]
            for source in range(cycle_size):
                target = source - source % GROUP + (source + away) % GROUP
                pairs.append((sample * cycle_size + source, sample * cycle_size + target))
        return lax.ppermute(value, ("dp", "ctx"), pairs)

    def next_row(value, rows):
        pairs = [(source, (source + rows * GROUP) % cycle_size) for source in range(cycle_size)]
        return lax.ppermute(value, "ctx", pairs)

    def swapped(messages):
        return [swap(message, slot) for slot, message in enumerate(messages)]

    first_messages, text = first_pack(key_rows, value_rows, lengths, image_flags)
    texts = [text] + [
        lax.ppermute(text, "dp", [(source, (source + away) % samples) for source in range(samples)])
        for away in range(1, samples)
    ]
    total_rows = float(row_count * cycle_size * samples)

    key_packs, query_packs, edges = [None] * CHUNKS, [None] * CHUNKS, [None] * CHUNKS
    key_packs[0] = first_messages
    key_packs[1] = pack(key_rows, value_rows, text, 1)
    key_blocks = [swapped(messages) for messages in key_packs]
    edges[0] = make_edge(
        key_rows, value_rows, key_blocks[0], (*texts[1:], key_packs[1][0]), 0, EDGE_COST[0]
    )
    after = edges[0]
    for index in range(CHUNKS):
        query_packs[index] = pack(query_rows, grad_rows, after, index)
        after = query_packs[index][0]
    marks = sides(lengths, image_flags, after, row_count // 2, cycle_size)
    edges[1] = make_edge(
        key_rows, value_rows, key_blocks[1], (marks[1],), 1, EDGE_COST[1]
    )
    query_blocks = [swapped(messages) for messages in query_packs]
    edges = [next_row(edge, 1) for edge in edges]
    arrays = (query_rows, key_rows, value_rows, grad_rows)
    halves = []
    for chunk in range(CHUNKS):
        *query_grads, main, far = attend(
            texts, marks, arrays,
            key_blocks[chunk], query_blocks[chunk], edges[chunk], chunk, total_rows,
        )
        halves.append((query_grads, main, next_row(far, -1)))
    (first_queries, main, far), (second_queries, last_main, last_far) = halves
    queries = [first_queries[0]] + swapped(first_queries[1:])
    mixed = settle(main, far, extra=second_queries, after=queries[1:])
    pairs = settle(last_main, last_far)
    mixed = [mixed[0]] + swapped(mixed[1:])
    pairs = [pairs[0]] + swapped(pairs[1:])
    grad_queries, grad_keys, grad_values = gathered(queries, mixed, pairs)
    return grad_queries[None], grad_keys[None], grad_values[None]


def solution(mesh):
    in_specs = (
        P("dp", "ctx", None),
        P("dp", "ctx", None),
        P("dp", "ctx", None),
        P("dp", "ctx", None),
        P("dp", None),
        P("dp", None),
    )
    out_specs = (P("dp", "ctx", None), P("dp", "ctx", None), P("dp", "ctx", None))
    return jax.shard_map(shards, mesh=mesh, in_specs=in_specs, out_specs=out_specs, check_vma=False)
```

```python
import functools

import jax
import jax.numpy as jnp
from jax import lax
from jax.experimental import pallas as pl
from jax.experimental.pallas import tpu as pltpu
from jax.sharding import PartitionSpec as P

HEAD = 128
STEPS = 4
GROUP = 4
CHUNKS = 2
LOG2E = 1.4426950408889634
MASKED = -1e30
VMEM = pl.BlockSpec(memory_space=pltpu.VMEM)
ANY = pl.BlockSpec(memory_space=pl.ANY)
LARGE = pltpu.CompilerParams(vmem_limit_bytes=60 * 1024 * 1024)
EDGE_COST = (0, 6000000000)
SETTLE_COST = 3000000000
SMALL = pltpu.CompilerParams(vmem_limit_bytes=10 * 1024 * 1024)


def aways():
    core = lax.rem(lax.axis_index("dp"), 2)
    return 0, 1 + 2 * core, 3 - 2 * core, 2


def columns(place, away, chunk, width):
    index = lax.rem(place + GROUP + away, GROUP)
    return pl.ds(pl.multiple_of((index * CHUNKS + chunk) * width, width), width)


def pack_kernel(chunk, first, second, after, one, two, three):
    width = one.shape[2]
    for away, message in zip(aways()[1:], (one, two, three)):
        lanes = columns(lax.rem(lax.axis_index("ctx"), GROUP), away, chunk, width)
        message[0] = first[:, lanes]
        message[1] = second[:, lanes]


def first_pack_kernel(first, second, lengths, flags, one, two, three, text, staged, held, sems):
    width = one.shape[2]
    place = lax.rem(lax.axis_index("ctx"), GROUP)
    inward, outward = [], []
    for slot, (away, message) in enumerate(zip(aways()[1:], (one, two, three))):
        lanes = columns(place, away, 0, width)
        for part, source in enumerate((first, second)):
            inward.append(
                pltpu.make_async_copy(
                    source.at[:, lanes], staged.at[slot, part], sems.at[len(inward)]
                )
            )
        outward.append(pltpu.make_async_copy(staged.at[slot], message, sems.at[8 + slot]))
    for part, source in enumerate((lengths, flags)):
        inward.append(pltpu.make_async_copy(source, held.at[part], sems.at[len(inward)]))
    for copy in inward:
        copy.start()
    for slot, copy in enumerate(outward):
        inward[2 * slot].wait()
        inward[2 * slot + 1].wait()
        copy.start()
    for copy in inward[6:]:
        copy.wait()
    text[...] = (held[0] * (1 - held[1])).astype(jnp.float32)
    for copy in outward:
        copy.wait()


def pack(first, second, after, chunk):
    rows, total = first.shape
    width = total // (GROUP * CHUNKS)
    message = jax.ShapeDtypeStruct((2, rows, width), first.dtype)
    return pl.pallas_call(
        functools.partial(pack_kernel, chunk),
        out_shape=(message,) * (GROUP - 1),
        in_specs=[VMEM, VMEM, ANY],
        out_specs=(VMEM,) * (GROUP - 1),
        compiler_params=SMALL,
        cost_estimate=pl.CostEstimate(flops=0, bytes_accessed=12 * rows * width * 2, transcendentals=0),
        name="pack",
    )(first, second, after)


def first_pack(first, second, lengths, flags):
    rows, total = first.shape
    width = total // (GROUP * CHUNKS)
    message = jax.ShapeDtypeStruct((2, rows, width), first.dtype)
    *messages, text = pl.pallas_call(
        first_pack_kernel,
        out_shape=(message,) * (GROUP - 1) + (jax.ShapeDtypeStruct(lengths.shape, jnp.float32),),
        in_specs=[ANY, ANY, ANY, ANY],
        out_specs=(ANY,) * (GROUP - 1) + (VMEM,),
        scratch_shapes=[
            pltpu.VMEM((GROUP - 1, 2, rows, width), first.dtype),
            pltpu.VMEM((2, *lengths.shape), lengths.dtype),
            pltpu.SemaphoreType.DMA((2 * GROUP + 3,)),
        ],
        compiler_params=LARGE,
        cost_estimate=pl.CostEstimate(flops=0, bytes_accessed=12 * rows * width * 2, transcendentals=0),
        name="first_pack",
    )(first, second, lengths, flags)
    return messages, text


def edge_kernel(chunk, first, second, one, two, three, *refs):
    edge = refs[-1]
    rows = edge.shape[1] // (GROUP - 1)
    width = edge.shape[2]
    place = lax.rem(lax.axis_index("ctx"), GROUP)
    for away, message in zip(aways(), (None, one, two, three)):
        index = lax.rem(place + GROUP - away, GROUP)

        @pl.when(index > 0)
        def put():
            at = pl.ds(pl.multiple_of((index - 1) * rows, rows), rows)
            if message is None:
                lanes = columns(place, 0, chunk, width)
                edge[0, at, :] = first[:, lanes]
                edge[1, at, :] = second[:, lanes]
            else:
                edge[:, at, :] = message[...]


def make_edge(first, second, blocks, afters, chunk, cost):
    _, rows, width = blocks[0].shape
    return pl.pallas_call(
        functools.partial(edge_kernel, chunk),
        out_shape=jax.ShapeDtypeStruct((2, (GROUP - 1) * rows, width), first.dtype),
        in_specs=[VMEM] * 5 + [ANY] * len(afters),
        out_specs=VMEM,
        compiler_params=SMALL,
        cost_estimate=pl.CostEstimate(flops=cost, bytes_accessed=0, transcendentals=0),
        name="edge",
    )(first, second, *blocks, *afters)


def sides_kernel(stretch_rows, cycle_size, lengths_ref, flags_ref, after, limit_ref, text_ref, key_ref):
    rows = 2 * stretch_rows
    device_here = lax.axis_index("ctx")
    start = device_here - lax.rem(device_here, GROUP)
    segments = lengths_ref.shape[1]
    square = (segments, segments)
    diagonal = lax.broadcasted_iota(jnp.int32, square, 0) == lax.broadcasted_iota(
        jnp.int32, square, 1
    )

    def upright(ref):
        row = jnp.broadcast_to(ref[...].astype(jnp.float32), square)
        return jnp.sum(jnp.where(diagonal, row, 0.0), axis=1, keepdims=True)

    lengths, flags = upright(lengths_ref), upright(flags_ref)
    source = lax.broadcasted_iota(jnp.int32, (segments, HEAD), 0)
    target = lax.broadcasted_iota(jnp.int32, (segments, HEAD), 1)

    def gathered_sum(mask, column):
        return jnp.sum(jnp.where(mask, column, 0.0), axis=0, keepdims=True)

    last = gathered_sum(source <= target, lengths)
    first = gathered_sum(source < target, lengths).astype(jnp.int32)
    flag = gathered_sum(source == target, flags)
    ending = last.astype(jnp.int32)
    shape = (rows, HEAD)
    offset = lax.broadcasted_iota(jnp.int32, shape, 0)
    for block in range(GROUP):
        device = start + block
        position = jnp.where(
            offset < stretch_rows,
            device * stretch_rows + offset,
            (2 * cycle_size - 2 - device) * stretch_rows + offset,
        )
        inside = (position >= first) & (position < ending)
        image = jnp.sum(jnp.where(inside, flag, 0.0), axis=1, keepdims=True)
        final = jnp.sum(jnp.where(inside, last, 0.0), axis=1, keepdims=True).astype(jnp.int32) - 1
        limit_ref[block] = jnp.where(image > 0.5, final, position)
        text_ref[block] = jnp.broadcast_to(1.0 - image, shape)
        lane = lax.broadcasted_iota(jnp.int32, (8, STEPS * rows), 1)
        step = jnp.zeros_like(lane)
        for edge in range(1, STEPS):
            step = step + (lane >= edge * rows).astype(jnp.int32)
        owner = device - (STEPS - 1) + step
        owner = jnp.where(owner < 0, owner + cycle_size, owner)
        within = lane - step * rows
        key_ref[block] = jnp.where(
            within < stretch_rows,
            owner * stretch_rows + within,
            (2 * cycle_size - 2 - owner) * stretch_rows + within,
        )


def sides(lengths, flags, after, stretch_rows, cycle_size):
    rows = 2 * stretch_rows
    return pl.pallas_call(
        functools.partial(sides_kernel, stretch_rows, cycle_size),
        out_shape=(
            jax.ShapeDtypeStruct((GROUP, rows, HEAD), jnp.int32),
            jax.ShapeDtypeStruct((GROUP, rows, HEAD), jnp.float32),
            jax.ShapeDtypeStruct((GROUP, 8, STEPS * rows), jnp.int32),
        ),
        in_specs=[VMEM, VMEM, ANY],
        out_specs=(VMEM,) * 3,
        compiler_params=SMALL,
        cost_estimate=pl.CostEstimate(flops=GROUP * rows * HEAD * 8, bytes_accessed=GROUP * rows * HEAD * 8, transcendentals=0),
        name="sides",
    )(lengths, flags, after)


def attend_kernel(
    chunk, total_rows, text_one, text_two, text_three, text_four, limit_ref, text_ref, keypos_ref,
    queries, keys, values, grads, key_one, key_two, key_three, query_one, query_two, query_three,
    edge_ref, query_own, query_to_one, query_to_two, query_to_three, main_ref, far_ref,
    key_all, value_all, query_all, grad_all, key_grad, value_grad, query_out,
):
    rows, width = queries.shape[0], edge_ref.shape[2]
    edge = (GROUP - 1) * rows
    span = STEPS * rows
    scale = HEAD ** (-0.5)
    place = lax.rem(lax.axis_index("ctx"), GROUP)
    counted = text_one[...] + text_two[...] + text_three[...] + text_four[...]
    factor = total_rows / jnp.sum(counted, axis=1, keepdims=True)
    lanes = columns(place, 0, chunk, width)
    key_all[:edge, :] = edge_ref[0]
    value_all[:edge, :] = edge_ref[1]
    sources = [(keys.at[:, lanes], values.at[:, lanes], queries.at[:, lanes], grads.at[:, lanes])]
    for pair, query_pair in ((key_one, query_one), (key_two, query_two), (key_three, query_three)):
        sources.append((pair.at[0], pair.at[1], query_pair.at[0], query_pair.at[1]))
    for slot, away in enumerate(aways()):
        start = pl.multiple_of(lax.rem(place + GROUP - away, GROUP) * rows, rows)
        key, value, query, grad = sources[slot]
        key_all[pl.ds(edge + start, rows), :] = key[...]
        value_all[pl.ds(edge + start, rows), :] = value[...]
        query_all[pl.ds(start, rows), :] = query[...]
        grad_all[pl.ds(start, rows), :] = grad[...]
    for block in range(GROUP):
        at = slice(block * rows, (block + 1) * rows)
        window = slice(block * rows, block * rows + span)
        limit = limit_ref[block]
        allowed = jnp.concatenate(
            [
                keypos_ref[block, 0:1, tile * HEAD : (tile + 1) * HEAD] <= limit
                for tile in range(span // HEAD)
            ],
            axis=1,
        )
        weight = text_ref[block] * factor
        for head in range(width // HEAD):
            lanes = slice(head * HEAD, (head + 1) * HEAD)
            query = query_all[at, lanes]
            grad = (grad_all[at, lanes].astype(jnp.float32) * weight).astype(jnp.bfloat16)
            key = key_all[window, lanes]
            value = value_all[window, lanes]
            scores = lax.dot_general(
                query, key, (((1,), (1,)), ((), ())), preferred_element_type=jnp.float32
            )
            scores = jnp.where(allowed, scores, MASKED)
            largest = jnp.max(scores, axis=1, keepdims=True)
            prob = jnp.exp2((scores - largest) * (scale * LOG2E))
            dprob = lax.dot_general(
                grad, value, (((1,), (1,)), ((), ())), preferred_element_type=jnp.float32
            )
            total = jnp.sum(prob, axis=1, keepdims=True)
            inverse = 1.0 / total
            delta = jnp.sum(prob * dprob, axis=1, keepdims=True) * inverse
            prob = prob * inverse
            dscore = (prob * (dprob - delta)).astype(jnp.bfloat16)
            prob_half = prob.astype(jnp.bfloat16)
            query_out[at, lanes] = (
                jnp.dot(dscore, key, preferred_element_type=jnp.float32) * scale
            ).astype(jnp.bfloat16)
            for kind, (left, right, held, scaling) in enumerate(
                ((dscore, query, key_grad, scale), (prob_half, grad, value_grad, 1.0))
            ):
                term = lax.dot_general(
                    right, left, (((0,), (0,)), ((), ())), preferred_element_type=jnp.float32
                ).T
                for step in range(STEPS):
                    index = block + step
                    here = slice(index * rows, (index + 1) * rows)
                    part = term[step * rows : (step + 1) * rows]
                    if block > 0 and step < STEPS - 1:
                        part = part + held[here, lanes]
                    if step > 0 and block < GROUP - 1:
                        held[here, lanes] = part
                    elif index < GROUP - 1:
                        far_ref[kind, here, lanes] = (part * scaling).astype(jnp.bfloat16)
                    else:
                        there = slice((index - GROUP + 1) * rows, (index - GROUP + 2) * rows)
                        main_ref[kind, there, lanes] = (part * scaling).astype(jnp.bfloat16)
    for away, block in zip(aways(), (query_own, query_to_one, query_to_two, query_to_three)):
        index = lax.rem(place + away, GROUP)
        block[...] = query_out[pl.ds(pl.multiple_of(index * rows, rows), rows), :]


def attend(texts, marks, arrays, key_blocks, query_blocks, edge, chunk, total_rows):
    _, rows, width = key_blocks[0].shape
    heads = width // HEAD
    keys = (2 * GROUP - 1) * rows
    pairs = heads * GROUP * rows * STEPS * rows
    return pl.pallas_call(
        functools.partial(attend_kernel, chunk, total_rows),
        out_shape=(
            *[jax.ShapeDtypeStruct((rows, width), jnp.bfloat16)] * GROUP,
            jax.ShapeDtypeStruct((2, GROUP * rows, width), jnp.bfloat16),
            jax.ShapeDtypeStruct((2, (GROUP - 1) * rows, width), jnp.bfloat16),
        ),
        in_specs=[VMEM] * (len(texts) + 14),
        out_specs=(VMEM,) * (GROUP + 2),
        scratch_shapes=[
            pltpu.VMEM((keys, width), jnp.bfloat16),
            pltpu.VMEM((keys, width), jnp.bfloat16),
            pltpu.VMEM((GROUP * rows, width), jnp.bfloat16),
            pltpu.VMEM((GROUP * rows, width), jnp.bfloat16),
            pltpu.VMEM((keys, width), jnp.float32),
            pltpu.VMEM((keys, width), jnp.float32),
            pltpu.VMEM((GROUP * rows, width), jnp.bfloat16),
        ],
        compiler_params=pltpu.CompilerParams(vmem_limit_bytes=24 * 1024 * 1024),
        cost_estimate=pl.CostEstimate(
            flops=4500000000, bytes_accessed=0, transcendentals=0
        ),
        name="attend",
    )(*texts, *marks, *arrays, *key_blocks, *query_blocks, edge)


def settle_kernel(main_ref, far_ref, *refs):
    extra = refs[: len(refs) // GROUP * GROUP - GROUP]
    outs = refs[len(refs) - GROUP :]
    rows = outs[0].shape[1]
    first_kind = 1 if extra else 0
    place = lax.rem(lax.axis_index("ctx"), GROUP)
    for slot, (away, block) in enumerate(zip(aways(), outs)):
        index = lax.rem(place + away, GROUP)
        start = pl.multiple_of(index * rows, rows)
        if extra:
            block[0] = extra[slot][...]

        @pl.when(index == 0)
        def first():
            block[first_kind:] = main_ref[:, :rows, :]

        @pl.when(index > 0)
        def later():
            behind = pl.multiple_of(start - rows, rows)
            block[first_kind:] = (
                main_ref[:, pl.ds(start, rows), :].astype(jnp.float32)
                + far_ref[:, pl.ds(behind, rows), :].astype(jnp.float32)
            ).astype(jnp.bfloat16)


def settle(main, far, extra=(), after=()):
    _, total, width = main.shape
    rows = total // GROUP
    count = 2 + (1 if extra else 0)

    def kernel(main_ref, far_ref, *refs):
        refs = list(refs)
        settle_kernel(main_ref, far_ref, *refs[: len(extra)], *refs[-GROUP:])

    return pl.pallas_call(
        kernel,
        out_shape=(jax.ShapeDtypeStruct((count, rows, width), jnp.bfloat16),) * GROUP,
        in_specs=[VMEM, VMEM] + [VMEM] * len(extra) + [ANY] * len(after),
        out_specs=(VMEM,) * GROUP,
        compiler_params=SMALL,
        cost_estimate=pl.CostEstimate(
            flops=SETTLE_COST if extra else 0, bytes_accessed=main.size * 8, transcendentals=0
        ),
        name="settle",
    )(main, far, *extra, *after)


def place_copies(moves, sems):
    copies = []
    for source, target, chunk, slot in moves:
        lanes = columns(lax.rem(lax.axis_index("ctx"), GROUP), -aways()[slot], chunk, source.shape[1])
        copies.append(pltpu.make_async_copy(source, target.at[:, lanes], sems.at[len(copies)]))
    for copy in copies:
        copy.start()
    for copy in copies:
        copy.wait()


def early_kernel(*refs):
    queries, mixed = refs[:GROUP], refs[GROUP : 2 * GROUP]
    query_ref, key_ref, value_ref, sems = refs[2 * GROUP :]
    moves = []
    for away in range(GROUP):
        moves += [
            (queries[away], query_ref, 0, away),
            (mixed[away].at[0], query_ref, 1, away),
            (mixed[away].at[1], key_ref, 0, away),
            (mixed[away].at[2], value_ref, 0, away),
        ]
    place_copies(moves, sems)


def late_kernel(*refs):
    pairs = refs[:GROUP]
    key_ref, value_ref, sems = refs[GROUP + 2 :]
    moves = []
    for away in range(GROUP):
        moves += [
            (pairs[away].at[0], key_ref, 1, away),
            (pairs[away].at[1], value_ref, 1, away),
        ]
    place_copies(moves, sems)


def gathered(queries, mixed, pairs):
    rows, width = queries[0].shape
    out = jax.ShapeDtypeStruct((rows, width * CHUNKS * GROUP), jnp.bfloat16)
    grad_queries, grad_keys, grad_values = pl.pallas_call(
        early_kernel,
        out_shape=(out, out, out),
        in_specs=[VMEM] * (2 * GROUP),
        out_specs=(ANY,) * 3,
        scratch_shapes=[pltpu.SemaphoreType.DMA((4 * GROUP,))],
        compiler_params=SMALL,
        cost_estimate=pl.CostEstimate(flops=0, bytes_accessed=out.size * 6, transcendentals=0),
        name="early",
    )(*queries, *mixed)
    grad_keys, grad_values = pl.pallas_call(
        late_kernel,
        out_shape=(out, out),
        in_specs=[VMEM] * GROUP + [ANY, ANY],
        out_specs=(ANY, ANY),
        input_output_aliases={GROUP: 0, GROUP + 1: 1},
        scratch_shapes=[pltpu.SemaphoreType.DMA((2 * GROUP,))],
        compiler_params=SMALL,
        cost_estimate=pl.CostEstimate(flops=0, bytes_accessed=out.size * 6, transcendentals=0),
        name="late",
    )(*pairs, grad_keys, grad_values)
    return grad_queries, grad_keys, grad_values


def shards(queries, keys, values, grad_out, lengths, image_flags):
    query_rows, key_rows, value_rows, grad_rows = queries[0], keys[0], values[0], grad_out[0]
    row_count = query_rows.shape[0]
    cycle_size = lax.axis_size("ctx")
    samples = lax.axis_size("dp")

    def swap(value, slot):
        pairs = []
        for sample in range(samples):
            core = sample % 2
            away = (1 + 2 * core, 3 - 2 * core, 2)[slot]
            for source in range(cycle_size):
                target = source - source % GROUP + (source + away) % GROUP
                pairs.append((sample * cycle_size + source, sample * cycle_size + target))
        return lax.ppermute(value, ("dp", "ctx"), pairs)

    def next_row(value, rows):
        pairs = [(source, (source + rows * GROUP) % cycle_size) for source in range(cycle_size)]
        return lax.ppermute(value, "ctx", pairs)

    def swapped(messages):
        return [swap(message, slot) for slot, message in enumerate(messages)]

    first_messages, text = first_pack(key_rows, value_rows, lengths, image_flags)
    texts = [text] + [
        lax.ppermute(text, "dp", [(source, (source + away) % samples) for source in range(samples)])
        for away in range(1, samples)
    ]
    total_rows = float(row_count * cycle_size * samples)

    key_packs, query_packs, edges = [None] * CHUNKS, [None] * CHUNKS, [None] * CHUNKS
    key_packs[0] = first_messages
    key_packs[1] = pack(key_rows, value_rows, text, 1)
    key_blocks = [swapped(messages) for messages in key_packs]
    edges[0] = make_edge(
        key_rows, value_rows, key_blocks[0], (*texts[1:], key_packs[1][0]), 0, EDGE_COST[0]
    )
    after = edges[0]
    for index in range(CHUNKS):
        query_packs[index] = pack(query_rows, grad_rows, after, index)
        after = query_packs[index][0]
    marks = sides(lengths, image_flags, after, row_count // 2, cycle_size)
    edges[1] = make_edge(
        key_rows, value_rows, key_blocks[1], (marks[1],), 1, EDGE_COST[1]
    )
    query_blocks = [swapped(messages) for messages in query_packs]
    edges = [next_row(edge, 1) for edge in edges]
    arrays = (query_rows, key_rows, value_rows, grad_rows)
    halves = []
    for chunk in range(CHUNKS):
        *query_grads, main, far = attend(
            texts, marks, arrays,
            key_blocks[chunk], query_blocks[chunk], edges[chunk], chunk, total_rows,
        )
        halves.append((query_grads, main, next_row(far, -1)))
    (first_queries, main, far), (second_queries, last_main, last_far) = halves
    queries = [first_queries[0]] + swapped(first_queries[1:])
    mixed = settle(main, far, extra=second_queries, after=queries[1:])
    pairs = settle(last_main, last_far)
    mixed = [mixed[0]] + swapped(mixed[1:])
    pairs = [pairs[0]] + swapped(pairs[1:])
    grad_queries, grad_keys, grad_values = gathered(queries, mixed, pairs)
    return grad_queries[None], grad_keys[None], grad_values[None]


def solution(mesh):
    in_specs = (
        P("dp", "ctx", None),
        P("dp", "ctx", None),
        P("dp", "ctx", None),
        P("dp", "ctx", None),
        P("dp", None),
        P("dp", None),
    )
    out_specs = (P("dp", "ctx", None), P("dp", "ctx", None), P("dp", "ctx", None))
    return jax.shard_map(shards, mesh=mesh, in_specs=in_specs, out_specs=out_specs, check_vma=False)
```
